32 devices in a mesh: groups: 2 (over y), inst: 4 (over z), feat: 4 (over x, core).
Axes of the slice: x: 2, y: 2, z: 4, core: 2. Of those that a mesh axis runs over, the one named last changes fastest.
Arguments:
- tiles: bfloat16 [8, 4, 64, 128, 128], P(('groups', 'inst'), 'feat'), parts along dimension 0, may hold values from -0.25 to 0.25
- tile_rows: int32 [8, 4, 64], P(('groups', 'inst'), 'feat'), parts along dimension 0, may hold values from 0 to 7, as said below
- tile_cols: int32 [8, 4, 64], P(('groups', 'inst'), 'feat'), parts along dimension 0, may hold values from 0 to 2047, as said below
- tile_count: int32 [8, 4], P(('groups', 'inst'), 'feat'), parts along dimension 0, may hold values from 16 to 64, as said below
- sample_ids: int32 [8, 512], P(('groups', 'inst')), parts along dimension 0, may hold values from 0 to 1023, as said below
- labels: int32 [8, 1024], P(('groups', 'inst')), parts along dimension 0, may hold values 0 or 1
- weights: float32 [8, 262144], P(('groups', 'feat')), parts along dimension 0, may hold values from -8 to 8
Outputs:
- newton_step: float32 [8, 262144], P(('groups', 'feat'), 'inst'), parts along dimension 0
- residual: float32 [8, 262144], P(('groups', 'feat'), 'inst'), parts along dimension 0
The draws below stay inside these ranges and needn't reach their ends.
There are 2 independent parts, one for each index of `groups`. The reference program is written for one: setup_inputs(seed, part) draws one part's arguments, and reference() takes and returns one part's arrays. A program takes and returns all parts, laid end to end along the dimension named above; each array names one. Nothing has to cross between parts.
Inputs may be any that keep to these rules, and one draw needn't show every extreme that they name: `tile_rows`: the (row, column) pairs of one device's slots are distinct. `tile_cols`: the (row, column) pairs of one device's slots are distinct; over all 64 slots of one device, at most 17 lie in one aligned run of 512 column blocks, and every device has a run with exactly 17. `tile_count`: slots at and beyond the count hold unused values; some device has exactly 64 live slots. `sample_ids`: distinct impressions of the instance block, numbered within it.
All inputs are finite; a program needn't handle non-finite values. No bound on the sum of `labels` on one device may be relied on, other than what follows from the above.
Results may differ from the reference program's by a relative error of at most 0.0003.
Values sent between devices are 32-bit elements; how exact they have to be, the bound alone decides.
No kernel may reach another device: no remote copies, remote signals or barrier semaphores. Data moves between devices by JAX's collectives and lax.ppermute only.
A program may use at most 64 MiB of HBM per device.

```python
import jax
import jax.numpy as jnp
from jax import lax

TILE = 128
CB_DEV = 2048
RB_DEV = 8
MAXT = 64
ITERS = 3
ROWS_DEV = 1024
SAMP_DEV = 512
FEAT_DEV = 262144
CAP = 17
N_INST = 4
N_FEAT = 4


def tile_places(key):
    seg_len = CB_DEV // N_INST
    group_total = (MAXT + CAP - 1) // CAP

    def one_device(single):
        first_owner = jax.random.randint(jax.random.fold_in(single, 1), (), 0, N_INST)
        group_keys = jax.random.split(jax.random.fold_in(single, 2), group_total)
        picks = jax.vmap(lambda gkey: jax.random.permutation(gkey, RB_DEV * seg_len)[:CAP])(group_keys)
        slot = jnp.arange(MAXT)
        group = slot // CAP
        owner = (group + first_owner) % N_INST
        cell = picks[group, slot % CAP]
        return ((cell // seg_len).astype(jnp.int32), (owner * seg_len + cell % seg_len).astype(jnp.int32))
    subkeys = jax.random.split(key, N_INST * N_FEAT)
    rows, cols = jax.vmap(one_device)(subkeys)
    return (rows.reshape(N_INST, N_FEAT, MAXT).astype(jnp.int32), cols.reshape(N_INST, N_FEAT, MAXT).astype(jnp.int32))


def draw_tile_rows(key, part):
    rows, cols = tile_places(key)
    return rows


def draw_tile_cols(key, part):
    rows, cols = tile_places(key)
    return cols


def draw_tile_count(key, part):
    key = jax.random.fold_in(key, 2)
    counts = jax.random.randint(key, (N_INST * N_FEAT,), max(1, MAXT // 4), MAXT + 1)
    chosen_dev = jax.random.randint(jax.random.fold_in(key, 7), (), 0, N_INST * N_FEAT)
    counts = jnp.where(jnp.arange(N_INST * N_FEAT) == chosen_dev, MAXT, counts)
    return counts.reshape(N_INST, N_FEAT).astype(jnp.int32)


def draw_sample_ids(key, part):
    key = jax.random.fold_in(key, 3)
    subkeys = jax.random.split(key, N_INST)
    chosen = jax.vmap(lambda single: jax.random.permutation(single, ROWS_DEV)[:SAMP_DEV])(subkeys)
    return chosen.astype(jnp.int32)


def with_ends(drawn, rng, least, largest):
    index_at = [jax.random.randint(jax.random.fold_in(rng, axis), (), 0, length) for axis, length in enumerate(drawn.shape)]
    widest = drawn.shape.index(max(drawn.shape))
    next_to = index_at[:widest] + [(index_at[widest] + 1) % drawn.shape[widest]] + index_at[widest + 1:]
    return drawn.at[tuple(index_at)].set(least).at[tuple(next_to)].set(largest)


def level_of(key, shape, pieces, low, high):
    level = 1.0
    for position, shards_of in pieces:
        draws = jax.random.uniform(jax.random.fold_in(jax.random.fold_in(key, 6), position), (shards_of,), jnp.float32, low / len(pieces), high / len(pieces))
        level = level * jnp.repeat(jnp.exp(draws), shape[position] // shards_of).reshape((-1,) + (1,) * (len(shape) - 1 - position))
    return level


def gaussian(rng, dims, scale, limit, pieces=(), kind=jnp.bfloat16):
    level = level_of(rng, dims, pieces, -0.22, 0.18) if pieces else 1.0
    array = jax.random.normal(rng, dims, jnp.float32) * scale * level
    return jnp.minimum(jnp.maximum(array, -limit), limit).astype(kind)


def setup_inputs(seed: int = 0, part: int = 0) -> dict:
    seeds = jax.random.split(jax.random.key(seed), 8)
    part_splits = jax.random.split(jax.random.fold_in(seeds[7], part), 8)
    tiles = gaussian(part_splits[0], (N_INST, N_FEAT, MAXT, TILE, TILE), 0.015625, 0.25, ((0, 4), (1, 4)))
    tile_rows = draw_tile_rows(jax.random.fold_in(jax.random.fold_in(seeds[7], part), 71), part)
    tile_cols = draw_tile_cols(jax.random.fold_in(jax.random.fold_in(seeds[7], part), 71), part)
    tile_count = draw_tile_count(jax.random.fold_in(jax.random.fold_in(seeds[7], part), 71), part)
    sample_ids = draw_sample_ids(jax.random.fold_in(jax.random.fold_in(seeds[7], part), 71), part)
    labels = with_ends((jax.random.randint(part_splits[5], (N_INST, ROWS_DEV), 0, 3) < 1).astype(jnp.int32), jax.random.fold_in(part_splits[5], 1), 0, 1)
    weights = gaussian(part_splits[6], (N_FEAT, FEAT_DEV), 1.5, 8.0, ((0, 4),), jnp.float32)
    return {"tiles": tiles, "tile_rows": tile_rows, "tile_cols": tile_cols, "tile_count": tile_count, "sample_ids": sample_ids, "labels": labels, "weights": weights}


LAMBDA = 0.02


def row_onehot(tile_row, filled):
    active = (jnp.arange(MAXT) < filled).astype(jnp.float32)
    match = (tile_row[None, :] == jnp.arange(RB_DEV)[:, None]).astype(jnp.float32)
    return match * active[None, :]


def device_forward(blocks, tile_row, tile_col, filled, vector):
    onehot = row_onehot(tile_row, filled)
    picked = vector.reshape(CB_DEV, TILE)[tile_col]
    product = jnp.einsum("tij,tj->ti", blocks.astype(jnp.float32), picked, precision=lax.Precision.HIGHEST)
    return jnp.dot(onehot, product, precision=lax.Precision.HIGHEST).reshape(-1)


def device_backward(blocks, tile_row, tile_col, filled, rowvec):
    onehot = row_onehot(tile_row, filled)
    spread = jnp.dot(onehot.T, rowvec.reshape(RB_DEV, TILE), precision=lax.Precision.HIGHEST)
    product = jnp.einsum("tij,ti->tj", blocks.astype(jnp.float32), spread, precision=lax.Precision.HIGHEST)
    return jax.ops.segment_sum(product, tile_col, num_segments=CB_DEV).reshape(-1)


def reference(tiles, tile_rows, tile_cols, tile_count, sample_ids, labels, weights):
    def forward_all(vector):
        def per_block(inst_index):
            terms = jax.vmap(device_forward)(tiles[inst_index], tile_rows[inst_index], tile_cols[inst_index], tile_count[inst_index], vector)
            return jnp.sum(terms, axis=0)
        return lax.map(per_block, jnp.arange(N_INST))

    def backward_all(rowvecs):
        def add_block(inst_index, total):
            terms = jax.vmap(device_backward, in_axes=(0, 0, 0, 0, None))(tiles[inst_index], tile_rows[inst_index], tile_cols[inst_index], tile_count[inst_index], rowvecs[inst_index])
            return total + terms
        return lax.fori_loop(0, N_INST, add_block, jnp.zeros((N_FEAT, FEAT_DEV), jnp.float32))

    sampled = jax.vmap(lambda chosen: jnp.any(chosen[:, None] == jnp.arange(ROWS_DEV)[None, :], axis=0))(sample_ids).astype(jnp.float32)
    margin = forward_all(weights)
    chance = jax.nn.sigmoid(margin)
    curv_weight = (float(ROWS_DEV) / float(SAMP_DEV)) * sampled * chance * (1.0 - chance)
    gradient = backward_all(chance - labels.astype(jnp.float32)) + LAMBDA * weights

    newton_step = jnp.zeros_like(weights)
    residual = -gradient
    direction = residual
    norm_now = jnp.sum(residual * residual)
    for iteration in range(ITERS):
        image = backward_all(curv_weight * forward_all(direction)) + LAMBDA * direction
        step_len = norm_now / jnp.sum(direction * image)
        newton_step = newton_step + step_len * direction
        residual = residual - step_len * image
        norm_next = jnp.sum(residual * residual)
        direction = residual + (norm_next / norm_now) * direction
        norm_now = norm_next
    return newton_step, residual
```

```python
import functools

import jax
import jax.numpy as jnp
from jax import lax
from jax.experimental import pallas as pl
from jax.experimental.pallas import tpu as pltpu
from jax.sharding import PartitionSpec as P

ITERS = 3
LAMBDA = 0.02

F32, BF16, I32 = jnp.float32, jnp.bfloat16, jnp.int32
LANES, SUB = 128, 8
TAIL = 8
COLS_ROW = 3


VM = pl.BlockSpec(memory_space=pltpu.VMEM)
SM = pl.BlockSpec(memory_space=pltpu.SMEM)
ANY = pl.BlockSpec(memory_space=pl.ANY)


def call(kernel, ins, in_specs, outs, out_specs=None, scratch=(), flops=1 << 21):
    return pl.pallas_call(
        kernel,
        in_specs=in_specs,
        out_shape=outs,
        out_specs=out_specs or [VM] * len(outs),
        scratch_shapes=list(scratch),
        compiler_params=pltpu.CompilerParams(vmem_limit_bytes=24 << 20),
        cost_estimate=pl.CostEstimate(flops=flops, bytes_accessed=1 << 20, transcendentals=0),
    )(*ins)


def f32(*shape):
    return jax.ShapeDtypeStruct(shape, F32)


def iota(shape, dim):
    return lax.broadcasted_iota(I32, shape, dim)


def total(x):
    return jnp.sum(x, axis=(0, 1), keepdims=True)


def split3(x):
    hi = x.astype(BF16)
    rest = x - hi.astype(F32)
    mid = rest.astype(BF16)
    low = (rest - mid.astype(F32)).astype(BF16)
    return jnp.concatenate([hi, mid, low], axis=1)


def exact_pick(pick, values):
    wide = values.shape[1]
    out = jnp.dot(pick, split3(values), preferred_element_type=F32)
    return out[:, :wide] + out[:, wide : 2 * wide] + out[:, 2 * wide :]


def by_rows(tiles, order, start, row_of, row_blocks):
    lane = iota((SUB, LANES), 1)
    groups = LANES // SUB
    out = jnp.zeros((SUB, LANES), F32)
    for block in range(row_blocks):

        def step(n, acc):
            slot = order[n]
            return acc + tiles[slot].astype(F32) * row_of(slot)

        acc = lax.fori_loop(start[block], start[block + 1], step, jnp.zeros((LANES, LANES), F32))
        for g in range(groups):
            sums = jnp.sum(acc[g * SUB : (g + 1) * SUB], axis=1, keepdims=True)
            out = jnp.where(lane == block * groups + g, sums, out)
    return out


def by_cols(tiles, rows, count, vec, spread, msg):
    slots = tiles.shape[0]
    groups = LANES // SUB
    for k in range(spread.shape[0] // SUB):
        spread[k * SUB : (k + 1) * SUB, :] = jnp.broadcast_to(vec[:, k : k + 1], (SUB, LANES))
    msg[0:slots, :] = jnp.zeros((slots, LANES), F32)

    def chunk(c, carry):
        base = pl.multiple_of(c * SUB, SUB)
        lines = []
        for s in range(SUB):
            slot = base + s
            at = pl.multiple_of(rows[slot] * LANES, LANES)
            prod = tiles[slot].astype(F32) * spread[pl.ds(at, LANES), :]
            part = jnp.sum(prod.reshape(groups, SUB, LANES), axis=0)
            line = jnp.sum(part, axis=0, keepdims=True)
            lines.append(jnp.where(slot < count, line, 0.0))
        msg[pl.ds(base, SUB), :] = jnp.concatenate(lines, axis=0)
        return carry

    lax.fori_loop(0, (count + SUB - 1) // SUB, chunk, 0)


def start_kernel(row_blocks, rows, cols, count, tiles_hbm, w_hbm, part, tiles, w, order, start, sems):
    slots = tiles.shape[0]
    w_copy = pltpu.make_async_copy(w_hbm, w, sems.at[0])
    t_copy = pltpu.make_async_copy(tiles_hbm, tiles, sems.at[1])
    w_copy.start()
    t_copy.start()
    live = count[0]
    for b in range(row_blocks + 1):
        start[b] = 0

    def tally(t, carry):
        start[rows[t] + 1] += 1
        return carry

    lax.fori_loop(0, live, tally, 0)
    for b in range(row_blocks):
        start[b + 1] += start[b]

    def place(t, carry):
        r = rows[t]
        at = start[r]
        order[at] = t
        start[r] = at + 1
        return carry

    lax.fori_loop(0, live, place, 0)
    for b in range(row_blocks, 0, -1):
        start[b] = start[b - 1]
    start[0] = 0
    w_copy.wait()
    squares = jnp.zeros((SUB, LANES), F32)
    rows_w = w.shape[0]
    step_rows = min(rows_w, 512)
    for b in range(0, rows_w, step_rows):
        block = w[b : b + step_rows, :]
        squares = squares + jnp.sum((block * block).reshape(step_rows // SUB, SUB, LANES), axis=0)
    part[SUB : 2 * SUB, :] = squares
    t_copy.wait()
    part[0:SUB, :] = by_rows(tiles, order, start, lambda s: w[pl.ds(cols[s], 1), :], row_blocks)


def prep_kernel(labels, ids, cols_line, count, mask_out, label_out, cols_out, own_out):
    def to_grid(index, value):
        n = index.shape[1]
        left = jnp.where((index & (SUB - 1)) == iota((SUB, n), 0), value, 0.0).astype(BF16)
        right = ((index >> 3) == iota((LANES, n), 0)).astype(F32).astype(BF16)
        return lax.dot_general(left, right, (((1,), (1,)), ((), ())), preferred_element_type=F32)

    row_total, slots = labels.shape[1], cols_line.shape[1]
    label_out[...] = to_grid(iota((1, row_total), 1), labels[...].astype(F32))
    mask_out[...] = jnp.minimum(to_grid(ids[...], jnp.ones(ids.shape, F32)), 1.0)
    line = jnp.where(iota((1, slots), 1) < count[0], cols_line[...], -1).astype(F32)
    twice = jnp.concatenate([line, line], axis=1)
    cols_out[...] = jnp.broadcast_to(twice, (SUB, LANES))
    wide = jnp.broadcast_to(twice, (slots, LANES))
    own = jnp.where(iota((slots, LANES), 0) == iota((slots, LANES), 1), wide, 0.0)
    own_out[...] = jnp.broadcast_to(jnp.sum(own, axis=1, keepdims=True), (slots, LANES))


def feat_sum(refs, first=0):
    out = None
    for ref, height in refs:
        for at in range(0, ref.shape[0], height):
            piece = ref[at + first : at + first + SUB, :]
            out = piece if out is None else out + piece
    return out


def parts_of(refs, slots):
    height = slots + TAIL
    return [(ref, at) for ref in refs for at in range(0, ref.shape[0], height)]


def summed(refs, slots, row):
    line = None
    for ref, at in parts_of(refs, slots):
        piece = ref[at + slots + row : at + slots + row + 1, :]
        line = piece if line is None else line + piece
    return total(line)


def slot_cols(refs, slots):
    parts = parts_of(refs, slots)
    low = iota((1, LANES), 1) < slots
    lines = []
    for a, b in zip(parts[::2], parts[1::2], strict=True):
        first, second = (r[at + slots + COLS_ROW : at + slots + COLS_ROW + 1, :] for r, at in (a, b))
        lines.append(jnp.where(low, first, second))
    return jnp.concatenate(lines, axis=1)


def slot_values(refs, slots):
    return jnp.concatenate([ref[at : at + slots, :] for ref, at in parts_of(refs, slots)], axis=0)


def write_tail(msg, slots, lines):
    pad = jnp.zeros((TAIL - len(lines), LANES), F32)
    msg[slots : slots + TAIL, :] = jnp.concatenate([*lines, pad], axis=0)


def line_of(x):
    return jnp.sum(x, axis=0, keepdims=True)


def margin_kernel(n_f, scale, rows, count, tiles, mask, label, cols, *refs):
    got, (msg, m_out, c_out, e_out, ww_out, spread) = refs[:n_f], refs[n_f:]
    slots = tiles.shape[0]
    pieces = [(ref, 2 * SUB) for ref in got]
    m = feat_sum(pieces)
    ww_out[...] = feat_sum(pieces, SUB)
    chance = jax.nn.sigmoid(m)
    c_out[...] = scale * mask[...] * chance * (1.0 - chance)
    e = chance - label[...]
    m_out[...] = m
    e_out[...] = e
    by_cols(tiles, rows, count[0], e, spread, msg)
    zero = jnp.zeros((1, LANES), F32)
    write_tail(msg, slots, [zero, zero, zero, cols[0:1, :]])


def match_kernel(n_i, own, *refs):
    got, (match,) = refs[:n_i], refs[n_i:]
    slots = own.shape[0]
    line = slot_cols(got, slots)
    for at in range(0, line.shape[1], LANES):
        same = own[...] == line[:, at : at + LANES]
        match[:, at : at + LANES] = same.astype(F32).astype(BF16)


def forward_kernel(n_i, row_blocks, order, start, tiles, match, *refs):
    got, (out, picked) = refs[:n_i], refs[n_i:]
    slots = tiles.shape[0]
    picked[...] = exact_pick(match[...], slot_values(got, slots))
    out[...] = by_rows(tiles, order, start, lambda s: picked[pl.ds(s, 1), :], row_blocks)


def first_kernel(n_f, rows, count, tiles, m, c, e, *refs):
    got, (msg, v_out, spread) = refs[:n_f], refs[n_f:]
    slots = tiles.shape[0]
    v = -(LAMBDA * m[...] + feat_sum([(ref, SUB) for ref in got]))
    v_out[...] = v
    u = c[...] * v
    by_cols(tiles, rows, count[0], u, spread, msg)
    s = -e[...]
    write_tail(msg, slots, [line_of(-LAMBDA * m[...] * s + s * v), line_of(u * v)])


def next_kernel(n_f, n_i, first, rows, count, tiles, m, c, ww, *refs):
    got, msgs = refs[:n_f], refs[n_f : n_f + n_i]
    vec, num, msg, vec_out, num_out, spread = refs[n_f + n_i :]
    slots = tiles.shape[0]
    mm, cc = m[...], c[...]

    def at(ref, k):
        return ref[k * SUB : (k + 1) * SUB, :]

    gram_r = feat_sum([(ref, SUB) for ref in got])
    rr_new = summed(msgs, slots, 0)
    cur_r = summed(msgs, slots, 1)
    if first:
        e, v = vec[0], vec[1]
        v_r, s_r = v[...], -e[...]
        v_d, s_d, gram_d = v_r, s_r, gram_r
        a_r = a_d = jnp.full((1, 1), -LAMBDA, F32)
        rr = dd = a_r * a_r * total(ww[...]) + rr_new
        cur = cur_r
    else:
        (old,) = vec
        v_r, v_d, s_r, s_d = (at(old, k) for k in range(4))
        numbers = num[0]
        rr_old, dd, cur, a_r, a_d = (numbers[k : k + 1, 0:1] for k in range(5))
        rr = a_r * a_r * total(ww[...]) + rr_new
        beta = rr / rr_old
        dd = rr + beta * beta * dd
        cur = cur_r + 2.0 * beta * summed(msgs, slots, 2) + beta * beta * cur
        a_d = a_r + beta * a_d
        v_d = v_r + beta * v_d
        s_d = s_r + beta * s_d
        gram_d = gram_r + beta * at(old, 4)
    alpha = rr / (cur + LAMBDA * dd)
    v_r = v_r - alpha * (gram_d + LAMBDA * v_d)
    s_r = s_r - alpha * (cc * v_d + LAMBDA * s_d)
    a_r = a_r - alpha * (LAMBDA * a_d)
    u = cc * v_r
    by_cols(tiles, rows, count[0], u, spread, msg)
    write_tail(
        msg, slots, [line_of(a_r * mm * s_r + s_r * v_r), line_of(u * v_r), line_of(u * v_d)]
    )
    for k, value in enumerate((v_r, v_d, s_r, s_d, gram_d)):
        vec_out[k * SUB : (k + 1) * SUB, :] = value
    beta_out = jnp.zeros((1, 1), F32) if first else beta
    lines = [rr, dd, cur, a_r, a_d, alpha, beta_out, jnp.zeros((1, 1), F32)]
    num_out[...] = jnp.concatenate([jnp.broadcast_to(x, (1, LANES)) for x in lines], axis=0)


def last_kernel(n_i, slots, ww, w, index, *refs):
    iters = ITERS
    msgs = [refs[k * n_i : (k + 1) * n_i] for k in range(iters + 1)]
    nums = refs[(iters + 1) * n_i : (iters + 1) * n_i + iters - 1]
    step_out, res_out = refs[-2:]
    own_blocks = step_out.shape[0]
    basis = iters + 2
    zero, one = jnp.zeros((1, 1), F32), jnp.ones((1, 1), F32)

    def unit(k):
        return [one if j == k else zero for j in range(basis)]

    def plus(x, factor, y):
        return [a + factor * b for a, b in zip(x, y, strict=True)]

    res = [-LAMBDA * one, -one] + [zero] * iters
    step, direction, curved = [zero] * basis, res, unit(2)
    for k in range(iters):
        if k < iters - 1:
            rr, dd, cur, alpha, beta = (nums[k][j : j + 1, 0:1] for j in (0, 1, 2, 5, 6))
            a_r = nums[k][3:4, 0:1]
        else:
            rr_old, dd_old, cur_old = rr, dd, cur
            rr = a_r * a_r * total(ww[...]) + summed(msgs[k + 1], slots, 0)
            beta = rr / rr_old
            dd = rr + beta * beta * dd_old
            cur = summed(msgs[k + 1], slots, 1) + beta * beta * cur_old
            cur = cur + 2.0 * beta * summed(msgs[k + 1], slots, 2)
            alpha = rr / (cur + LAMBDA * dd)
        if k:
            direction = plus(res, beta, direction)
            curved = plus(unit(2 + k), beta, curved)
        step = plus(step, alpha, direction)
        res = plus(res, -alpha, plus(curved, LAMBDA, direction))

    values = [slot_values(group, slots) for group in msgs]
    mixed = []
    for weights_of in (step, res):
        mix = weights_of[1] * values[0]
        for k in range(1, iters + 1):
            mix = mix + weights_of[1 + k] * values[k]
        mixed.append(mix)
    line = slot_cols(msgs[0], slots)
    offset = index[0] * own_blocks
    own = (iota((own_blocks, LANES), 0) + offset).astype(F32)
    pick = jnp.concatenate(
        [(own == line[:, a : a + LANES]).astype(F32).astype(BF16) for a in range(0, line.shape[1], LANES)],
        axis=1,
    )
    mine = w[pl.ds(pl.multiple_of(offset, own_blocks), own_blocks), :]
    for out, mix, factor in ((step_out, mixed[0], step[0]), (res_out, mixed[1], res[0])):
        out[...] = factor * mine + exact_pick(pick, mix)


def exchange(x, axis):
    size = lax.axis_size(axis)
    if size & (size - 1) or size > 8:
        return [lax.all_gather(x, axis, axis=0, tiled=True)]
    return [x] + [
        lax.ppermute(x, axis, [(i, i ^ k) for i in range(size)]) for k in range(size - 1, 0, -1)
    ]


def body(tiles, tile_rows, tile_cols, tile_count, sample_ids, labels, weights):
    slots, edge = tiles.shape[2], tiles.shape[3]
    row_total, feat_len = labels.shape[1], weights.shape[1]
    row_blocks, col_blocks = row_total // edge, feat_len // edge
    own_len = feat_len // lax.axis_size("inst")
    own_blocks = own_len // edge
    tiles = tiles.reshape(slots, edge, edge)
    rows, cols = tile_rows.reshape(slots), tile_cols.reshape(slots)
    count = tile_count.reshape(1)
    scale = float(row_total) / float(sample_ids.shape[1])
    index = lax.axis_index("inst").astype(I32).reshape(1)
    spread = pltpu.VMEM((row_total, LANES), F32)
    grid = f32(SUB, LANES)
    msg_shape = f32(slots + TAIL, LANES)

    part, tiles, w, order, start = call(
        functools.partial(start_kernel, row_blocks),
        (rows, cols, count, tiles, weights.reshape(col_blocks, edge)),
        [SM, SM, SM, ANY, ANY],
        [
            f32(2 * SUB, LANES),
            jax.ShapeDtypeStruct((slots, edge, edge), BF16),
            f32(col_blocks, edge),
            jax.ShapeDtypeStruct((slots,), I32),
            jax.ShapeDtypeStruct((row_blocks + 1,), I32),
        ],
        [VM, VM, VM, SM, SM],
        [pltpu.SemaphoreType.DMA((2,))],
    )
    mask, label, cols_line, own = call(
        prep_kernel,
        (labels, sample_ids, cols.reshape(1, slots), count),
        [VM, VM, VM, SM],
        [grid, grid, grid, f32(slots, LANES)],
    )
    got = exchange(part, "feat")
    n_f = len(got)
    msg, m, c, e, ww = call(
        functools.partial(margin_kernel, n_f, scale),
        (rows, count, tiles, mask, label, cols_line, *got),
        [SM, SM] + [VM] * (4 + n_f),
        [msg_shape, grid, grid, grid, grid],
        scratch=[spread],
    )
    msgs = exchange(msg, "inst")
    n_i = len(msgs)
    (match,) = call(
        functools.partial(match_kernel, n_i),
        (own, *msgs),
        [VM] * (1 + n_i),
        [jax.ShapeDtypeStruct((slots, slots * lax.axis_size("inst")), BF16)],
    )

    def forward(msgs):
        (out,) = call(
            functools.partial(forward_kernel, n_i, row_blocks),
            (order, start, tiles, match, *msgs),
            [SM, SM] + [VM] * (2 + n_i),
            [grid],
            scratch=[pltpu.VMEM((slots, LANES), F32)],
        )
        return exchange(out, "feat")

    history = [msgs]
    got = forward(msgs)
    msg, v = call(
        functools.partial(first_kernel, n_f),
        (rows, count, tiles, m, c, e, *got),
        [SM, SM] + [VM] * (4 + n_f),
        [msg_shape, grid],
        scratch=[spread],
    )
    history.append(exchange(msg, "inst"))
    state, nums = [e, v], []
    for k in range(ITERS - 1):
        got = forward(history[-1])
        if k == 0:
            kernel = functools.partial(wrapped_first, n_f, n_i)
            extra = state
        else:
            kernel = functools.partial(wrapped_next, n_f, n_i)
            extra = state + [nums[-1]]
        msg, vec, num = call(
            kernel,
            (rows, count, tiles, m, c, ww, *got, *history[-1], *extra),
            [SM, SM] + [VM] * (4 + n_f + n_i + len(extra)),
            [msg_shape, f32(5 * SUB, LANES), grid],
            scratch=[spread],
        )
        history.append(exchange(msg, "inst"))
        state = [vec]
        nums.append(num)
    step, res = call(
        functools.partial(last_kernel, n_i, slots),
        (ww, w, index, *(ref for group in history for ref in group), *nums),
        [VM, VM, SM] + [VM] * (n_i * (ITERS + 1) + len(nums)),
        [f32(own_blocks, edge), f32(own_blocks, edge)],
    )
    return step.reshape(1, own_len), res.reshape(1, own_len)


def wrapped_first(n_f, n_i, *refs):
    base = 6 + n_f + n_i
    next_kernel(n_f, n_i, True, *refs[:base], refs[base : base + 2], (), *refs[base + 2 :])


def wrapped_next(n_f, n_i, *refs):
    base = 6 + n_f + n_i
    next_kernel(
        n_f, n_i, False, *refs[:base], refs[base : base + 1], refs[base + 1 : base + 2], *refs[base + 2 :]
    )


def solution(mesh):
    return jax.shard_map(
        body,
        mesh=mesh,
        in_specs=(
            P(("groups", "inst"), "feat", None, None, None),
            P(("groups", "inst"), "feat", None),
            P(("groups", "inst"), "feat", None),
            P(("groups", "inst"), "feat"),
            P(("groups", "inst"), None),
            P(("groups", "inst"), None),
            P(("groups", "feat"), None),
        ),
        out_specs=(P(("groups", "feat"), "inst"), P(("groups", "feat"), "inst")),
        check_vma=False,
    )
```

```python
import functools

import jax
import jax.numpy as jnp
from jax import lax
from jax.experimental import pallas as pl
from jax.experimental.pallas import tpu as pltpu
from jax.sharding import PartitionSpec as P

ITERS = 3
LAMBDA = 0.02

F32, BF16, I32 = jnp.float32, jnp.bfloat16, jnp.int32
LANES, SUB = 128, 8
TAIL = 8
COLS_ROW = 3


VM = pl.BlockSpec(memory_space=pltpu.VMEM)
SM = pl.BlockSpec(memory_space=pltpu.SMEM)
ANY = pl.BlockSpec(memory_space=pl.ANY)
HBM = pl.BlockSpec(memory_space=pltpu.HBM)


def call(kernel, ins, in_specs, outs, out_specs=None, scratch=(), flops=1 << 21):
    return pl.pallas_call(
        kernel,
        in_specs=in_specs,
        out_shape=outs,
        out_specs=out_specs or [VM] * len(outs),
        scratch_shapes=list(scratch),
        compiler_params=pltpu.CompilerParams(vmem_limit_bytes=24 << 20),
        cost_estimate=pl.CostEstimate(flops=flops, bytes_accessed=1 << 20, transcendentals=0),
    )(*ins)


def f32(*shape):
    return jax.ShapeDtypeStruct(shape, F32)


def iota(shape, dim):
    return lax.broadcasted_iota(I32, shape, dim)


def total(x):
    return jnp.sum(x, axis=(0, 1), keepdims=True)


def split3(x):
    hi = x.astype(BF16).astype(F32)
    rest = x - hi
    mid = rest.astype(BF16).astype(F32)
    return hi, mid, (rest - mid).astype(BF16).astype(F32)


def exact_pick(pick, values):
    wide = values.shape[1]
    pieces = jnp.concatenate(split3(values), axis=1).astype(BF16)
    out = jnp.dot(pick, pieces, preferred_element_type=F32)
    return out[:, :wide] + out[:, wide : 2 * wide] + out[:, 2 * wide :]


def left_of(pieces):
    return jnp.concatenate([*pieces, jnp.zeros((SUB, LANES), F32)], axis=0).astype(BF16)


def fold3(acc, at=0):
    return acc[at : at + SUB] + acc[at + SUB : at + 2 * SUB] + acc[at + 2 * SUB : at + 3 * SUB]


def save_pieces(x, pieces):
    slots = x.shape[0]
    for p, piece in enumerate(split3(x)):
        pieces[p * slots : (p + 1) * slots, :] = piece


def masked_line(pieces, slots, slot, mask):
    return [
        mask * jnp.broadcast_to(pieces[p * slots + slot : p * slots + slot + 1, :], (SUB, LANES))
        for p in range(3)
    ]


def by_rows(turned, pieces, row_mask):
    slots = turned.shape[0]
    acc = jnp.zeros((4 * SUB, LANES), F32)
    for s in range(0, slots, 2):
        left = [
            left_of(masked_line(pieces, slots, t, row_mask[t * SUB : (t + 1) * SUB, :]))
            for t in (s, s + 1)
        ]
        right = jnp.concatenate([turned[s], turned[s + 1]], axis=0)
        acc = acc + jnp.dot(
            jnp.concatenate(left, axis=1), right, preferred_element_type=F32
        )
    return fold3(acc)


def by_cols(tiles, row_pick, vec, msg):
    slots = tiles.shape[0]
    pieces = jnp.concatenate(split3(vec), axis=1)
    pad = jnp.zeros((LANES - SUB, 3 * LANES), F32)
    stacked = jnp.concatenate([pieces, pad], axis=0).astype(BF16)
    lines = jnp.dot(row_pick[...], stacked, preferred_element_type=F32)
    sub = iota((SUB, LANES), 0)
    for g in range(0, slots, SUB):
        group = [lines[g : g + SUB, p * LANES : (p + 1) * LANES] for p in range(3)]
        acc = jnp.zeros((4 * SUB, LANES), F32)
        for s in range(0, SUB, 2):
            left = [left_of([jnp.where(sub == t, piece, 0.0) for piece in group]) for t in (s, s + 1)]
            right = jnp.concatenate([tiles[g + s], tiles[g + s + 1]], axis=0)
            acc = acc + jnp.dot(jnp.concatenate(left, axis=1), right, preferred_element_type=F32)
        msg[g : g + SUB, :] = fold3(acc)


CHUNKS = 4


def start_kernel(
    rows_hbm, cols_hbm, count_hbm, tiles_hbm, w_hbm,
    part, tiles, w, row_mask,
    rows, cols, count, picked, pieces, sems,
):
    slots = tiles.shape[0]
    each = slots // CHUNKS
    small = [
        pltpu.make_async_copy(src, dst, sems.at[k])
        for k, (src, dst) in enumerate(((cols_hbm, cols), (rows_hbm, rows), (count_hbm, count)))
    ]
    w_copy = pltpu.make_async_copy(w_hbm, w, sems.at[3])
    t_copies = [
        pltpu.make_async_copy(
            tiles_hbm.at[pl.ds(k * each, each)], tiles.at[pl.ds(k * each, each)], sems.at[4 + k]
        )
        for k in range(CHUNKS)
    ]
    for copy in [*small, w_copy, *t_copies]:
        copy.start()
    for copy in small:
        copy.wait()
    live = count[0]
    sub = iota((SUB, LANES), 0)
    for t in range(slots):
        row = jnp.where(t < live, rows[t], -1)
        row_mask[t * SUB : (t + 1) * SUB, :] = (sub == row).astype(F32)
    w_copy.wait()
    for t in range(slots):
        col = jnp.where(t < live, cols[t], 0)
        picked[t : t + 1, :] = w[pl.ds(col, 1), :]
    save_pieces(picked[...], pieces)
    squares = jnp.zeros((SUB, LANES), F32)
    rows_w = w.shape[0]
    step_rows = min(rows_w, 256)
    for b in range(0, rows_w, step_rows):
        block = w[b : b + step_rows, :]
        squares = squares + jnp.sum((block * block).reshape(step_rows // SUB, SUB, LANES), axis=0)
    part[SUB : 2 * SUB, :] = squares
    acc = jnp.zeros((6 * SUB, 2 * LANES), F32)
    for s in range(0, slots, 4):
        if s % each == 0:
            t_copies[s // each].wait()
        a, b, c, d = (
            masked_line(pieces, slots, t, row_mask[t * SUB : (t + 1) * SUB, :]) for t in range(s, s + 4)
        )
        left = [jnp.concatenate([*x, *y], axis=0).astype(BF16) for x, y in ((a, c), (b, d))]
        right = [jnp.concatenate([tiles[t], tiles[t + 1]], axis=1) for t in (s, s + 2)]
        acc = acc + lax.dot_general(
            jnp.concatenate(left, axis=1),
            jnp.concatenate(right, axis=0),
            (((1,), (1,)), ((), ())),
            preferred_element_type=F32,
        )
    part[0:SUB, :] = fold3(acc[:, :LANES]) + fold3(acc[:, LANES:], 3 * SUB)


def turn_kernel(tiles, turned):
    for t in range(tiles.shape[0]):
        turned[t] = tiles[t].T


def prep_kernel(ids, rows_line, cols_line, count, mask_out, pick_out, cols_out, own_out):
    slots = cols_line.shape[1]
    n = ids.shape[1]
    left = ((ids[...] >> 7) == iota((SUB, n), 0)).astype(F32).astype(BF16)
    right = ((ids[...] & (LANES - 1)) == iota((LANES, n), 0)).astype(F32).astype(BF16)
    hits = lax.dot_general(left, right, (((1,), (1,)), ((), ())), preferred_element_type=F32)
    mask_out[...] = jnp.minimum(hits, 1.0)
    live = iota((1, slots), 1) < count[...]

    def both(line):
        line = jnp.where(live, line, -1).astype(F32)
        line = jnp.concatenate([line, line], axis=1)
        wide = jnp.broadcast_to(line, (slots, LANES))
        own = jnp.where(iota((slots, LANES), 0) == iota((slots, LANES), 1), wide, 0.0)
        return line, jnp.broadcast_to(jnp.sum(own, axis=1, keepdims=True), (slots, LANES))

    line, own = both(cols_line[...])
    cols_out[...] = jnp.broadcast_to(line, (SUB, LANES))
    own_out[...] = own
    _, own = both(rows_line[...])
    pick_out[...] = (own == iota((slots, LANES), 1).astype(F32)).astype(F32).astype(BF16)


def feat_sum(refs, first=0):
    out = None
    for ref, height in refs:
        for at in range(0, ref.shape[0], height):
            piece = ref[at + first : at + first + SUB, :]
            out = piece if out is None else out + piece
    return out


def parts_of(refs, slots):
    height = slots + TAIL
    return [(ref, at) for ref in refs for at in range(0, ref.shape[0], height)]


def summed(refs, slots, row):
    line = None
    for ref, at in parts_of(refs, slots):
        piece = ref[at + slots + row : at + slots + row + 1, :]
        line = piece if line is None else line + piece
    return total(line)


def slot_cols(refs, slots):
    parts = parts_of(refs, slots)
    low = iota((1, LANES), 1) < slots
    lines = []
    for a, b in zip(parts[::2], parts[1::2], strict=True):
        first, second = (r[at + slots + COLS_ROW : at + slots + COLS_ROW + 1, :] for r, at in (a, b))
        lines.append(jnp.where(low, first, second))
    return jnp.concatenate(lines, axis=1)


def slot_values(refs, slots):
    return jnp.concatenate([ref[at : at + slots, :] for ref, at in parts_of(refs, slots)], axis=0)


def write_tail(msg, slots, lines):
    pad = jnp.zeros((TAIL - len(lines), LANES), F32)
    msg[slots : slots + TAIL, :] = jnp.concatenate([*lines, pad], axis=0)


def line_of(x):
    return jnp.sum(x, axis=0, keepdims=True)


def margin_kernel(n_f, scale, tiles, row_pick, mask, labels, cols, *refs):
    got, (msg, m_out, c_out, e_out, ww_out) = refs[:n_f], refs[n_f:]
    slots = tiles.shape[0]
    pieces = [(ref, 2 * SUB) for ref in got]
    m = feat_sum(pieces)
    chance = jax.nn.sigmoid(m)
    e = chance - labels[...].astype(F32)
    by_cols(tiles, row_pick, e, msg)
    zero = jnp.zeros((1, LANES), F32)
    write_tail(msg, slots, [zero, zero, zero, cols[0:1, :]])
    ww_out[...] = feat_sum(pieces, SUB)
    c_out[...] = scale * mask[...] * chance * (1.0 - chance)
    m_out[...] = m
    e_out[...] = e


def match_kernel(n_i, own, *refs):
    got, (match,) = refs[:n_i], refs[n_i:]
    slots = own.shape[0]
    line = slot_cols(got, slots)
    for at in range(0, line.shape[1], LANES):
        same = own[...] == line[:, at : at + LANES]
        match[:, at : at + LANES] = same.astype(F32).astype(BF16)


def forward_kernel(n_i, turned, row_mask, match, *refs):
    got, (out, pieces) = refs[:n_i], refs[n_i:]
    slots = turned.shape[0]
    save_pieces(exact_pick(match[...], slot_values(got, slots)), pieces)
    out[...] = by_rows(turned, pieces, row_mask)


def first_kernel(n_f, tiles, row_pick, m, c, e, *refs):
    got, (msg, v_out) = refs[:n_f], refs[n_f:]
    slots = tiles.shape[0]
    v = -(LAMBDA * m[...] + feat_sum([(ref, SUB) for ref in got]))
    v_out[...] = v
    u = c[...] * v
    by_cols(tiles, row_pick, u, msg)
    s = -e[...]
    write_tail(msg, slots, [line_of(-LAMBDA * m[...] * s + s * v), line_of(u * v)])


NUMBERS = ("rr", "dd", "cur", "a_r", "a_d", "alpha", "beta")


def numbers_of(num):
    return {name: num[k : k + 1, 0:1] for k, name in enumerate(NUMBERS)}


def save_numbers(num, values):
    lines = [jnp.broadcast_to(values[name], (1, LANES)) for name in NUMBERS]
    num[...] = jnp.concatenate([*lines, jnp.zeros((1, LANES), F32)], axis=0)


def advance(msgs, slots, ww, old):
    rr_new, cur_r = summed(msgs, slots, 0), summed(msgs, slots, 1)
    if old is None:
        a_r = a_d = jnp.full((1, 1), -LAMBDA, F32)
        rr = a_r * a_r * total(ww[...]) + rr_new
        dd, cur, beta = rr, cur_r, jnp.zeros((1, 1), F32)
    else:
        cross = summed(msgs, slots, 2)
        rr = old["a_r"] * old["a_r"] * total(ww[...]) + rr_new
        beta = rr / old["rr"]
        a_d = old["a_r"] + beta * old["a_d"]
        dd = rr + beta * beta * old["dd"]
        cur = cur_r + 2.0 * beta * cross + beta * beta * old["cur"]
        a_r = old["a_r"]
    alpha = rr / (cur + LAMBDA * dd)
    a_r = a_r - alpha * (LAMBDA * a_d)
    return {"rr": rr, "dd": dd, "cur": cur, "a_r": a_r, "a_d": a_d, "alpha": alpha, "beta": beta}


def at(ref, k):
    return ref[k * SUB : (k + 1) * SUB, :]


def save_all(ref, values):
    for k, value in enumerate(values):
        ref[k * SUB : (k + 1) * SUB, :] = value


def numbers_kernel(n_i, slots, first, m, c, ww, *refs):
    msgs = refs[:n_i]
    vec_out, num_out = refs[-2:]
    if first:
        e, v = refs[n_i:-2]
        new = advance(msgs, slots, ww, None)
        v_r, s_r = v[...], -e[...]
        v_d, s_d, gram = v_r, s_r, jnp.zeros((SUB, LANES), F32)
    else:
        v, gram_d, vec, num = refs[n_i:-2]
        new = advance(msgs, slots, ww, numbers_of(num))
        v_r, s_r = v[...], at(vec, 2)
        v_d = v_r + new["beta"] * at(vec, 1)
        s_d = s_r + new["beta"] * at(vec, 3)
        gram = new["beta"] * gram_d[...]
    v_r = v_r - new["alpha"] * (gram + LAMBDA * v_d)
    s_r = s_r - new["alpha"] * (c[...] * v_d + LAMBDA * s_d)
    save_all(vec_out, (v_r, v_d, s_r, s_d, new["a_r"] * m[...] * s_r, gram))
    save_numbers(num_out, new)


def next_kernel(n_f, tiles, row_pick, c, vec, num, *refs):
    got, (msg, *kept) = refs[:n_f], refs[n_f:]
    slots = tiles.shape[0]
    gram = feat_sum([(ref, SUB) for ref in got])
    v = at(vec, 0) - numbers_of(num)["alpha"] * gram
    u = c[...] * v
    by_cols(tiles, row_pick, u, msg)
    write_tail(
        msg, slots, [line_of(at(vec, 4) + at(vec, 2) * v), line_of(u * v), line_of(u * at(vec, 1))]
    )
    for out, value in zip(kept, (v, gram + at(vec, 5))):
        out[...] = value


def dense_kernel(n_i, slots, iters, w, index, *refs):
    msgs = [refs[k * n_i : (k + 1) * n_i] for k in range(iters)]
    nums = [numbers_of(num) for num in refs[iters * n_i : iters * n_i + iters - 1]]
    res_out, dir_out, step_out, curved_out, pick_out = refs[-5:]
    own_blocks = res_out.shape[0]
    line = slot_cols(msgs[0], slots)
    offset = index[0] * own_blocks
    own = (iota((own_blocks, LANES), 0) + offset).astype(F32)
    for a in range(0, line.shape[1], LANES):
        pick_out[:, a : a + LANES] = (own == line[:, a : a + LANES]).astype(F32).astype(BF16)
    mine = w[pl.ds(pl.multiple_of(offset, own_blocks), own_blocks), :]
    res = -LAMBDA * mine - exact_pick(pick_out[...], slot_values(msgs[0], slots))
    step = jnp.zeros_like(res)
    for k in range(iters - 1):
        image = exact_pick(pick_out[...], slot_values(msgs[k + 1], slots))
        if k == 0:
            direction, curved = res, image
        else:
            direction = res + nums[k]["beta"] * direction
            curved = image + nums[k]["beta"] * curved
        step = step + nums[k]["alpha"] * direction
        res = res - nums[k]["alpha"] * (curved + LAMBDA * direction)
    res_out[...] = res
    dir_out[...] = direction
    step_out[...] = step
    curved_out[...] = curved


def last_kernel(n_i, slots, ww, num, res, direction, step, curved, pick, *refs):
    msgs, (step_out, res_out) = refs[:n_i], refs[n_i:]
    image = exact_pick(pick[...], slot_values(msgs, slots))
    new = advance(msgs, slots, ww, numbers_of(num))
    last = res[...] + new["beta"] * direction[...]
    step_out[...] = step[...] + new["alpha"] * last
    image = image + new["beta"] * curved[...] + LAMBDA * last
    res_out[...] = res[...] - new["alpha"] * image


def exchange(x, axis):
    size = lax.axis_size(axis)
    if size & (size - 1) or size > 8:
        return [lax.all_gather(x, axis, axis=0, tiled=True)]
    return [x] + [
        lax.ppermute(x, axis, [(i, i ^ k) for i in range(size)]) for k in range(size - 1, 0, -1)
    ]


def in_hbm(x):
    return pltpu.with_memory_space_constraint(x, pltpu.HBM)


def body(tiles, tile_rows, tile_cols, tile_count, sample_ids, labels, weights):
    slots, edge = tiles.shape[2], tiles.shape[3]
    row_total, feat_len = labels.shape[1], weights.shape[1]
    row_blocks, col_blocks = row_total // edge, feat_len // edge
    assert row_blocks == SUB and edge == LANES and 2 * slots == LANES
    inst = lax.axis_size("inst")
    own_len = feat_len // inst
    own_blocks = own_len // edge
    tiles = tiles.reshape(slots, edge, edge)
    scale = float(row_total) / float(sample_ids.shape[1])
    index = lax.axis_index("inst").astype(I32).reshape(1)
    grid, msg_shape = f32(SUB, LANES), f32(slots + TAIL, LANES)
    tile_shape = jax.ShapeDtypeStruct((slots, edge, edge), BF16)
    picks = jax.ShapeDtypeStruct

    part, tiles, w, row_mask = call(
        start_kernel,
        (
            in_hbm(tile_rows.reshape(slots)),
            in_hbm(tile_cols.reshape(slots)),
            tile_count.reshape(1),
            in_hbm(tiles),
            in_hbm(weights.reshape(col_blocks, edge)),
        ),
        [HBM] * 2 + [ANY] + [HBM] * 2,
        [f32(2 * SUB, LANES), tile_shape, f32(col_blocks, edge), f32(slots * SUB, LANES)],
        scratch=[
            pltpu.SMEM((slots,), I32),
            pltpu.SMEM((slots,), I32),
            pltpu.SMEM((1,), I32),
            pltpu.VMEM((slots, LANES), F32),
            pltpu.VMEM((3 * slots, LANES), F32),
            pltpu.SemaphoreType.DMA((4 + CHUNKS,)),
        ],
    )
    mask, row_pick, cols_line, own = call(
        prep_kernel,
        (
            sample_ids,
            tile_rows.reshape(1, slots),
            tile_cols.reshape(1, slots),
            tile_count.reshape(1, 1),
        ),
        [VM] * 4,
        [grid, picks((slots, LANES), BF16), grid, f32(slots, LANES)],
    )
    (turned,) = call(turn_kernel, (tiles,), [VM], [tile_shape])
    got = exchange(part, "feat")
    n_f = len(got)
    msg, m, c, e, ww = call(
        functools.partial(margin_kernel, n_f, scale),
        (tiles, row_pick, mask, labels.reshape(SUB, LANES), cols_line, *got),
        [VM] * (5 + n_f),
        [msg_shape, grid, grid, grid, grid],
    )
    msgs = exchange(msg, "inst")
    n_i = len(msgs)
    (match,) = call(
        functools.partial(match_kernel, n_i),
        (own, *msgs),
        [VM] * (1 + n_i),
        [picks((slots, slots * inst), BF16)],
    )

    def forward(msgs):
        (out,) = call(
            functools.partial(forward_kernel, n_i),
            (turned, row_mask, match, *msgs),
            [VM] * (3 + n_i),
            [grid],
            scratch=[pltpu.VMEM((3 * slots, LANES), F32)],
        )
        return exchange(out, "feat")

    got = forward(msgs)
    msg, v = call(
        functools.partial(first_kernel, n_f),
        (tiles, row_pick, m, c, e, *got),
        [VM] * (5 + n_f),
        [msg_shape, grid],
    )
    history = [msgs, exchange(msg, "inst")]
    state, nums = (e, v), []
    for k in range(ITERS - 1):
        got = forward(history[-1])
        vec, num = call(
            functools.partial(numbers_kernel, n_i, slots, k == 0),
            (m, c, ww, *history[-1], *state),
            [VM] * (3 + n_i + len(state)),
            [f32(6 * SUB, LANES), grid],
        )
        msg, *kept = call(
            functools.partial(next_kernel, n_f),
            (tiles, row_pick, c, vec, num, *got),
            [VM] * (5 + n_f),
            [msg_shape] + [grid, grid] * (k < ITERS - 2),
        )
        history.append(exchange(msg, "inst"))
        state = (*kept, vec, num)
        nums.append(num)
    block = f32(own_blocks, edge)
    *dense, pick = call(
        functools.partial(dense_kernel, n_i, slots, ITERS),
        (w, index, *(ref for group in history[:ITERS] for ref in group), *nums),
        [VM, SM] + [VM] * (n_i * ITERS + len(nums)),
        [block, block, block, block, picks((own_blocks, slots * inst), BF16)],
    )
    step, res = call(
        functools.partial(last_kernel, n_i, slots),
        (ww, nums[-1], *dense, pick, *history[-1]),
        [VM] * (7 + n_i),
        [block, block],
    )
    return step.reshape(1, own_len), res.reshape(1, own_len)


def solution(mesh):
    return jax.shard_map(
        body,
        mesh=mesh,
        in_specs=(
            P(("groups", "inst"), "feat", None, None, None),
            P(("groups", "inst"), "feat", None),
            P(("groups", "inst"), "feat", None),
            P(("groups", "inst"), "feat"),
            P(("groups", "inst"), None),
            P(("groups", "inst"), None),
            P(("groups", "feat"), None),
        ),
        out_specs=(P(("groups", "feat"), "inst"), P(("groups", "feat"), "inst")),
        check_vma=False,
    )
```

```python
import functools

import jax
import jax.numpy as jnp
from jax import lax
from jax.experimental import pallas as pl
from jax.experimental.pallas import tpu as pltpu
from jax.sharding import PartitionSpec as P

ITERS = 3
LAMBDA = 0.02
ORDERS = ((3, 2, 1), (1, 3, 2)) + ((3, 2, 1),) * (ITERS - 1)

F32, BF16, I32 = jnp.float32, jnp.bfloat16, jnp.int32
LANES, SUB = 128, 8
TAIL = 8
COLS_ROW = 3


VM = pl.BlockSpec(memory_space=pltpu.VMEM)
SM = pl.BlockSpec(memory_space=pltpu.SMEM)
ANY = pl.BlockSpec(memory_space=pl.ANY)
HBM = pl.BlockSpec(memory_space=pltpu.HBM)


def call(kernel, ins, in_specs, outs, out_specs=None, scratch=(), flops=1 << 21):
    return pl.pallas_call(
        kernel,
        in_specs=in_specs,
        out_shape=outs,
        out_specs=out_specs or [VM] * len(outs),
        scratch_shapes=list(scratch),
        compiler_params=pltpu.CompilerParams(vmem_limit_bytes=24 << 20),
        cost_estimate=pl.CostEstimate(flops=flops, bytes_accessed=1 << 20, transcendentals=0),
    )(*ins)


def f32(*shape):
    return jax.ShapeDtypeStruct(shape, F32)


def iota(shape, dim):
    return lax.broadcasted_iota(I32, shape, dim)


def total(x):
    return jnp.sum(x, axis=(0, 1), keepdims=True)


def split3(x):
    hi = x.astype(BF16).astype(F32)
    rest = x - hi
    mid = rest.astype(BF16).astype(F32)
    return hi, mid, (rest - mid).astype(BF16).astype(F32)


def exact_pick(pick, values):
    wide = values.shape[1]
    pieces = jnp.concatenate(split3(values), axis=1).astype(BF16)
    out = jnp.dot(pick, pieces, preferred_element_type=F32)
    return out[:, :wide] + out[:, wide : 2 * wide] + out[:, 2 * wide :]


def left_of(pieces):
    return jnp.concatenate([*pieces, jnp.zeros((SUB, LANES), F32)], axis=0).astype(BF16)


def fold3(acc, at=0):
    return acc[at : at + SUB] + acc[at + SUB : at + 2 * SUB] + acc[at + 2 * SUB : at + 3 * SUB]


def save_pieces(x, pieces):
    slots = x.shape[0]
    for p, piece in enumerate(split3(x)):
        pieces[p * slots : (p + 1) * slots, :] = piece


def masked_line(pieces, slots, slot, mask):
    return [
        mask * jnp.broadcast_to(pieces[p * slots + slot : p * slots + slot + 1, :], (SUB, LANES))
        for p in range(3)
    ]


def by_rows(turned, pieces, row_mask):
    slots = turned.shape[0]
    acc = jnp.zeros((4 * SUB, LANES), F32)
    for s in range(0, slots, 2):
        left = [
            left_of(masked_line(pieces, slots, t, row_mask[t * SUB : (t + 1) * SUB, :]))
            for t in (s, s + 1)
        ]
        right = jnp.concatenate([turned[s], turned[s + 1]], axis=0)
        acc = acc + jnp.dot(
            jnp.concatenate(left, axis=1), right, preferred_element_type=F32
        )
    return fold3(acc)


def by_cols(tiles, row_pick, vec, msg):
    slots = tiles.shape[0]
    pieces = jnp.concatenate(split3(vec), axis=1)
    pad = jnp.zeros((LANES - SUB, 3 * LANES), F32)
    stacked = jnp.concatenate([pieces, pad], axis=0).astype(BF16)
    lines = jnp.dot(row_pick[...], stacked, preferred_element_type=F32)
    sub = iota((SUB, LANES), 0)
    for g in range(0, slots, SUB):
        group = [lines[g : g + SUB, p * LANES : (p + 1) * LANES] for p in range(3)]
        acc = jnp.zeros((4 * SUB, LANES), F32)
        for s in range(0, SUB, 2):
            left = [left_of([jnp.where(sub == t, piece, 0.0) for piece in group]) for t in (s, s + 1)]
            right = jnp.concatenate([tiles[g + s], tiles[g + s + 1]], axis=0)
            acc = acc + jnp.dot(jnp.concatenate(left, axis=1), right, preferred_element_type=F32)
        msg[g : g + SUB, :] = fold3(acc)


def start_kernel(
    count, rows_hbm, cols_hbm, tiles_hbm, w_hbm,
    part, tiles, w, row_mask,
    rows, cols, picked, pieces, sems,
):
    slots = tiles.shape[0]
    small = [
        pltpu.make_async_copy(src, dst, sems.at[k])
        for k, (src, dst) in enumerate(((cols_hbm, cols), (rows_hbm, rows)))
    ]
    w_copy = pltpu.make_async_copy(w_hbm, w, sems.at[3])
    t_copy = pltpu.make_async_copy(tiles_hbm, tiles, sems.at[2])
    for copy in [*small, w_copy, t_copy]:
        copy.start()
    for copy in small:
        copy.wait()
    live = count[0, 0]
    sub = iota((SUB, LANES), 0)
    for t in range(slots):
        row = jnp.where(t < live, rows[t], -1)
        row_mask[t * SUB : (t + 1) * SUB, :] = (sub == row).astype(F32)
    w_copy.wait()
    for t in range(slots):
        col = jnp.where(t < live, cols[t], 0)
        picked[t : t + 1, :] = w[pl.ds(col, 1), :]
    save_pieces(picked[...], pieces)
    squares = jnp.zeros((SUB, LANES), F32)
    rows_w = w.shape[0]
    step_rows = min(rows_w, 256)
    for b in range(0, rows_w, step_rows):
        block = w[b : b + step_rows, :]
        squares = squares + jnp.sum((block * block).reshape(step_rows // SUB, SUB, LANES), axis=0)
    part[SUB : 2 * SUB, :] = squares
    acc = jnp.zeros((6 * SUB, 2 * LANES), F32)
    t_copy.wait()
    for s in range(0, slots, 4):
        a, b, c, d = (
            masked_line(pieces, slots, t, row_mask[t * SUB : (t + 1) * SUB, :]) for t in range(s, s + 4)
        )
        left = [jnp.concatenate([*x, *y], axis=0).astype(BF16) for x, y in ((a, c), (b, d))]
        right = [jnp.concatenate([tiles[t], tiles[t + 1]], axis=1) for t in (s, s + 2)]
        acc = acc + lax.dot_general(
            jnp.concatenate(left, axis=1),
            jnp.concatenate(right, axis=0),
            (((1,), (1,)), ((), ())),
            preferred_element_type=F32,
        )
    part[0:SUB, :] = fold3(acc[:, :LANES]) + fold3(acc[:, LANES:], 3 * SUB)


def turn_kernel(tiles, turned):
    for t in range(tiles.shape[0]):
        turned[t] = tiles[t].T


def prep_kernel(ids, rows_line, cols_line, count, mask_out, pick_out, cols_out, own_out):
    slots = cols_line.shape[1]
    n = ids.shape[1]
    left = ((ids[...] >> 7) == iota((SUB, n), 0)).astype(F32).astype(BF16)
    right = ((ids[...] & (LANES - 1)) == iota((LANES, n), 0)).astype(F32).astype(BF16)
    hits = lax.dot_general(left, right, (((1,), (1,)), ((), ())), preferred_element_type=F32)
    mask_out[...] = jnp.minimum(hits, 1.0)
    live = iota((1, slots), 1) < count[0, 0]

    def both(line):
        line = jnp.where(live, line, -1).astype(F32)
        line = jnp.concatenate([line, line], axis=1)
        wide = jnp.broadcast_to(line, (slots, LANES))
        own = jnp.where(iota((slots, LANES), 0) == iota((slots, LANES), 1), wide, 0.0)
        return line, jnp.broadcast_to(jnp.sum(own, axis=1, keepdims=True), (slots, LANES))

    line, own = both(cols_line[...])
    cols_out[...] = jnp.broadcast_to(line, (SUB, LANES))
    own_out[...] = own
    _, own = both(rows_line[...])
    pick_out[...] = (own == iota((slots, LANES), 1).astype(F32)).astype(F32).astype(BF16)


def feat_sum(refs, first=0):
    out = None
    for ref, height in refs:
        for at in range(0, ref.shape[0], height):
            piece = ref[at + first : at + first + SUB, :]
            out = piece if out is None else out + piece
    return out


def parts_of(refs, slots):
    height = slots + TAIL
    return [(ref, at) for ref in refs for at in range(0, ref.shape[0], height)]


def summed(refs, slots, row):
    line = None
    for ref, at in parts_of(refs, slots):
        piece = ref[at + slots + row : at + slots + row + 1, :]
        line = piece if line is None else line + piece
    return total(line)


def slot_cols(refs, slots):
    parts = parts_of(refs, slots)
    low = iota((1, LANES), 1) < slots
    lines = []
    for a, b in zip(parts[::2], parts[1::2], strict=True):
        first, second = (r[at + slots + COLS_ROW : at + slots + COLS_ROW + 1, :] for r, at in (a, b))
        lines.append(jnp.where(low, first, second))
    return jnp.concatenate(lines, axis=1)


def slot_values(refs, slots):
    return jnp.concatenate([ref[at : at + slots, :] for ref, at in parts_of(refs, slots)], axis=0)


def write_tail(msg, slots, lines):
    pad = jnp.zeros((TAIL - len(lines), LANES), F32)
    msg[slots : slots + TAIL, :] = jnp.concatenate([*lines, pad], axis=0)


def line_of(x):
    return jnp.sum(x, axis=0, keepdims=True)


def margin_kernel(n_f, scale, tiles, row_pick, mask, labels, cols, *refs):
    got, (msg, m_out, c_out, e_out, ww_out) = refs[:n_f], refs[n_f:]
    slots = tiles.shape[0]
    pieces = [(ref, 2 * SUB) for ref in got]
    m = feat_sum(pieces)
    chance = jax.nn.sigmoid(m)
    e = chance - labels[...].astype(F32)
    by_cols(tiles, row_pick, e, msg)
    zero = jnp.zeros((1, LANES), F32)
    write_tail(msg, slots, [zero, zero, zero, cols[0:1, :]])
    ww_out[...] = feat_sum(pieces, SUB)
    c_out[...] = scale * mask[...] * chance * (1.0 - chance)
    m_out[...] = m
    e_out[...] = e


def match_kernel(n_i, own, *refs):
    got, (match,) = refs[:n_i], refs[n_i:]
    slots = own.shape[0]
    line = slot_cols(got, slots)
    for at in range(0, line.shape[1], LANES):
        same = own[...] == line[:, at : at + LANES]
        match[:, at : at + LANES] = same.astype(F32).astype(BF16)


def forward_kernel(n_i, order, turned, row_mask, match, *refs):
    got, (out, pieces) = sorted_as(order, refs[:n_i]), refs[n_i:]
    slots = turned.shape[0]
    save_pieces(exact_pick(match[...], slot_values(got, slots)), pieces)
    out[...] = by_rows(turned, pieces, row_mask)


def first_kernel(n_f, tiles, row_pick, m, c, e, *refs):
    got, (msg, v_out) = refs[:n_f], refs[n_f:]
    slots = tiles.shape[0]
    v = -(LAMBDA * m[...] + feat_sum([(ref, SUB) for ref in got]))
    v_out[...] = v
    u = c[...] * v
    by_cols(tiles, row_pick, u, msg)
    s = -e[...]
    write_tail(msg, slots, [line_of(-LAMBDA * m[...] * s + s * v), line_of(u * v)])


NUMBERS = ("rr", "dd", "cur", "a_r", "a_d", "alpha", "beta")


def numbers_of(num):
    return {name: num[k : k + 1, 0:1] for k, name in enumerate(NUMBERS)}


def save_numbers(num, values):
    lines = [jnp.broadcast_to(values[name], (1, LANES)) for name in NUMBERS]
    num[...] = jnp.concatenate([*lines, jnp.zeros((1, LANES), F32)], axis=0)


def advance(msgs, slots, ww, old):
    rr_new, cur_r = summed(msgs, slots, 0), summed(msgs, slots, 1)
    if old is None:
        a_r = a_d = jnp.full((1, 1), -LAMBDA, F32)
        rr = a_r * a_r * total(ww[...]) + rr_new
        dd, cur, beta = rr, cur_r, jnp.zeros((1, 1), F32)
    else:
        cross = summed(msgs, slots, 2)
        rr = old["a_r"] * old["a_r"] * total(ww[...]) + rr_new
        beta = rr / old["rr"]
        a_d = old["a_r"] + beta * old["a_d"]
        dd = rr + beta * beta * old["dd"]
        cur = cur_r + 2.0 * beta * cross + beta * beta * old["cur"]
        a_r = old["a_r"]
    alpha = rr / (cur + LAMBDA * dd)
    a_r = a_r - alpha * (LAMBDA * a_d)
    return {"rr": rr, "dd": dd, "cur": cur, "a_r": a_r, "a_d": a_d, "alpha": alpha, "beta": beta}


def at(ref, k):
    return ref[k * SUB : (k + 1) * SUB, :]


def save_all(ref, values):
    for k, value in enumerate(values):
        ref[k * SUB : (k + 1) * SUB, :] = value


def numbers_kernel(n_i, slots, first, m, c, ww, *refs):
    msgs = refs[:n_i]
    vec_out, num_out = refs[-2:]
    if first:
        e, v = refs[n_i:-2]
        new = advance(msgs, slots, ww, None)
        v_r, s_r = v[...], -e[...]
        v_d, s_d, gram = v_r, s_r, jnp.zeros((SUB, LANES), F32)
    else:
        v, gram_d, vec, num = refs[n_i:-2]
        new = advance(msgs, slots, ww, numbers_of(num))
        v_r, s_r = v[...], at(vec, 2)
        v_d = v_r + new["beta"] * at(vec, 1)
        s_d = s_r + new["beta"] * at(vec, 3)
        gram = new["beta"] * gram_d[...]
    v_r = v_r - new["alpha"] * (gram + LAMBDA * v_d)
    s_r = s_r - new["alpha"] * (c[...] * v_d + LAMBDA * s_d)
    save_all(vec_out, (v_r, v_d, s_r, s_d, new["a_r"] * m[...] * s_r, gram))
    save_numbers(num_out, new)


def next_kernel(n_f, tiles, row_pick, c, vec, num, *refs):
    got, (msg, *kept) = refs[:n_f], refs[n_f:]
    slots = tiles.shape[0]
    gram = feat_sum([(ref, SUB) for ref in got])
    v = at(vec, 0) - numbers_of(num)["alpha"] * gram
    u = c[...] * v
    by_cols(tiles, row_pick, u, msg)
    write_tail(
        msg, slots, [line_of(at(vec, 4) + at(vec, 2) * v), line_of(u * v), line_of(u * at(vec, 1))]
    )
    for out, value in zip(kept, (v, gram + at(vec, 5))):
        out[...] = value


def dense_kernel(n_i, orders, slots, iters, w, index, *refs):
    msgs = [sorted_as(orders[k], refs[k * n_i : (k + 1) * n_i]) for k in range(iters)]
    nums = [numbers_of(num) for num in refs[iters * n_i : iters * n_i + iters - 1]]
    res_out, dir_out, step_out, curved_out, pick_out = refs[-5:]
    own_blocks = res_out.shape[0]
    line = slot_cols(msgs[0], slots)
    offset = index[0] * own_blocks
    own = (iota((own_blocks, LANES), 0) + offset).astype(F32)
    for a in range(0, line.shape[1], LANES):
        pick_out[:, a : a + LANES] = (own == line[:, a : a + LANES]).astype(F32).astype(BF16)
    mine = w[pl.ds(pl.multiple_of(offset, own_blocks), own_blocks), :]
    res = -LAMBDA * mine - exact_pick(pick_out[...], slot_values(msgs[0], slots))
    step = jnp.zeros_like(res)
    for k in range(iters - 1):
        image = exact_pick(pick_out[...], slot_values(msgs[k + 1], slots))
        if k == 0:
            direction, curved = res, image
        else:
            direction = res + nums[k]["beta"] * direction
            curved = image + nums[k]["beta"] * curved
        step = step + nums[k]["alpha"] * direction
        res = res - nums[k]["alpha"] * (curved + LAMBDA * direction)
    res_out[...] = res
    dir_out[...] = direction
    step_out[...] = step
    curved_out[...] = curved


def last_kernel(n_i, order, slots, ww, num, res, direction, step, curved, pick, *refs):
    msgs, (step_out, res_out) = sorted_as(order, refs[:n_i]), refs[n_i:]
    image = exact_pick(pick[...], slot_values(msgs, slots))
    new = advance(msgs, slots, ww, numbers_of(num))
    last = res[...] + new["beta"] * direction[...]
    step_out[...] = step[...] + new["alpha"] * last
    image = image + new["beta"] * curved[...] + LAMBDA * last
    res_out[...] = res[...] - new["alpha"] * image


def exchange(x, axis, order=(3, 2, 1)):
    size = lax.axis_size(axis)
    if size != 4:
        return [lax.all_gather(x, axis, axis=0, tiled=True)]
    return [x] + [lax.ppermute(x, axis, [(i, i ^ k) for i in range(size)]) for k in order]


def sorted_as(order, refs):
    if len(refs) == 1:
        return refs
    return [refs[0]] + [refs[1 + order.index(k)] for k in (3, 2, 1)]


def in_hbm(x):
    return pltpu.with_memory_space_constraint(x, pltpu.HBM)


def body(tiles, tile_rows, tile_cols, tile_count, sample_ids, labels, weights):
    slots, edge = tiles.shape[2], tiles.shape[3]
    row_total, feat_len = labels.shape[1], weights.shape[1]
    row_blocks, col_blocks = row_total // edge, feat_len // edge
    assert row_blocks == SUB and edge == LANES and 2 * slots == LANES
    inst = lax.axis_size("inst")
    own_len = feat_len // inst
    own_blocks = own_len // edge
    tiles = tiles.reshape(slots, edge, edge)
    scale = float(row_total) / float(sample_ids.shape[1])
    index = lax.axis_index("inst").astype(I32).reshape(1)
    grid, msg_shape = f32(SUB, LANES), f32(slots + TAIL, LANES)
    tile_shape = jax.ShapeDtypeStruct((slots, edge, edge), BF16)
    picks = jax.ShapeDtypeStruct

    part, tiles, w, row_mask = call(
        start_kernel,
        (
            tile_count,
            in_hbm(tile_rows.reshape(slots)),
            in_hbm(tile_cols.reshape(slots)),
            in_hbm(tiles),
            in_hbm(weights.reshape(col_blocks, edge)),
        ),
        [SM] + [HBM] * 4,
        [f32(2 * SUB, LANES), tile_shape, f32(col_blocks, edge), f32(slots * SUB, LANES)],
        scratch=[
            pltpu.SMEM((slots,), I32),
            pltpu.SMEM((slots,), I32),
            pltpu.VMEM((slots, LANES), F32),
            pltpu.VMEM((3 * slots, LANES), F32),
            pltpu.SemaphoreType.DMA((4,)),
        ],
    )
    mask, row_pick, cols_line, own = call(
        prep_kernel,
        (
            sample_ids,
            tile_rows.reshape(1, slots),
            tile_cols.reshape(1, slots),
            tile_count,
        ),
        [VM] * 3 + [SM],
        [grid, picks((slots, LANES), BF16), grid, f32(slots, LANES)],
    )
    (turned,) = call(turn_kernel, (tiles,), [VM], [tile_shape])
    got = exchange(part, "feat")
    n_f = len(got)
    msg, m, c, e, ww = call(
        functools.partial(margin_kernel, n_f, scale),
        (tiles, row_pick, mask, labels.reshape(SUB, LANES), cols_line, *got),
        [VM] * (5 + n_f),
        [msg_shape, grid, grid, grid, grid],
    )
    msgs = exchange(msg, "inst", ORDERS[0])
    n_i = len(msgs)
    (match,) = call(
        functools.partial(match_kernel, n_i),
        (own, *msgs),
        [VM] * (1 + n_i),
        [picks((slots, slots * inst), BF16)],
    )

    def forward(msgs, order):
        (out,) = call(
            functools.partial(forward_kernel, n_i, order),
            (turned, row_mask, match, *msgs),
            [VM] * (3 + n_i),
            [grid],
            scratch=[pltpu.VMEM((3 * slots, LANES), F32)],
        )
        return exchange(out, "feat")

    got = forward(msgs, ORDERS[0])
    msg, v = call(
        functools.partial(first_kernel, n_f),
        (tiles, row_pick, m, c, e, *got),
        [VM] * (5 + n_f),
        [msg_shape, grid],
    )
    history = [msgs, exchange(msg, "inst", ORDERS[1])]
    state, nums = (e, v), []
    for k in range(ITERS - 1):
        got = forward(history[-1], ORDERS[k + 1])
        vec, num = call(
            functools.partial(numbers_kernel, n_i, slots, k == 0),
            (m, c, ww, *history[-1], *state),
            [VM] * (3 + n_i + len(state)),
            [f32(6 * SUB, LANES), grid],
        )
        msg, *kept = call(
            functools.partial(next_kernel, n_f),
            (tiles, row_pick, c, vec, num, *got),
            [VM] * (5 + n_f),
            [msg_shape] + [grid, grid] * (k < ITERS - 2),
        )
        history.append(exchange(msg, "inst", ORDERS[k + 2]))
        state = (*kept, vec, num)
        nums.append(num)
    block = f32(own_blocks, edge)
    *dense, pick = call(
        functools.partial(dense_kernel, n_i, ORDERS, slots, ITERS),
        (w, index, *(ref for group in history[:ITERS] for ref in group), *nums),
        [VM, SM] + [VM] * (n_i * ITERS + len(nums)),
        [block, block, block, block, picks((own_blocks, slots * inst), BF16)],
    )
    step, res = call(
        functools.partial(last_kernel, n_i, ORDERS[ITERS], slots),
        (ww, nums[-1], *dense, pick, *history[-1]),
        [VM] * (7 + n_i),
        [block, block],
    )
    return step.reshape(1, own_len), res.reshape(1, own_len)


def solution(mesh):
    return jax.shard_map(
        body,
        mesh=mesh,
        in_specs=(
            P(("groups", "inst"), "feat", None, None, None),
            P(("groups", "inst"), "feat", None),
            P(("groups", "inst"), "feat", None),
            P(("groups", "inst"), "feat"),
            P(("groups", "inst"), None),
            P(("groups", "inst"), None),
            P(("groups", "feat"), None),
        ),
        out_specs=(P(("groups", "feat"), "inst"), P(("groups", "feat"), "inst")),
        check_vma=False,
    )
```

```python
import functools

import jax
import jax.numpy as jnp
from jax import lax
from jax.experimental import pallas as pl
from jax.experimental.pallas import tpu as pltpu
from jax.sharding import PartitionSpec as P

ITERS = 3
LAMBDA = 0.02
ORDERS = ((1, 2, 3),) * ITERS + ((3, 2, 1),)
FEAT_ORDER = (1, 2, 3)

F32, BF16, I32 = jnp.float32, jnp.bfloat16, jnp.int32
LANES, SUB = 128, 8
TAIL = 8
COLS_ROW = 3
CAP, CAP_RUN = 17, 512
SHORT, SHORT_PAD = 24, 32


VM = pl.BlockSpec(memory_space=pltpu.VMEM)
SM = pl.BlockSpec(memory_space=pltpu.SMEM)
ANY = pl.BlockSpec(memory_space=pl.ANY)
HBM = pl.BlockSpec(memory_space=pltpu.HBM)


def call(kernel, ins, in_specs, outs, out_specs=None, scratch=(), flops=1 << 21):
    return pl.pallas_call(
        kernel,
        in_specs=in_specs,
        out_shape=outs,
        out_specs=out_specs or [VM] * len(outs),
        scratch_shapes=list(scratch),
        compiler_params=pltpu.CompilerParams(vmem_limit_bytes=24 << 20),
        cost_estimate=pl.CostEstimate(flops=flops, bytes_accessed=1 << 20, transcendentals=0),
    )(*ins)


def f32(*shape):
    return jax.ShapeDtypeStruct(shape, F32)


def iota(shape, dim):
    return lax.broadcasted_iota(I32, shape, dim)


def total(x):
    return jnp.sum(x, axis=(0, 1), keepdims=True)


def split3(x):
    hi = x.astype(BF16).astype(F32)
    rest = x - hi
    mid = rest.astype(BF16).astype(F32)
    return hi, mid, (rest - mid).astype(BF16).astype(F32)


def exact_pick(pick, values):
    wide = values.shape[1]
    pieces = jnp.concatenate(split3(values), axis=1).astype(BF16)
    out = jnp.dot(pick, pieces, preferred_element_type=F32)
    return out[:, :wide] + out[:, wide : 2 * wide] + out[:, 2 * wide :]


def left_of(pieces):
    return jnp.concatenate([*pieces, jnp.zeros((SUB, LANES), F32)], axis=0).astype(BF16)


def fold3(acc, at=0):
    return acc[at : at + SUB] + acc[at + SUB : at + 2 * SUB] + acc[at + 2 * SUB : at + 3 * SUB]


def save_pieces(x, pieces):
    slots = x.shape[0]
    for p, piece in enumerate(split3(x)):
        pieces[p * slots : (p + 1) * slots, :] = piece


def masked_line(pieces, slots, slot, mask):
    return [
        mask * jnp.broadcast_to(pieces[p * slots + slot : p * slots + slot + 1, :], (SUB, LANES))
        for p in range(3)
    ]


def by_rows(turned, pieces, row_mask):
    slots = turned.shape[0]
    acc = jnp.zeros((4 * SUB, LANES), F32)
    for s in range(0, slots, 2):
        left = [
            left_of(masked_line(pieces, slots, t, row_mask[t * SUB : (t + 1) * SUB, :]))
            for t in (s, s + 1)
        ]
        right = jnp.concatenate([turned[s], turned[s + 1]], axis=0)
        acc = acc + jnp.dot(
            jnp.concatenate(left, axis=1), right, preferred_element_type=F32
        )
    return fold3(acc)


def by_cols(tiles, row_pick, vec, msg):
    slots = tiles.shape[0]
    pieces = jnp.concatenate(split3(vec), axis=1)
    pad = jnp.zeros((LANES - SUB, 3 * LANES), F32)
    stacked = jnp.concatenate([pieces, pad], axis=0).astype(BF16)
    lines = jnp.dot(row_pick[...], stacked, preferred_element_type=F32)
    sub = iota((SUB, LANES), 0)
    for g in range(0, slots, SUB):
        group = [lines[g : g + SUB, p * LANES : (p + 1) * LANES] for p in range(3)]
        acc = jnp.zeros((4 * SUB, LANES), F32)
        for s in range(0, SUB, 2):
            left = [left_of([jnp.where(sub == t, piece, 0.0) for piece in group]) for t in (s, s + 1)]
            right = jnp.concatenate([tiles[g + s], tiles[g + s + 1]], axis=0)
            acc = acc + jnp.dot(jnp.concatenate(left, axis=1), right, preferred_element_type=F32)
        msg[g : g + SUB, :] = fold3(acc)


def start_kernel(
    count, rows_hbm, cols_hbm, tiles_hbm, w_hbm,
    part, tiles, w, row_mask,
    rows, cols, picked, pieces, sems,
):
    slots = tiles.shape[0]
    small = [
        pltpu.make_async_copy(src, dst, sems.at[k])
        for k, (src, dst) in enumerate(((cols_hbm, cols), (rows_hbm, rows)))
    ]
    w_copy = pltpu.make_async_copy(w_hbm, w, sems.at[3])
    t_copy = pltpu.make_async_copy(tiles_hbm, tiles, sems.at[2])
    for copy in [*small, w_copy, t_copy]:
        copy.start()
    for copy in small:
        copy.wait()
    live = count[0, 0]
    sub = iota((SUB, LANES), 0)
    for t in range(slots):
        row = jnp.where(t < live, rows[t], -1)
        row_mask[t * SUB : (t + 1) * SUB, :] = (sub == row).astype(F32)
    w_copy.wait()
    for t in range(slots):
        col = jnp.where(t < live, cols[t], 0)
        picked[t : t + 1, :] = w[pl.ds(col, 1), :]
    save_pieces(picked[...], pieces)
    squares = jnp.zeros((SUB, LANES), F32)
    rows_w = w.shape[0]
    step_rows = min(rows_w, 256)
    for b in range(0, rows_w, step_rows):
        block = w[b : b + step_rows, :]
        squares = squares + jnp.sum((block * block).reshape(step_rows // SUB, SUB, LANES), axis=0)
    part[SUB : 2 * SUB, :] = squares
    acc = jnp.zeros((6 * SUB, 2 * LANES), F32)
    t_copy.wait()
    for s in range(0, slots, 4):
        a, b, c, d = (
            masked_line(pieces, slots, t, row_mask[t * SUB : (t + 1) * SUB, :]) for t in range(s, s + 4)
        )
        left = [jnp.concatenate([*x, *y], axis=0).astype(BF16) for x, y in ((a, c), (b, d))]
        right = [jnp.concatenate([tiles[t], tiles[t + 1]], axis=1) for t in (s, s + 2)]
        acc = acc + lax.dot_general(
            jnp.concatenate(left, axis=1),
            jnp.concatenate(right, axis=0),
            (((1,), (1,)), ((), ())),
            preferred_element_type=F32,
        )
    part[0:SUB, :] = fold3(acc[:, :LANES]) + fold3(acc[:, LANES:], 3 * SUB)


def turn_kernel(tiles, turned):
    for t in range(tiles.shape[0]):
        turned[t] = tiles[t].T


def ranks(line, column, parts):
    shift = CAP_RUN.bit_length() - 1
    run, run_column = line.astype(I32) >> shift, column.astype(I32) >> shift
    sub, lane = iota(column.shape, 0), iota(column.shape, 1)
    same = (run == run_column) & (sub < lane)
    if parts == 2:
        same = same & ((sub < LANES // 2) == (lane < LANES // 2))
    return run, jnp.sum(same.astype(F32), axis=0, keepdims=True).astype(I32)


def column_of(line, rows):
    wide = jnp.broadcast_to(line, (rows, LANES))
    own = jnp.where(iota((rows, LANES), 0) == iota((rows, LANES), 1), wide, 0.0)
    return jnp.broadcast_to(jnp.sum(own, axis=1, keepdims=True), (rows, LANES))


def prep_kernel(
    ids, rows_line, cols_line, count, index, mask_out, pick_out, cols_out, own_out, *send_out
):
    slots = cols_line.shape[1]
    n = ids.shape[1]
    left = ((ids[...] >> 7) == iota((SUB, n), 0)).astype(F32).astype(BF16)
    right = ((ids[...] & (LANES - 1)) == iota((LANES, n), 0)).astype(F32).astype(BF16)
    hits = lax.dot_general(left, right, (((1,), (1,)), ((), ())), preferred_element_type=F32)
    mask_out[...] = jnp.minimum(hits, 1.0)
    live = iota((1, slots), 1) < count[0, 0]

    def both(line):
        line = jnp.where(live, line, -1).astype(F32)
        line = jnp.concatenate([line, line], axis=1)
        return line, column_of(line, slots)

    line, own = both(cols_line[...])
    cols_out[...] = jnp.broadcast_to(line, (SUB, LANES))
    own_out[...] = own
    for out in send_out:
        run, rank = ranks(line, own, 1)
        row = iota((SHORT, LANES), 0)
        for j, k in enumerate((0, 3, 2, 1)):
            sent = (row == rank) & (run == (index[0] ^ k))
            out[j * SHORT : (j + 1) * SHORT, :] = sent.astype(F32)[:, :slots].astype(BF16)
    _, own = both(rows_line[...])
    pick_out[...] = (own == iota((slots, LANES), 1).astype(F32)).astype(F32).astype(BF16)


def feat_sum(refs, first=0):
    out = None
    for ref, height in refs:
        for at in range(0, ref.shape[0], height):
            piece = ref[at + first : at + first + SUB, :]
            out = piece if out is None else out + piece
    return out


def parts_of(refs, slots):
    height = slots + TAIL
    return [(ref, at) for ref in refs for at in range(0, ref.shape[0], height)]


def summed(refs, slots, row):
    line = None
    for ref, at in parts_of(refs, slots):
        piece = ref[at + slots + row : at + slots + row + 1, :]
        line = piece if line is None else line + piece
    return total(line)


def slot_cols(refs, slots):
    parts = parts_of(refs, slots)
    low = iota((1, LANES), 1) < slots
    lines = []
    for a, b in zip(parts[::2], parts[1::2], strict=True):
        first, second = (r[at + slots + COLS_ROW : at + slots + COLS_ROW + 1, :] for r, at in (a, b))
        lines.append(jnp.where(low, first, second))
    return jnp.concatenate(lines, axis=1)


def slot_values(refs, slots):
    return jnp.concatenate([ref[at : at + slots, :] for ref, at in parts_of(refs, slots)], axis=0)


def write_tail(msg, slots, lines):
    pad = jnp.zeros((TAIL - len(lines), LANES), F32)
    msg[slots : slots + TAIL, :] = jnp.concatenate([*lines, pad], axis=0)


def line_of(x):
    return jnp.sum(x, axis=0, keepdims=True)


def margin_kernel(n_f, scale, tiles, row_pick, mask, labels, cols, *refs):
    got, (msg, m_out, c_out, e_out, ww_out) = refs[:n_f], refs[n_f:]
    slots = tiles.shape[0]
    pieces = [(ref, 2 * SUB) for ref in got]
    m = feat_sum(pieces)
    chance = jax.nn.sigmoid(m)
    e = chance - labels[...].astype(F32)
    by_cols(tiles, row_pick, e, msg)
    zero = jnp.zeros((1, LANES), F32)
    write_tail(msg, slots, [zero, zero, zero, cols[0:1, :]])
    ww_out[...] = feat_sum(pieces, SUB)
    c_out[...] = scale * mask[...] * chance * (1.0 - chance)
    m_out[...] = m
    e_out[...] = e


def match_kernel(n_i, order, own, *refs):
    got, (match,) = sorted_as(order, refs[:n_i]), refs[n_i:]
    slots = own.shape[0]
    line = slot_cols(got, slots)
    for at in range(0, line.shape[1], LANES):
        same = own[...] == line[:, at : at + LANES]
        match[:, at : at + LANES] = same.astype(F32).astype(BF16)


def forward_kernel(n_i, order, turned, row_mask, match, *refs):
    got, (out, pieces) = sorted_as(order, refs[:n_i]), refs[n_i:]
    slots = turned.shape[0]
    save_pieces(exact_pick(match[...], slot_values(got, slots)), pieces)
    out[...] = by_rows(turned, pieces, row_mask)


def first_kernel(n_f, tiles, row_pick, m, c, e, *refs):
    got, (msg, v_out) = refs[:n_f], refs[n_f:]
    slots = tiles.shape[0]
    v = -(LAMBDA * m[...] + feat_sum([(ref, SUB) for ref in got]))
    v_out[...] = v
    u = c[...] * v
    by_cols(tiles, row_pick, u, msg)
    s = -e[...]
    write_tail(msg, slots, [line_of(-LAMBDA * m[...] * s + s * v), line_of(u * v)])


NUMBERS = ("rr", "dd", "cur", "a_r", "a_d", "alpha", "beta")


def numbers_of(num):
    return {name: num[k : k + 1, 0:1] for k, name in enumerate(NUMBERS)}


def save_numbers(num, values):
    lines = [jnp.broadcast_to(values[name], (1, LANES)) for name in NUMBERS]
    num[...] = jnp.concatenate([*lines, jnp.zeros((1, LANES), F32)], axis=0)


def advance(msgs, slots, ww, old, shift=0):
    rr_new, cur_r = summed(msgs, slots, shift), summed(msgs, slots, shift + 1)
    if old is None:
        a_r = a_d = jnp.full((1, 1), -LAMBDA, F32)
        rr = a_r * a_r * total(ww[...]) + rr_new
        dd, cur, beta = rr, cur_r, jnp.zeros((1, 1), F32)
    else:
        cross = summed(msgs, slots, shift + 2)
        rr = old["a_r"] * old["a_r"] * total(ww[...]) + rr_new
        beta = rr / old["rr"]
        a_d = old["a_r"] + beta * old["a_d"]
        dd = rr + beta * beta * old["dd"]
        cur = cur_r + 2.0 * beta * cross + beta * beta * old["cur"]
        a_r = old["a_r"]
    alpha = rr / (cur + LAMBDA * dd)
    a_r = a_r - alpha * (LAMBDA * a_d)
    return {"rr": rr, "dd": dd, "cur": cur, "a_r": a_r, "a_d": a_d, "alpha": alpha, "beta": beta}


def at(ref, k):
    return ref[k * SUB : (k + 1) * SUB, :]


def save_all(ref, values):
    for k, value in enumerate(values):
        ref[k * SUB : (k + 1) * SUB, :] = value


def numbers_kernel(n_i, slots, first, m, c, ww, *refs):
    msgs = refs[:n_i]
    vec_out, num_out = refs[-2:]
    if first:
        e, v = refs[n_i:-2]
        new = advance(msgs, slots, ww, None)
        v_r, s_r = v[...], -e[...]
        v_d, s_d, gram = v_r, s_r, jnp.zeros((SUB, LANES), F32)
    else:
        v, gram_d, vec, num = refs[n_i:-2]
        new = advance(msgs, slots, ww, numbers_of(num))
        v_r, s_r = v[...], at(vec, 2)
        v_d = v_r + new["beta"] * at(vec, 1)
        s_d = s_r + new["beta"] * at(vec, 3)
        gram = new["beta"] * gram_d[...]
    v_r = v_r - new["alpha"] * (gram + LAMBDA * v_d)
    s_r = s_r - new["alpha"] * (c[...] * v_d + LAMBDA * s_d)
    save_all(vec_out, (v_r, v_d, s_r, s_d, new["a_r"] * m[...] * s_r, gram))
    save_numbers(num_out, new)


def next_kernel(n_f, short, tiles, row_pick, c, vec, num, *refs):
    got, (msg, *kept) = refs[:n_f], refs[n_f:]
    slots = tiles.shape[0]
    if short:
        send, *outs, msg = refs[n_f:]
    gram = feat_sum([(ref, SUB) for ref in got])
    v = at(vec, 0) - numbers_of(num)["alpha"] * gram
    u = c[...] * v
    by_cols(tiles, row_pick, u, msg)
    lines = [line_of(at(vec, 4) + at(vec, 2) * v), line_of(u * v), line_of(u * at(vec, 1))]
    if short:
        chosen = exact_pick(send[...], msg[...])
        pad = [jnp.zeros((n, LANES), F32) for n in (CAP, SHORT - CAP - len(lines))]
        tail = jnp.concatenate([pad[0], *lines, pad[1]], axis=0)
        for j, out in enumerate(outs):
            slots_rows = chosen[j * SHORT : (j + 1) * SHORT]
            out[...] = jnp.where(iota((SHORT, LANES), 0) < CAP, slots_rows, tail)
        return
    write_tail(msg, slots, lines)
    for out, value in zip(kept, (v, gram + at(vec, 5))):
        out[...] = value


def dense_kernel(n_i, short, orders, slots, iters, w, index, *refs):
    msgs = [sorted_as(orders[k], refs[k * n_i : (k + 1) * n_i]) for k in range(iters)]
    nums = [numbers_of(num) for num in refs[iters * n_i : iters * n_i + iters - 1]]
    res_out, dir_out, step_out, curved_out, pick_out = refs[iters * n_i + iters - 1 :][:5]
    if short:
        short_out, pick_out = refs[-2:]
    own_blocks = res_out.shape[0]
    line = slot_cols(msgs[0], slots)
    offset = index[0] * own_blocks
    own = (iota((own_blocks, LANES), 0) + offset).astype(F32)
    for a in range(0, line.shape[1], LANES):
        pick_out[:, a : a + LANES] = (own == line[:, a : a + LANES]).astype(F32).astype(BF16)
    mine = w[pl.ds(pl.multiple_of(offset, own_blocks), own_blocks), :]
    res = -LAMBDA * mine - exact_pick(pick_out[...], slot_values(msgs[0], slots))
    step = jnp.zeros_like(res)
    for k in range(iters - 1):
        image = exact_pick(pick_out[...], slot_values(msgs[k + 1], slots))
        if k == 0:
            direction, curved = res, image
        else:
            direction = res + nums[k]["beta"] * direction
            curved = image + nums[k]["beta"] * curved
        step = step + nums[k]["alpha"] * direction
        res = res - nums[k]["alpha"] * (curved + LAMBDA * direction)
    if short:
        blocks = []
        for a in range(0, line.shape[1], LANES):
            pair = line[:, a : a + LANES]
            run, rank = ranks(pair, column_of(pair, LANES), 2)
            first = a // slots * SHORT_PAD
            second = iota((1, LANES), 1) >= slots
            want = rank + jnp.where(second, first + SHORT_PAD, first)
            row = iota((LANES, LANES), 0)
            blocks.append(((row == want) & (run == index[0])).astype(F32).astype(BF16))
        short_out[...] = lax.dot_general(
            pick_out[...],
            jnp.concatenate(blocks, axis=1),
            (((1,), (1,)), ((), ())),
            preferred_element_type=F32,
        ).astype(BF16)
    res_out[...] = res
    dir_out[...] = direction
    step_out[...] = step
    curved_out[...] = curved


def last_kernel(n_i, short, order, slots, ww, num, res, direction, step, curved, pick, *refs):
    msgs, (step_out, res_out) = sorted_as(order, refs[:n_i]), refs[n_i:]
    if short:
        pad = jnp.zeros((SHORT_PAD - SHORT, LANES), F32)
        values = jnp.concatenate([piece for msg in msgs for piece in (msg[...], pad)], axis=0)
        new = advance(msgs, SHORT - TAIL, ww, numbers_of(num), CAP - (SHORT - TAIL))
    else:
        values = slot_values(msgs, slots)
        new = advance(msgs, slots, ww, numbers_of(num))
    image = exact_pick(pick[...], values)
    last = res[...] + new["beta"] * direction[...]
    step_out[...] = step[...] + new["alpha"] * last
    image = image + new["beta"] * curved[...] + LAMBDA * last
    res_out[...] = res[...] - new["alpha"] * image


def exchange(x, axis, order=FEAT_ORDER):
    size = lax.axis_size(axis)
    if size != 4:
        return [lax.all_gather(x, axis, axis=0, tiled=True)]
    return [x] + [lax.ppermute(x, axis, [(i, i ^ k) for i in range(size)]) for k in order]


def exchange_each(arrays, axis):
    keys = (3, 2, 1)
    return [arrays[0]] + [
        lax.ppermute(x, axis, [(i, i ^ k) for i in range(4)])
        for k, x in zip(keys, arrays[1:], strict=True)
    ]


def sorted_as(order, refs):
    if len(refs) == 1:
        return refs
    return [refs[0]] + [refs[1 + order.index(k)] for k in (3, 2, 1)]


def in_hbm(x):
    return pltpu.with_memory_space_constraint(x, pltpu.HBM)


def body(tiles, tile_rows, tile_cols, tile_count, sample_ids, labels, weights):
    slots, edge = tiles.shape[2], tiles.shape[3]
    row_total, feat_len = labels.shape[1], weights.shape[1]
    row_blocks, col_blocks = row_total // edge, feat_len // edge
    assert row_blocks == SUB and edge == LANES and 2 * slots == LANES
    inst = lax.axis_size("inst")
    own_len = feat_len // inst
    own_blocks = own_len // edge
    tiles = tiles.reshape(slots, edge, edge)
    scale = float(row_total) / float(sample_ids.shape[1])
    index = lax.axis_index("inst").astype(I32).reshape(1)
    grid, msg_shape = f32(SUB, LANES), f32(slots + TAIL, LANES)
    short = inst == 4 and own_blocks == CAP_RUN
    tile_shape = jax.ShapeDtypeStruct((slots, edge, edge), BF16)
    picks = jax.ShapeDtypeStruct

    part, tiles, w, row_mask = call(
        start_kernel,
        (
            tile_count,
            in_hbm(tile_rows.reshape(slots)),
            in_hbm(tile_cols.reshape(slots)),
            in_hbm(tiles),
            in_hbm(weights.reshape(col_blocks, edge)),
        ),
        [SM] + [HBM] * 4,
        [f32(2 * SUB, LANES), tile_shape, f32(col_blocks, edge), f32(slots * SUB, LANES)],
        scratch=[
            pltpu.SMEM((slots,), I32),
            pltpu.SMEM((slots,), I32),
            pltpu.VMEM((slots, LANES), F32),
            pltpu.VMEM((3 * slots, LANES), F32),
            pltpu.SemaphoreType.DMA((4,)),
        ],
    )
    mask, row_pick, cols_line, own, *send = call(
        prep_kernel,
        (
            sample_ids,
            tile_rows.reshape(1, slots),
            tile_cols.reshape(1, slots),
            tile_count,
            index,
        ),
        [VM] * 3 + [SM] * 2,
        [grid, picks((slots, LANES), BF16), grid, f32(slots, LANES)]
        + [picks((4 * SHORT, slots), BF16)] * short,
    )
    (turned,) = call(turn_kernel, (tiles,), [VM], [tile_shape])
    got = exchange(part, "feat")
    n_f = len(got)
    msg, m, c, e, ww = call(
        functools.partial(margin_kernel, n_f, scale),
        (tiles, row_pick, mask, labels.reshape(SUB, LANES), cols_line, *got),
        [VM] * (5 + n_f),
        [msg_shape, grid, grid, grid, grid],
    )
    msgs = exchange(msg, "inst", ORDERS[0])
    n_i = len(msgs)
    (match,) = call(
        functools.partial(match_kernel, n_i, ORDERS[0]),
        (own, *msgs),
        [VM] * (1 + n_i),
        [picks((slots, slots * inst), BF16)],
    )

    def forward(msgs, order):
        (out,) = call(
            functools.partial(forward_kernel, n_i, order),
            (turned, row_mask, match, *msgs),
            [VM] * (3 + n_i),
            [grid],
            scratch=[pltpu.VMEM((3 * slots, LANES), F32)],
        )
        return exchange(out, "feat")

    got = forward(msgs, ORDERS[0])
    msg, v = call(
        functools.partial(first_kernel, n_f),
        (tiles, row_pick, m, c, e, *got),
        [VM] * (5 + n_f),
        [msg_shape, grid],
    )
    history = [msgs, exchange(msg, "inst", ORDERS[1])]
    state, nums = (e, v), []
    for k in range(ITERS - 1):
        got = forward(history[-1], ORDERS[k + 1])
        vec, num = call(
            functools.partial(numbers_kernel, n_i, slots, k == 0),
            (m, c, ww, *history[-1], *state),
            [VM] * (3 + n_i + len(state)),
            [f32(6 * SUB, LANES), grid],
        )
        if short and k == ITERS - 2:
            to_each = call(
                functools.partial(next_kernel, n_f, True),
                (tiles, row_pick, c, vec, num, *got, *send),
                [VM] * (6 + n_f),
                [f32(SHORT, LANES)] * 4,
                scratch=[pltpu.VMEM((slots, LANES), F32)],
            )
            history.append(exchange_each(to_each, "inst"))
            nums.append(num)
            break
        msg, *kept = call(
            functools.partial(next_kernel, n_f, False),
            (tiles, row_pick, c, vec, num, *got),
            [VM] * (5 + n_f),
            [msg_shape] + [grid, grid] * (k < ITERS - 2),
        )
        history.append(exchange(msg, "inst", ORDERS[k + 2]))
        state = (*kept, vec, num)
        nums.append(num)
    block = f32(own_blocks, edge)
    *dense, pick = call(
        functools.partial(dense_kernel, n_i, short, ORDERS, slots, ITERS),
        (w, index, *(ref for group in history[:ITERS] for ref in group), *nums),
        [VM, SM] + [VM] * (n_i * ITERS + len(nums)),
        [block] * 4 + [picks((own_blocks, LANES if short else slots * inst), BF16)],
        scratch=[pltpu.VMEM((own_blocks, slots * inst), BF16)] * short,
    )
    step, res = call(
        functools.partial(last_kernel, n_i, short, ORDERS[ITERS], slots),
        (ww, nums[-1], *dense, pick, *history[-1]),
        [VM] * (7 + n_i),
        [block, block],
    )
    return step.reshape(1, own_len), res.reshape(1, own_len)


def solution(mesh):
    return jax.shard_map(
        body,
        mesh=mesh,
        in_specs=(
            P(("groups", "inst"), "feat", None, None, None),
            P(("groups", "inst"), "feat", None),
            P(("groups", "inst"), "feat", None),
            P(("groups", "inst"), "feat"),
            P(("groups", "inst"), None),
            P(("groups", "inst"), None),
            P(("groups", "feat"), None),
        ),
        out_specs=(P(("groups", "feat"), "inst"), P(("groups", "feat"), "inst")),
        check_vma=False,
    )
```

```python
import functools

import jax
import jax.numpy as jnp
from jax import lax
from jax.experimental import pallas as pl
from jax.experimental.pallas import tpu as pltpu
from jax.sharding import PartitionSpec as P

ITERS = 3
LAMBDA = 0.02
ORDERS = ((1, 2, 3),) * ITERS + ((3, 2, 1),)
FEAT_ORDER = (1, 2, 3)

F32, BF16, I32 = jnp.float32, jnp.bfloat16, jnp.int32
LANES, SUB = 128, 8
TAIL = 8
COLS_ROW = 3
CAP, CAP_RUN = 17, 512
SHORT, SHORT_PAD = 24, 32


VM = pl.BlockSpec(memory_space=pltpu.VMEM)
SM = pl.BlockSpec(memory_space=pltpu.SMEM)
ANY = pl.BlockSpec(memory_space=pl.ANY)
HBM = pl.BlockSpec(memory_space=pltpu.HBM)


def call(kernel, ins, in_specs, outs, out_specs=None, scratch=(), flops=1 << 21):
    return pl.pallas_call(
        kernel,
        in_specs=in_specs,
        out_shape=outs,
        out_specs=out_specs or [VM] * len(outs),
        scratch_shapes=list(scratch),
        compiler_params=pltpu.CompilerParams(vmem_limit_bytes=24 << 20),
        cost_estimate=pl.CostEstimate(flops=flops, bytes_accessed=1 << 20, transcendentals=0),
    )(*ins)


def f32(*shape):
    return jax.ShapeDtypeStruct(shape, F32)


def iota(shape, dim):
    return lax.broadcasted_iota(I32, shape, dim)


def total(x):
    return jnp.sum(x, axis=(0, 1), keepdims=True)


def split3(x):
    hi = x.astype(BF16).astype(F32)
    rest = x - hi
    mid = rest.astype(BF16).astype(F32)
    return hi, mid, (rest - mid).astype(BF16).astype(F32)


def exact_pick(pick, values):
    wide = values.shape[1]
    pieces = jnp.concatenate(split3(values), axis=1).astype(BF16)
    out = jnp.dot(pick, pieces, preferred_element_type=F32)
    return out[:, :wide] + out[:, wide : 2 * wide] + out[:, 2 * wide :]


def left_of(pieces):
    return jnp.concatenate([*pieces, jnp.zeros((SUB, LANES), F32)], axis=0).astype(BF16)


def fold3(acc, at=0):
    return acc[at : at + SUB] + acc[at + SUB : at + 2 * SUB] + acc[at + 2 * SUB : at + 3 * SUB]


def save_pieces(x, pieces):
    slots = x.shape[0]
    for p, piece in enumerate(split3(x)):
        pieces[p * slots : (p + 1) * slots, :] = piece


def masked_line(pieces, slots, slot, mask):
    return [
        mask * jnp.broadcast_to(pieces[p * slots + slot : p * slots + slot + 1, :], (SUB, LANES))
        for p in range(3)
    ]


def by_rows(turned, pieces, row_mask):
    slots = turned.shape[0]
    acc = jnp.zeros((4 * SUB, LANES), F32)
    for s in range(0, slots, 2):
        left = [
            left_of(masked_line(pieces, slots, t, row_mask[t * SUB : (t + 1) * SUB, :]))
            for t in (s, s + 1)
        ]
        right = jnp.concatenate([turned[s], turned[s + 1]], axis=0)
        acc = acc + jnp.dot(
            jnp.concatenate(left, axis=1), right, preferred_element_type=F32
        )
    return fold3(acc)


def by_cols(tiles, row_pick, vec, msg):
    slots = tiles.shape[0]
    pieces = jnp.concatenate(split3(vec), axis=1)
    pad = jnp.zeros((LANES - SUB, 3 * LANES), F32)
    stacked = jnp.concatenate([pieces, pad], axis=0).astype(BF16)
    lines = jnp.dot(row_pick[...], stacked, preferred_element_type=F32)
    sub = iota((SUB, LANES), 0)
    for g in range(0, slots, SUB):
        group = [lines[g : g + SUB, p * LANES : (p + 1) * LANES] for p in range(3)]
        acc = jnp.zeros((4 * SUB, LANES), F32)
        for s in range(0, SUB, 2):
            left = [left_of([jnp.where(sub == t, piece, 0.0) for piece in group]) for t in (s, s + 1)]
            right = jnp.concatenate([tiles[g + s], tiles[g + s + 1]], axis=0)
            acc = acc + jnp.dot(jnp.concatenate(left, axis=1), right, preferred_element_type=F32)
        msg[g : g + SUB, :] = fold3(acc)


def first_look_kernel(rows_hbm, cols_hbm, rows_out, slot_out, cols_out, rows_line, sems):
    pairs = ((rows_hbm, rows_line), (cols_hbm, cols_out))
    copies = [pltpu.make_async_copy(src, dst, sems.at[k]) for k, (src, dst) in enumerate(pairs)]
    for copy in copies:
        copy.start()
    slots = rows_line.shape[1]
    slot_out[...] = iota((slots, LANES), 0)
    copies[0].wait()
    line = rows_line[...].astype(F32)
    rows_out[...] = column_of(jnp.concatenate([line, line], axis=1), slots)
    copies[1].wait()


def start_kernel(cols, rows, tiles, w, part, row_mask, picked, pieces):
    slots = tiles.shape[0]
    sub = iota((SUB, LANES), 0).astype(F32)
    for t in range(slots):
        row_mask[t * SUB : (t + 1) * SUB, :] = (sub == rows[t : t + 1, :]).astype(F32)
    for t in range(slots):
        picked[t : t + 1, :] = w[pl.ds(cols[0, t], 1), :]
    save_pieces(picked[...], pieces)
    squares = jnp.zeros((SUB, LANES), F32)
    rows_w = w.shape[0]
    step_rows = min(rows_w, 256)
    for b in range(0, rows_w, step_rows):
        block = w[b : b + step_rows, :]
        squares = squares + jnp.sum((block * block).reshape(step_rows // SUB, SUB, LANES), axis=0)
    part[SUB : 2 * SUB, :] = squares
    acc = jnp.zeros((6 * SUB, 2 * LANES), F32)
    for s in range(0, slots, 4):
        a, b, c, d = (
            masked_line(pieces, slots, t, row_mask[t * SUB : (t + 1) * SUB, :]) for t in range(s, s + 4)
        )
        left = [jnp.concatenate([*x, *y], axis=0).astype(BF16) for x, y in ((a, c), (b, d))]
        right = [jnp.concatenate([tiles[t], tiles[t + 1]], axis=1) for t in (s, s + 2)]
        acc = acc + lax.dot_general(
            jnp.concatenate(left, axis=1),
            jnp.concatenate(right, axis=0),
            (((1,), (1,)), ((), ())),
            preferred_element_type=F32,
        )
    part[0:SUB, :] = fold3(acc[:, :LANES]) + fold3(acc[:, LANES:], 3 * SUB)


def turn_kernel(tiles, turned):
    for t in range(tiles.shape[0]):
        turned[t] = tiles[t].T


def ranks(line, column, parts):
    shift = CAP_RUN.bit_length() - 1
    run, run_column = line.astype(I32) >> shift, column.astype(I32) >> shift
    sub, lane = iota(column.shape, 0), iota(column.shape, 1)
    same = (run == run_column) & (sub < lane)
    if parts == 2:
        same = same & ((sub < LANES // 2) == (lane < LANES // 2))
    return run, jnp.sum(same.astype(F32), axis=0, keepdims=True).astype(I32)


def column_of(line, rows):
    wide = jnp.broadcast_to(line, (rows, LANES))
    own = jnp.where(iota((rows, LANES), 0) == iota((rows, LANES), 1), wide, 0.0)
    return jnp.broadcast_to(jnp.sum(own, axis=1, keepdims=True), (rows, LANES))


def prep_kernel(ids, rows, cols_line, index, mask_out, pick_out, cols_out, own_out, *send_out):
    n = ids.shape[1]
    left = ((ids[...] >> 7) == iota((SUB, n), 0)).astype(F32).astype(BF16)
    right = ((ids[...] & (LANES - 1)) == iota((LANES, n), 0)).astype(F32).astype(BF16)
    hits = lax.dot_general(left, right, (((1,), (1,)), ((), ())), preferred_element_type=F32)
    mask_out[...] = jnp.minimum(hits, 1.0)
    slots = rows.shape[0]
    sub, lane = iota((slots, LANES), 0), iota((slots, LANES), 1)
    line = cols_line[...].astype(F32)
    line = jnp.concatenate([line, line], axis=1)
    own = jnp.where(rows[...] >= 0.0, column_of(line, slots), -1.0)
    line = jnp.sum(jnp.where(sub == (lane & (slots - 1)), own, 0.0), axis=0, keepdims=True)
    cols_out[...] = jnp.broadcast_to(line, (SUB, LANES))
    own_out[...] = own
    pick_out[...] = (rows[...] == lane.astype(F32)).astype(F32).astype(BF16)
    for out in send_out:
        run, rank = ranks(line, own, 1)
        row = iota((SHORT, LANES), 0)
        for j, k in enumerate((0, 3, 2, 1)):
            sent = (row == rank) & (run == (index[0] ^ k))
            out[j * SHORT : (j + 1) * SHORT, :] = sent.astype(F32)[:, :slots].astype(BF16)


def feat_sum(refs, first=0):
    out = None
    for ref, height in refs:
        for at in range(0, ref.shape[0], height):
            piece = ref[at + first : at + first + SUB, :]
            out = piece if out is None else out + piece
    return out


def parts_of(refs, slots):
    height = slots + TAIL
    return [(ref, at) for ref in refs for at in range(0, ref.shape[0], height)]


def summed(refs, slots, row):
    line = None
    for ref, at in parts_of(refs, slots):
        piece = ref[at + slots + row : at + slots + row + 1, :]
        line = piece if line is None else line + piece
    return total(line)


def slot_cols(refs, slots):
    parts = parts_of(refs, slots)
    low = iota((1, LANES), 1) < slots
    lines = []
    for a, b in zip(parts[::2], parts[1::2], strict=True):
        first, second = (r[at + slots + COLS_ROW : at + slots + COLS_ROW + 1, :] for r, at in (a, b))
        lines.append(jnp.where(low, first, second))
    return jnp.concatenate(lines, axis=1)


def slot_values(refs, slots):
    return jnp.concatenate([ref[at : at + slots, :] for ref, at in parts_of(refs, slots)], axis=0)


def write_tail(msg, slots, lines):
    pad = jnp.zeros((TAIL - len(lines), LANES), F32)
    msg[slots : slots + TAIL, :] = jnp.concatenate([*lines, pad], axis=0)


def line_of(x):
    return jnp.sum(x, axis=0, keepdims=True)


def margin_kernel(n_f, scale, tiles, row_pick, mask, labels, cols, *refs):
    got, (msg, m_out, c_out, e_out, ww_out) = refs[:n_f], refs[n_f:]
    slots = tiles.shape[0]
    pieces = [(ref, 2 * SUB) for ref in got]
    m = feat_sum(pieces)
    chance = jax.nn.sigmoid(m)
    e = chance - labels[...].astype(F32)
    by_cols(tiles, row_pick, e, msg)
    zero = jnp.zeros((1, LANES), F32)
    write_tail(msg, slots, [zero, zero, zero, cols[0:1, :]])
    ww_out[...] = feat_sum(pieces, SUB)
    c_out[...] = scale * mask[...] * chance * (1.0 - chance)
    m_out[...] = m
    e_out[...] = e


def match_kernel(n_i, order, own, *refs):
    got, (match,) = sorted_as(order, refs[:n_i]), refs[n_i:]
    slots = own.shape[0]
    line = slot_cols(got, slots)
    for at in range(0, line.shape[1], LANES):
        same = own[...] == line[:, at : at + LANES]
        match[:, at : at + LANES] = same.astype(F32).astype(BF16)


def forward_kernel(n_i, order, turned, row_mask, match, *refs):
    got, (out, pieces) = sorted_as(order, refs[:n_i]), refs[n_i:]
    slots = turned.shape[0]
    save_pieces(exact_pick(match[...], slot_values(got, slots)), pieces)
    out[...] = by_rows(turned, pieces, row_mask)


def first_kernel(n_f, tiles, row_pick, m, c, e, *refs):
    got, (msg, v_out) = refs[:n_f], refs[n_f:]
    slots = tiles.shape[0]
    v = -(LAMBDA * m[...] + feat_sum([(ref, SUB) for ref in got]))
    v_out[...] = v
    u = c[...] * v
    by_cols(tiles, row_pick, u, msg)
    s = -e[...]
    write_tail(msg, slots, [line_of(-LAMBDA * m[...] * s + s * v), line_of(u * v)])


NUMBERS = ("rr", "dd", "cur", "a_r", "a_d", "alpha", "beta")


def numbers_of(num):
    return {name: num[k : k + 1, 0:1] for k, name in enumerate(NUMBERS)}


def save_numbers(num, values):
    lines = [jnp.broadcast_to(values[name], (1, LANES)) for name in NUMBERS]
    num[...] = jnp.concatenate([*lines, jnp.zeros((1, LANES), F32)], axis=0)


def advance(msgs, slots, ww, old, shift=0):
    rr_new, cur_r = summed(msgs, slots, shift), summed(msgs, slots, shift + 1)
    if old is None:
        a_r = a_d = jnp.full((1, 1), -LAMBDA, F32)
        rr = a_r * a_r * total(ww[...]) + rr_new
        dd, cur, beta = rr, cur_r, jnp.zeros((1, 1), F32)
    else:
        cross = summed(msgs, slots, shift + 2)
        rr = old["a_r"] * old["a_r"] * total(ww[...]) + rr_new
        beta = rr / old["rr"]
        a_d = old["a_r"] + beta * old["a_d"]
        dd = rr + beta * beta * old["dd"]
        cur = cur_r + 2.0 * beta * cross + beta * beta * old["cur"]
        a_r = old["a_r"]
    alpha = rr / (cur + LAMBDA * dd)
    a_r = a_r - alpha * (LAMBDA * a_d)
    return {"rr": rr, "dd": dd, "cur": cur, "a_r": a_r, "a_d": a_d, "alpha": alpha, "beta": beta}


def at(ref, k):
    return ref[k * SUB : (k + 1) * SUB, :]


def save_all(ref, values):
    for k, value in enumerate(values):
        ref[k * SUB : (k + 1) * SUB, :] = value


def numbers_kernel(n_i, slots, first, m, c, ww, *refs):
    msgs = refs[:n_i]
    vec_out, num_out = refs[-2:]
    if first:
        e, v = refs[n_i:-2]
        new = advance(msgs, slots, ww, None)
        v_r, s_r = v[...], -e[...]
        v_d, s_d, gram = v_r, s_r, jnp.zeros((SUB, LANES), F32)
    else:
        v, gram_d, vec, num = refs[n_i:-2]
        new = advance(msgs, slots, ww, numbers_of(num))
        v_r, s_r = v[...], at(vec, 2)
        v_d = v_r + new["beta"] * at(vec, 1)
        s_d = s_r + new["beta"] * at(vec, 3)
        gram = new["beta"] * gram_d[...]
    v_r = v_r - new["alpha"] * (gram + LAMBDA * v_d)
    s_r = s_r - new["alpha"] * (c[...] * v_d + LAMBDA * s_d)
    save_all(vec_out, (v_r, v_d, s_r, s_d, new["a_r"] * m[...] * s_r, gram))
    save_numbers(num_out, new)


def next_kernel(n_f, short, tiles, row_pick, c, vec, num, *refs):
    got, (msg, *kept) = refs[:n_f], refs[n_f:]
    slots = tiles.shape[0]
    if short:
        send, *outs, msg = refs[n_f:]
    gram = feat_sum([(ref, SUB) for ref in got])
    v = at(vec, 0) - numbers_of(num)["alpha"] * gram
    u = c[...] * v
    by_cols(tiles, row_pick, u, msg)
    lines = [line_of(at(vec, 4) + at(vec, 2) * v), line_of(u * v), line_of(u * at(vec, 1))]
    if short:
        chosen = exact_pick(send[...], msg[...])
        pad = [jnp.zeros((n, LANES), F32) for n in (CAP, SHORT - CAP - len(lines))]
        tail = jnp.concatenate([pad[0], *lines, pad[1]], axis=0)
        for j, out in enumerate(outs):
            slots_rows = chosen[j * SHORT : (j + 1) * SHORT]
            out[...] = jnp.where(iota((SHORT, LANES), 0) < CAP, slots_rows, tail)
        return
    write_tail(msg, slots, lines)
    for out, value in zip(kept, (v, gram + at(vec, 5))):
        out[...] = value


def dense_kernel(n_i, short, orders, slots, iters, w, index, *refs):
    msgs = [sorted_as(orders[k], refs[k * n_i : (k + 1) * n_i]) for k in range(iters)]
    nums = [numbers_of(num) for num in refs[iters * n_i : iters * n_i + iters - 1]]
    res_out, dir_out, step_out, curved_out, pick_out = refs[iters * n_i + iters - 1 :][:5]
    if short:
        short_out, pick_out = refs[-2:]
    own_blocks = res_out.shape[0]
    line = slot_cols(msgs[0], slots)
    offset = index[0] * own_blocks
    own = (iota((own_blocks, LANES), 0) + offset).astype(F32)
    for a in range(0, line.shape[1], LANES):
        pick_out[:, a : a + LANES] = (own == line[:, a : a + LANES]).astype(F32).astype(BF16)
    mine = w[pl.ds(pl.multiple_of(offset, own_blocks), own_blocks), :]
    res = -LAMBDA * mine - exact_pick(pick_out[...], slot_values(msgs[0], slots))
    step = jnp.zeros_like(res)
    for k in range(iters - 1):
        image = exact_pick(pick_out[...], slot_values(msgs[k + 1], slots))
        if k == 0:
            direction, curved = res, image
        else:
            direction = res + nums[k]["beta"] * direction
            curved = image + nums[k]["beta"] * curved
        step = step + nums[k]["alpha"] * direction
        res = res - nums[k]["alpha"] * (curved + LAMBDA * direction)
    if short:
        blocks = []
        for a in range(0, line.shape[1], LANES):
            pair = line[:, a : a + LANES]
            run, rank = ranks(pair, column_of(pair, LANES), 2)
            first = a // slots * SHORT_PAD
            second = iota((1, LANES), 1) >= slots
            want = rank + jnp.where(second, first + SHORT_PAD, first)
            row = iota((LANES, LANES), 0)
            blocks.append(((row == want) & (run == index[0])).astype(F32).astype(BF16))
        short_out[...] = lax.dot_general(
            pick_out[...],
            jnp.concatenate(blocks, axis=1),
            (((1,), (1,)), ((), ())),
            preferred_element_type=F32,
        ).astype(BF16)
    res_out[...] = res
    dir_out[...] = direction
    step_out[...] = step
    curved_out[...] = curved


def last_kernel(n_i, short, order, slots, ww, num, res, direction, step, curved, pick, *refs):
    msgs, (step_out, res_out) = sorted_as(order, refs[:n_i]), refs[n_i:]
    if short:
        pad = jnp.zeros((SHORT_PAD - SHORT, LANES), F32)
        values = jnp.concatenate([piece for msg in msgs for piece in (msg[...], pad)], axis=0)
        new = advance(msgs, SHORT - TAIL, ww, numbers_of(num), CAP - (SHORT - TAIL))
    else:
        values = slot_values(msgs, slots)
        new = advance(msgs, slots, ww, numbers_of(num))
    image = exact_pick(pick[...], values)
    last = res[...] + new["beta"] * direction[...]
    step_out[...] = step[...] + new["alpha"] * last
    image = image + new["beta"] * curved[...] + LAMBDA * last
    res_out[...] = res[...] - new["alpha"] * image


def exchange(x, axis, order=FEAT_ORDER):
    size = lax.axis_size(axis)
    if size != 4:
        return [lax.all_gather(x, axis, axis=0, tiled=True)]
    return [x] + [lax.ppermute(x, axis, [(i, i ^ k) for i in range(size)]) for k in order]


def exchange_each(arrays, axis):
    keys = (3, 2, 1)
    return [arrays[0]] + [
        lax.ppermute(x, axis, [(i, i ^ k) for i in range(4)])
        for k, x in zip(keys, arrays[1:], strict=True)
    ]


def sorted_as(order, refs):
    if len(refs) == 1:
        return refs
    return [refs[0]] + [refs[1 + order.index(k)] for k in (3, 2, 1)]


def in_hbm(x):
    return pltpu.with_memory_space_constraint(x, pltpu.HBM)


def body(tiles, tile_rows, tile_cols, tile_count, sample_ids, labels, weights):
    slots, edge = tiles.shape[2], tiles.shape[3]
    row_total, feat_len = labels.shape[1], weights.shape[1]
    row_blocks, col_blocks = row_total // edge, feat_len // edge
    assert row_blocks == SUB and edge == LANES and 2 * slots == LANES
    inst = lax.axis_size("inst")
    own_len = feat_len // inst
    own_blocks = own_len // edge
    tiles = tiles.reshape(slots, edge, edge)
    scale = float(row_total) / float(sample_ids.shape[1])
    index = lax.axis_index("inst").astype(I32).reshape(1)
    grid, msg_shape = f32(SUB, LANES), f32(slots + TAIL, LANES)
    short = inst == 4 and own_blocks == CAP_RUN
    tile_shape = jax.ShapeDtypeStruct((slots, edge, edge), BF16)
    picks = jax.ShapeDtypeStruct

    w = weights.reshape(col_blocks, edge)
    rows, slot, cols = call(
        first_look_kernel,
        (in_hbm(tile_rows.reshape(1, slots)), in_hbm(tile_cols.reshape(1, slots))),
        [HBM] * 2,
        [f32(slots, LANES), picks((slots, LANES), I32), pltpu.SMEM((1, slots), I32)],
        [VM, VM, SM],
        scratch=[pltpu.VMEM((1, slots), I32), pltpu.SemaphoreType.DMA((2,))],
        flops=1 << 30,
    )
    rows = jnp.where(slot < tile_count, rows, -1.0)
    part, row_mask = call(
        start_kernel,
        (cols, rows, tiles, w),
        [SM, VM, VM, VM],
        [f32(2 * SUB, LANES), f32(slots * SUB, LANES)],
        scratch=[pltpu.VMEM((slots, LANES), F32), pltpu.VMEM((3 * slots, LANES), F32)],
    )
    mask, row_pick, cols_line, own, *send = call(
        prep_kernel,
        (sample_ids, rows, tile_cols.reshape(1, slots), index),
        [VM] * 3 + [SM],
        [grid, picks((slots, LANES), BF16), grid, f32(slots, LANES)]
        + [picks((4 * SHORT, slots), BF16)] * short,
    )
    (turned,) = call(turn_kernel, (tiles,), [VM], [tile_shape])
    got = exchange(part, "feat")
    n_f = len(got)
    msg, m, c, e, ww = call(
        functools.partial(margin_kernel, n_f, scale),
        (tiles, row_pick, mask, labels.reshape(SUB, LANES), cols_line, *got),
        [VM] * (5 + n_f),
        [msg_shape, grid, grid, grid, grid],
    )
    msgs = exchange(msg, "inst", ORDERS[0])
    n_i = len(msgs)
    (match,) = call(
        functools.partial(match_kernel, n_i, ORDERS[0]),
        (own, *msgs),
        [VM] * (1 + n_i),
        [picks((slots, slots * inst), BF16)],
    )

    def forward(msgs, order):
        (out,) = call(
            functools.partial(forward_kernel, n_i, order),
            (turned, row_mask, match, *msgs),
            [VM] * (3 + n_i),
            [grid],
            scratch=[pltpu.VMEM((3 * slots, LANES), F32)],
        )
        return exchange(out, "feat")

    got = forward(msgs, ORDERS[0])
    msg, v = call(
        functools.partial(first_kernel, n_f),
        (tiles, row_pick, m, c, e, *got),
        [VM] * (5 + n_f),
        [msg_shape, grid],
    )
    history = [msgs, exchange(msg, "inst", ORDERS[1])]
    state, nums = (e, v), []
    for k in range(ITERS - 1):
        got = forward(history[-1], ORDERS[k + 1])
        vec, num = call(
            functools.partial(numbers_kernel, n_i, slots, k == 0),
            (m, c, ww, *history[-1], *state),
            [VM] * (3 + n_i + len(state)),
            [f32(6 * SUB, LANES), grid],
        )
        if short and k == ITERS - 2:
            to_each = call(
                functools.partial(next_kernel, n_f, True),
                (tiles, row_pick, c, vec, num, *got, *send),
                [VM] * (6 + n_f),
                [f32(SHORT, LANES)] * 4,
                scratch=[pltpu.VMEM((slots, LANES), F32)],
            )
            history.append(exchange_each(to_each, "inst"))
            nums.append(num)
            break
        msg, *kept = call(
            functools.partial(next_kernel, n_f, False),
            (tiles, row_pick, c, vec, num, *got),
            [VM] * (5 + n_f),
            [msg_shape] + [grid, grid] * (k < ITERS - 2),
        )
        history.append(exchange(msg, "inst", ORDERS[k + 2]))
        state = (*kept, vec, num)
        nums.append(num)
    block = f32(own_blocks, edge)
    *dense, pick = call(
        functools.partial(dense_kernel, n_i, short, ORDERS, slots, ITERS),
        (w, index, *(ref for group in history[:ITERS] for ref in group), *nums),
        [VM, SM] + [VM] * (n_i * ITERS + len(nums)),
        [block] * 4 + [picks((own_blocks, LANES if short else slots * inst), BF16)],
        scratch=[pltpu.VMEM((own_blocks, slots * inst), BF16)] * short,
    )
    step, res = call(
        functools.partial(last_kernel, n_i, short, ORDERS[ITERS], slots),
        (ww, nums[-1], *dense, pick, *history[-1]),
        [VM] * (7 + n_i),
        [block, block],
    )
    return step.reshape(1, own_len), res.reshape(1, own_len)


def solution(mesh):
    return jax.shard_map(
        body,
        mesh=mesh,
        in_specs=(
            P(("groups", "inst"), "feat", None, None, None),
            P(("groups", "inst"), "feat", None),
            P(("groups", "inst"), "feat", None),
            P(("groups", "inst"), "feat"),
            P(("groups", "inst"), None),
            P(("groups", "inst"), None),
            P(("groups", "feat"), None),
        ),
        out_specs=(P(("groups", "feat"), "inst"), P(("groups", "feat"), "inst")),
        check_vma=False,
    )
```

```python
import functools

import jax
import jax.numpy as jnp
from jax import lax
from jax.experimental import pallas as pl
from jax.experimental.pallas import tpu as pltpu
from jax.sharding import PartitionSpec as P

ITERS = 3
LAMBDA = 0.02
ORDERS = ((1, 2, 3),) * ITERS + ((3, 2, 1),)
FEAT_ORDER = (1, 2, 3)

F32, BF16, I32 = jnp.float32, jnp.bfloat16, jnp.int32
LANES, SUB = 128, 8
TAIL = 8
COLS_ROW = 3
CAP, CAP_RUN = 17, 512
SHORT, SHORT_PAD = 24, 32


VM = pl.BlockSpec(memory_space=pltpu.VMEM)
SM = pl.BlockSpec(memory_space=pltpu.SMEM)
ANY = pl.BlockSpec(memory_space=pl.ANY)
HBM = pl.BlockSpec(memory_space=pltpu.HBM)


def call(kernel, ins, in_specs, outs, out_specs=None, scratch=(), flops=1 << 21):
    return pl.pallas_call(
        kernel,
        in_specs=in_specs,
        out_shape=outs,
        out_specs=out_specs or [VM] * len(outs),
        scratch_shapes=list(scratch),
        compiler_params=pltpu.CompilerParams(vmem_limit_bytes=24 << 20),
        cost_estimate=pl.CostEstimate(flops=flops, bytes_accessed=1 << 20, transcendentals=0),
    )(*ins)


def f32(*shape):
    return jax.ShapeDtypeStruct(shape, F32)


def iota(shape, dim):
    return lax.broadcasted_iota(I32, shape, dim)


def total(x):
    return jnp.sum(x, axis=(0, 1), keepdims=True)


def split3(x):
    hi = x.astype(BF16).astype(F32)
    rest = x - hi
    mid = rest.astype(BF16).astype(F32)
    return hi, mid, (rest - mid).astype(BF16).astype(F32)


def exact_pick(pick, values):
    wide = values.shape[1]
    pieces = jnp.concatenate(split3(values), axis=1).astype(BF16)
    out = jnp.dot(pick, pieces, preferred_element_type=F32)
    return out[:, :wide] + out[:, wide : 2 * wide] + out[:, 2 * wide :]


def left_of(pieces):
    return jnp.concatenate([*pieces, jnp.zeros((SUB, LANES), F32)], axis=0).astype(BF16)


def fold3(acc, at=0):
    return acc[at : at + SUB] + acc[at + SUB : at + 2 * SUB] + acc[at + 2 * SUB : at + 3 * SUB]


def save_pieces(x, pieces):
    slots = x.shape[0]
    for p, piece in enumerate(split3(x)):
        pieces[p * slots : (p + 1) * slots, :] = piece


def masked_line(pieces, slots, slot, mask):
    return [
        mask * jnp.broadcast_to(pieces[p * slots + slot : p * slots + slot + 1, :], (SUB, LANES))
        for p in range(3)
    ]


def by_rows(turned, pieces, row_mask):
    slots = turned.shape[0]
    acc = jnp.zeros((4 * SUB, LANES), F32)
    for s in range(0, slots, 2):
        left = [
            left_of(masked_line(pieces, slots, t, row_mask[t * SUB : (t + 1) * SUB, :]))
            for t in (s, s + 1)
        ]
        right = jnp.concatenate([turned[s], turned[s + 1]], axis=0)
        acc = acc + jnp.dot(
            jnp.concatenate(left, axis=1), right, preferred_element_type=F32
        )
    return fold3(acc)


def by_cols(tiles, rows, vec, msg):
    slots = tiles.shape[0]
    blocks = [jnp.broadcast_to(vec[r : r + 1, :], (SUB, LANES)) for r in range(SUB)]
    sub = iota((SUB, LANES), 0)
    for g in range(0, slots, SUB):
        row = rows[g : g + SUB, :]
        lines = jnp.zeros((SUB, LANES), F32)
        for r in range(SUB):
            lines = jnp.where(row == float(r), blocks[r], lines)
        group = split3(lines)
        acc = jnp.zeros((4 * SUB, LANES), F32)
        for s in range(0, SUB, 2):
            left = [left_of([jnp.where(sub == t, piece, 0.0) for piece in group]) for t in (s, s + 1)]
            right = jnp.concatenate([tiles[g + s], tiles[g + s + 1]], axis=0)
            acc = acc + jnp.dot(jnp.concatenate(left, axis=1), right, preferred_element_type=F32)
        msg[g : g + SUB, :] = fold3(acc)


def first_look_kernel(rows_hbm, cols_hbm, rows_out, slot_out, cols_out, rows_line, sems):
    pairs = ((rows_hbm, rows_line), (cols_hbm, cols_out))
    copies = [pltpu.make_async_copy(src, dst, sems.at[k]) for k, (src, dst) in enumerate(pairs)]
    for copy in copies:
        copy.start()
    slots = rows_line.shape[1]
    slot_out[...] = iota((slots, LANES), 0)
    copies[0].wait()
    line = rows_line[...].astype(F32)
    rows_out[...] = column_of(jnp.concatenate([line, line], axis=1), slots)
    copies[1].wait()


def start_kernel(cols, rows, tiles, w, part, row_mask, picked, pieces):
    slots = tiles.shape[0]
    sub = iota((SUB, LANES), 0).astype(F32)
    for t in range(slots):
        row_mask[t * SUB : (t + 1) * SUB, :] = (sub == rows[t : t + 1, :]).astype(F32)
    for t in range(slots):
        picked[t : t + 1, :] = w[pl.ds(cols[0, t], 1), :]
    save_pieces(picked[...], pieces)
    squares = jnp.zeros((SUB, LANES), F32)
    rows_w = w.shape[0]
    step_rows = min(rows_w, 256)
    for b in range(0, rows_w, step_rows):
        block = w[b : b + step_rows, :]
        squares = squares + jnp.sum((block * block).reshape(step_rows // SUB, SUB, LANES), axis=0)
    part[SUB : 2 * SUB, :] = squares
    acc = jnp.zeros((6 * SUB, 2 * LANES), F32)
    for s in range(0, slots, 4):
        a, b, c, d = (
            masked_line(pieces, slots, t, row_mask[t * SUB : (t + 1) * SUB, :]) for t in range(s, s + 4)
        )
        left = [jnp.concatenate([*x, *y], axis=0).astype(BF16) for x, y in ((a, c), (b, d))]
        right = [jnp.concatenate([tiles[t], tiles[t + 1]], axis=1) for t in (s, s + 2)]
        acc = acc + lax.dot_general(
            jnp.concatenate(left, axis=1),
            jnp.concatenate(right, axis=0),
            (((1,), (1,)), ((), ())),
            preferred_element_type=F32,
        )
    part[0:SUB, :] = fold3(acc[:, :LANES]) + fold3(acc[:, LANES:], 3 * SUB)


def turn_kernel(tiles, turned):
    for t in range(tiles.shape[0]):
        turned[t] = tiles[t].T


def ranks(line, column, parts):
    shift = CAP_RUN.bit_length() - 1
    run, run_column = line.astype(I32) >> shift, column.astype(I32) >> shift
    sub, lane = iota(column.shape, 0), iota(column.shape, 1)
    same = (run == run_column) & (sub < lane)
    if parts == 2:
        same = same & ((sub < LANES // 2) == (lane < LANES // 2))
    return run, jnp.sum(same.astype(F32), axis=0, keepdims=True).astype(I32)


def column_of(line, rows):
    wide = jnp.broadcast_to(line, (rows, LANES))
    own = jnp.where(iota((rows, LANES), 0) == iota((rows, LANES), 1), wide, 0.0)
    return jnp.broadcast_to(jnp.sum(own, axis=1, keepdims=True), (rows, LANES))


def prep_kernel(ids, rows, cols_line, index, mask_out, cols_out, own_out, *send_out):
    n = ids.shape[1]
    left = ((ids[...] >> 7) == iota((SUB, n), 0)).astype(F32).astype(BF16)
    right = ((ids[...] & (LANES - 1)) == iota((LANES, n), 0)).astype(F32).astype(BF16)
    hits = lax.dot_general(left, right, (((1,), (1,)), ((), ())), preferred_element_type=F32)
    mask_out[...] = jnp.minimum(hits, 1.0)
    slots = rows.shape[0]
    sub, lane = iota((slots, LANES), 0), iota((slots, LANES), 1)
    line = cols_line[...].astype(F32)
    line = jnp.concatenate([line, line], axis=1)
    own = jnp.where(rows[...] >= 0.0, column_of(line, slots), -1.0)
    line = jnp.sum(jnp.where(sub == (lane & (slots - 1)), own, 0.0), axis=0, keepdims=True)
    cols_out[...] = jnp.broadcast_to(line, (SUB, LANES))
    own_out[...] = own
    for out in send_out:
        run, rank = ranks(line, own, 1)
        row = iota((SHORT, LANES), 0)
        for j, k in enumerate((0, 3, 2, 1)):
            sent = (row == rank) & (run == (index[0] ^ k))
            out[j * SHORT : (j + 1) * SHORT, :] = sent.astype(F32)[:, :slots].astype(BF16)


def feat_sum(refs, first=0):
    out = None
    for ref, height in refs:
        for at in range(0, ref.shape[0], height):
            piece = ref[at + first : at + first + SUB, :]
            out = piece if out is None else out + piece
    return out


def parts_of(refs, slots):
    height = slots + TAIL
    return [(ref, at) for ref in refs for at in range(0, ref.shape[0], height)]


def summed(refs, slots, row):
    line = None
    for ref, at in parts_of(refs, slots):
        piece = ref[at + slots + row : at + slots + row + 1, :]
        line = piece if line is None else line + piece
    return total(line)


def slot_cols(refs, slots):
    parts = parts_of(refs, slots)
    low = iota((1, LANES), 1) < slots
    lines = []
    for a, b in zip(parts[::2], parts[1::2], strict=True):
        first, second = (r[at + slots + COLS_ROW : at + slots + COLS_ROW + 1, :] for r, at in (a, b))
        lines.append(jnp.where(low, first, second))
    return jnp.concatenate(lines, axis=1)


def slot_values(refs, slots):
    return jnp.concatenate([ref[at : at + slots, :] for ref, at in parts_of(refs, slots)], axis=0)


def write_tail(msg, slots, lines):
    pad = jnp.zeros((TAIL - len(lines), LANES), F32)
    msg[slots : slots + TAIL, :] = jnp.concatenate([*lines, pad], axis=0)


def line_of(x):
    return jnp.sum(x, axis=0, keepdims=True)


def margin_kernel(n_f, scale, tiles, rows, mask, labels, cols, *refs):
    got, (msg, m_out, c_out, e_out, ww_out) = refs[:n_f], refs[n_f:]
    slots = tiles.shape[0]
    pieces = [(ref, 2 * SUB) for ref in got]
    m = feat_sum(pieces)
    chance = jax.nn.sigmoid(m)
    e = chance - labels[...].astype(F32)
    by_cols(tiles, rows, e, msg)
    zero = jnp.zeros((1, LANES), F32)
    write_tail(msg, slots, [zero, zero, zero, cols[0:1, :]])
    ww_out[...] = feat_sum(pieces, SUB)
    c_out[...] = scale * mask[...] * chance * (1.0 - chance)
    m_out[...] = m
    e_out[...] = e


def match_kernel(n_i, order, own, *refs):
    got, (match,) = sorted_as(order, refs[:n_i]), refs[n_i:]
    slots = own.shape[0]
    line = slot_cols(got, slots)
    for at in range(0, line.shape[1], LANES):
        same = own[...] == line[:, at : at + LANES]
        match[:, at : at + LANES] = same.astype(F32).astype(BF16)


def forward_kernel(n_i, order, turned, row_mask, match, *refs):
    got, (out, pieces) = sorted_as(order, refs[:n_i]), refs[n_i:]
    slots = turned.shape[0]
    save_pieces(exact_pick(match[...], slot_values(got, slots)), pieces)
    out[...] = by_rows(turned, pieces, row_mask)


def first_kernel(n_f, tiles, rows, m, c, e, *refs):
    got, (msg, v_out) = refs[:n_f], refs[n_f:]
    slots = tiles.shape[0]
    v = -(LAMBDA * m[...] + feat_sum([(ref, SUB) for ref in got]))
    v_out[...] = v
    u = c[...] * v
    by_cols(tiles, rows, u, msg)
    s = -e[...]
    write_tail(msg, slots, [line_of(-LAMBDA * m[...] * s + s * v), line_of(u * v)])


NUMBERS = ("rr", "dd", "cur", "a_r", "a_d", "alpha", "beta")


def numbers_of(num):
    return {name: num[k : k + 1, 0:1] for k, name in enumerate(NUMBERS)}


def save_numbers(num, values):
    lines = [jnp.broadcast_to(values[name], (1, LANES)) for name in NUMBERS]
    num[...] = jnp.concatenate([*lines, jnp.zeros((1, LANES), F32)], axis=0)


def advance(msgs, slots, ww, old, shift=0):
    rr_new, cur_r = summed(msgs, slots, shift), summed(msgs, slots, shift + 1)
    if old is None:
        a_r = a_d = jnp.full((1, 1), -LAMBDA, F32)
        rr = a_r * a_r * total(ww[...]) + rr_new
        dd, cur, beta = rr, cur_r, jnp.zeros((1, 1), F32)
    else:
        cross = summed(msgs, slots, shift + 2)
        rr = old["a_r"] * old["a_r"] * total(ww[...]) + rr_new
        beta = rr / old["rr"]
        a_d = old["a_r"] + beta * old["a_d"]
        dd = rr + beta * beta * old["dd"]
        cur = cur_r + 2.0 * beta * cross + beta * beta * old["cur"]
        a_r = old["a_r"]
    alpha = rr / (cur + LAMBDA * dd)
    a_r = a_r - alpha * (LAMBDA * a_d)
    return {"rr": rr, "dd": dd, "cur": cur, "a_r": a_r, "a_d": a_d, "alpha": alpha, "beta": beta}


def at(ref, k):
    return ref[k * SUB : (k + 1) * SUB, :]


def save_all(ref, values):
    for k, value in enumerate(values):
        ref[k * SUB : (k + 1) * SUB, :] = value


def numbers_kernel(n_i, slots, first, m, c, ww, *refs):
    msgs = refs[:n_i]
    vec_out, num_out = refs[-2:]
    if first:
        e, v = refs[n_i:-2]
        new = advance(msgs, slots, ww, None)
        v_r, s_r = v[...], -e[...]
        v_d, s_d, gram = v_r, s_r, jnp.zeros((SUB, LANES), F32)
    else:
        v, gram_d, vec, num = refs[n_i:-2]
        new = advance(msgs, slots, ww, numbers_of(num))
        v_r, s_r = v[...], at(vec, 2)
        v_d = v_r + new["beta"] * at(vec, 1)
        s_d = s_r + new["beta"] * at(vec, 3)
        gram = new["beta"] * gram_d[...]
    v_r = v_r - new["alpha"] * (gram + LAMBDA * v_d)
    s_r = s_r - new["alpha"] * (c[...] * v_d + LAMBDA * s_d)
    save_all(vec_out, (v_r, v_d, s_r, s_d, new["a_r"] * m[...] * s_r, gram))
    save_numbers(num_out, new)


def next_kernel(n_f, short, tiles, rows, c, vec, num, *refs):
    got, (msg, *kept) = refs[:n_f], refs[n_f:]
    slots = tiles.shape[0]
    if short:
        send, *outs, msg = refs[n_f:]
    gram = feat_sum([(ref, SUB) for ref in got])
    v = at(vec, 0) - numbers_of(num)["alpha"] * gram
    u = c[...] * v
    by_cols(tiles, rows, u, msg)
    lines = [line_of(at(vec, 4) + at(vec, 2) * v), line_of(u * v), line_of(u * at(vec, 1))]
    if short:
        chosen = exact_pick(send[...], msg[...])
        pad = [jnp.zeros((n, LANES), F32) for n in (CAP, SHORT - CAP - len(lines))]
        tail = jnp.concatenate([pad[0], *lines, pad[1]], axis=0)
        for j, out in enumerate(outs):
            slots_rows = chosen[j * SHORT : (j + 1) * SHORT]
            out[...] = jnp.where(iota((SHORT, LANES), 0) < CAP, slots_rows, tail)
        return
    write_tail(msg, slots, lines)
    for out, value in zip(kept, (v, gram + at(vec, 5))):
        out[...] = value


def dense_kernel(n_i, short, orders, slots, iters, w, index, *refs):
    msgs = [sorted_as(orders[k], refs[k * n_i : (k + 1) * n_i]) for k in range(iters)]
    nums = [numbers_of(num) for num in refs[iters * n_i : iters * n_i + iters - 1]]
    res_out, dir_out, step_out, curved_out, pick_out = refs[iters * n_i + iters - 1 :][:5]
    if short:
        short_out, pick_out = refs[-2:]
    own_blocks = res_out.shape[0]
    line = slot_cols(msgs[0], slots)
    offset = index[0] * own_blocks
    own = (iota((own_blocks, LANES), 0) + offset).astype(F32)
    for a in range(0, line.shape[1], LANES):
        pick_out[:, a : a + LANES] = (own == line[:, a : a + LANES]).astype(F32).astype(BF16)
    mine = w[pl.ds(pl.multiple_of(offset, own_blocks), own_blocks), :]
    res = -LAMBDA * mine - exact_pick(pick_out[...], slot_values(msgs[0], slots))
    step = jnp.zeros_like(res)
    for k in range(iters - 1):
        image = exact_pick(pick_out[...], slot_values(msgs[k + 1], slots))
        if k == 0:
            direction, curved = res, image
        else:
            direction = res + nums[k]["beta"] * direction
            curved = image + nums[k]["beta"] * curved
        step = step + nums[k]["alpha"] * direction
        res = res - nums[k]["alpha"] * (curved + LAMBDA * direction)
    if short:
        blocks = []
        for a in range(0, line.shape[1], LANES):
            pair = line[:, a : a + LANES]
            run, rank = ranks(pair, column_of(pair, LANES), 2)
            first = a // slots * SHORT_PAD
            second = iota((1, LANES), 1) >= slots
            want = rank + jnp.where(second, first + SHORT_PAD, first)
            row = iota((LANES, LANES), 0)
            blocks.append(((row == want) & (run == index[0])).astype(F32).astype(BF16))
        short_out[...] = lax.dot_general(
            pick_out[...],
            jnp.concatenate(blocks, axis=1),
            (((1,), (1,)), ((), ())),
            preferred_element_type=F32,
        ).astype(BF16)
    res_out[...] = res
    dir_out[...] = direction
    step_out[...] = step
    curved_out[...] = curved


def last_kernel(n_i, short, order, slots, ww, num, res, direction, step, curved, pick, *refs):
    msgs, (step_out, res_out) = sorted_as(order, refs[:n_i]), refs[n_i:]
    if short:
        pad = jnp.zeros((SHORT_PAD - SHORT, LANES), F32)
        values = jnp.concatenate([piece for msg in msgs for piece in (msg[...], pad)], axis=0)
        new = advance(msgs, SHORT - TAIL, ww, numbers_of(num), CAP - (SHORT - TAIL))
    else:
        values = slot_values(msgs, slots)
        new = advance(msgs, slots, ww, numbers_of(num))
    image = exact_pick(pick[...], values)
    last = res[...] + new["beta"] * direction[...]
    step_out[...] = step[...] + new["alpha"] * last
    image = image + new["beta"] * curved[...] + LAMBDA * last
    res_out[...] = res[...] - new["alpha"] * image


def exchange(x, axis, order=FEAT_ORDER):
    size = lax.axis_size(axis)
    if size != 4:
        return [lax.all_gather(x, axis, axis=0, tiled=True)]
    return [x] + [lax.ppermute(x, axis, [(i, i ^ k) for i in range(size)]) for k in order]


def exchange_each(arrays, axis):
    keys = (3, 2, 1)
    return [arrays[0]] + [
        lax.ppermute(x, axis, [(i, i ^ k) for i in range(4)])
        for k, x in zip(keys, arrays[1:], strict=True)
    ]


def sorted_as(order, refs):
    if len(refs) == 1:
        return refs
    return [refs[0]] + [refs[1 + order.index(k)] for k in (3, 2, 1)]


def in_hbm(x):
    return pltpu.with_memory_space_constraint(x, pltpu.HBM)


def body(tiles, tile_rows, tile_cols, tile_count, sample_ids, labels, weights):
    slots, edge = tiles.shape[2], tiles.shape[3]
    row_total, feat_len = labels.shape[1], weights.shape[1]
    row_blocks, col_blocks = row_total // edge, feat_len // edge
    assert row_blocks == SUB and edge == LANES and 2 * slots == LANES
    inst = lax.axis_size("inst")
    own_len = feat_len // inst
    own_blocks = own_len // edge
    tiles = tiles.reshape(slots, edge, edge)
    scale = float(row_total) / float(sample_ids.shape[1])
    index = lax.axis_index("inst").astype(I32).reshape(1)
    grid, msg_shape = f32(SUB, LANES), f32(slots + TAIL, LANES)
    short = inst == 4 and own_blocks == CAP_RUN
    tile_shape = jax.ShapeDtypeStruct((slots, edge, edge), BF16)
    picks = jax.ShapeDtypeStruct

    w = weights.reshape(col_blocks, edge)
    rows, slot, cols = call(
        first_look_kernel,
        (in_hbm(tile_rows.reshape(1, slots)), in_hbm(tile_cols.reshape(1, slots))),
        [HBM] * 2,
        [f32(slots, LANES), picks((slots, LANES), I32), pltpu.SMEM((1, slots), I32)],
        [VM, VM, SM],
        scratch=[pltpu.VMEM((1, slots), I32), pltpu.SemaphoreType.DMA((2,))],
        flops=1 << 30,
    )
    rows = jnp.where(slot < tile_count, rows, -1.0)
    part, row_mask = call(
        start_kernel,
        (cols, rows, tiles, w),
        [SM, VM, VM, VM],
        [f32(2 * SUB, LANES), f32(slots * SUB, LANES)],
        scratch=[pltpu.VMEM((slots, LANES), F32), pltpu.VMEM((3 * slots, LANES), F32)],
    )
    mask, cols_line, own, *send = call(
        prep_kernel,
        (sample_ids, rows, tile_cols.reshape(1, slots), index),
        [VM] * 3 + [SM],
        [grid, grid, f32(slots, LANES)]
        + [picks((4 * SHORT, slots), BF16)] * short,
    )
    (turned,) = call(turn_kernel, (tiles,), [VM], [tile_shape])
    got = exchange(part, "feat")
    n_f = len(got)
    msg, m, c, e, ww = call(
        functools.partial(margin_kernel, n_f, scale),
        (tiles, rows, mask, labels.reshape(SUB, LANES), cols_line, *got),
        [VM] * (5 + n_f),
        [msg_shape, grid, grid, grid, grid],
    )
    msgs = exchange(msg, "inst", ORDERS[0])
    n_i = len(msgs)
    (match,) = call(
        functools.partial(match_kernel, n_i, ORDERS[0]),
        (own, *msgs),
        [VM] * (1 + n_i),
        [picks((slots, slots * inst), BF16)],
    )

    def forward(msgs, order):
        (out,) = call(
            functools.partial(forward_kernel, n_i, order),
            (turned, row_mask, match, *msgs),
            [VM] * (3 + n_i),
            [grid],
            scratch=[pltpu.VMEM((3 * slots, LANES), F32)],
        )
        return exchange(out, "feat")

    got = forward(msgs, ORDERS[0])
    msg, v = call(
        functools.partial(first_kernel, n_f),
        (tiles, rows, m, c, e, *got),
        [VM] * (5 + n_f),
        [msg_shape, grid],
    )
    history = [msgs, exchange(msg, "inst", ORDERS[1])]
    state, nums = (e, v), []
    for k in range(ITERS - 1):
        got = forward(history[-1], ORDERS[k + 1])
        vec, num = call(
            functools.partial(numbers_kernel, n_i, slots, k == 0),
            (m, c, ww, *history[-1], *state),
            [VM] * (3 + n_i + len(state)),
            [f32(6 * SUB, LANES), grid],
        )
        if short and k == ITERS - 2:
            to_each = call(
                functools.partial(next_kernel, n_f, True),
                (tiles, rows, c, vec, num, *got, *send),
                [VM] * (6 + n_f),
                [f32(SHORT, LANES)] * 4,
                scratch=[pltpu.VMEM((slots, LANES), F32)],
            )
            history.append(exchange_each(to_each, "inst"))
            nums.append(num)
            break
        msg, *kept = call(
            functools.partial(next_kernel, n_f, False),
            (tiles, rows, c, vec, num, *got),
            [VM] * (5 + n_f),
            [msg_shape] + [grid, grid] * (k < ITERS - 2),
        )
        history.append(exchange(msg, "inst", ORDERS[k + 2]))
        state = (*kept, vec, num)
        nums.append(num)
    block = f32(own_blocks, edge)
    *dense, pick = call(
        functools.partial(dense_kernel, n_i, short, ORDERS, slots, ITERS),
        (w, index, *(ref for group in history[:ITERS] for ref in group), *nums),
        [VM, SM] + [VM] * (n_i * ITERS + len(nums)),
        [block] * 4 + [picks((own_blocks, LANES if short else slots * inst), BF16)],
        scratch=[pltpu.VMEM((own_blocks, slots * inst), BF16)] * short,
    )
    step, res = call(
        functools.partial(last_kernel, n_i, short, ORDERS[ITERS], slots),
        (ww, nums[-1], *dense, pick, *history[-1]),
        [VM] * (7 + n_i),
        [block, block],
    )
    return step.reshape(1, own_len), res.reshape(1, own_len)


def solution(mesh):
    return jax.shard_map(
        body,
        mesh=mesh,
        in_specs=(
            P(("groups", "inst"), "feat", None, None, None),
            P(("groups", "inst"), "feat", None),
            P(("groups", "inst"), "feat", None),
            P(("groups", "inst"), "feat"),
            P(("groups", "inst"), None),
            P(("groups", "inst"), None),
            P(("groups", "feat"), None),
        ),
        out_specs=(P(("groups", "feat"), "inst"), P(("groups", "feat"), "inst")),
        check_vma=False,
    )
```

```python
import functools

import jax
import jax.numpy as jnp
from jax import lax
from jax.experimental import pallas as pl
from jax.experimental.pallas import tpu as pltpu
from jax.sharding import PartitionSpec as P

ITERS = 3
LAMBDA = 0.02
ORDERS = ((1, 3, 2),) * ITERS + ((2, 3, 1),)
FEAT_ORDER = (1, 2, 3)

F32, BF16, I32 = jnp.float32, jnp.bfloat16, jnp.int32
LANES, SUB = 128, 8
TAIL = 8
COLS_ROW = 3
CAP, CAP_RUN = 17, 512
SHORT, SHORT_PAD = 24, 32


VM = pl.BlockSpec(memory_space=pltpu.VMEM)
SM = pl.BlockSpec(memory_space=pltpu.SMEM)
ANY = pl.BlockSpec(memory_space=pl.ANY)
HBM = pl.BlockSpec(memory_space=pltpu.HBM)


def call(kernel, ins, in_specs, outs, out_specs=None, scratch=(), flops=1 << 21):
    return pl.pallas_call(
        kernel,
        in_specs=in_specs,
        out_shape=outs,
        out_specs=out_specs or [VM] * len(outs),
        scratch_shapes=list(scratch),
        compiler_params=pltpu.CompilerParams(vmem_limit_bytes=24 << 20),
        cost_estimate=pl.CostEstimate(flops=flops, bytes_accessed=1 << 20, transcendentals=0),
    )(*ins)


def f32(*shape):
    return jax.ShapeDtypeStruct(shape, F32)


def iota(shape, dim):
    return lax.broadcasted_iota(I32, shape, dim)


def total(x):
    return jnp.sum(x, axis=(0, 1), keepdims=True)


def split3(x):
    hi = x.astype(BF16).astype(F32)
    rest = x - hi
    mid = rest.astype(BF16).astype(F32)
    return hi, mid, (rest - mid).astype(BF16).astype(F32)


def exact_pick(pick, values):
    wide = values.shape[1]
    pieces = jnp.concatenate(split3(values), axis=1).astype(BF16)
    out = jnp.dot(pick, pieces, preferred_element_type=F32)
    return out[:, :wide] + out[:, wide : 2 * wide] + out[:, 2 * wide :]


def left_of(pieces):
    return jnp.concatenate([*pieces, jnp.zeros((SUB, LANES), F32)], axis=0).astype(BF16)


def fold3(acc, at=0):
    return acc[at : at + SUB] + acc[at + SUB : at + 2 * SUB] + acc[at + 2 * SUB : at + 3 * SUB]


def save_pieces(x, pieces):
    slots = x.shape[0]
    for p, piece in enumerate(split3(x)):
        pieces[p * slots : (p + 1) * slots, :] = piece


def masked_line(pieces, slots, slot, mask):
    return [
        mask * jnp.broadcast_to(pieces[p * slots + slot : p * slots + slot + 1, :], (SUB, LANES))
        for p in range(3)
    ]


def by_rows(turned, pieces, row_mask):
    slots = turned.shape[0]
    acc = jnp.zeros((4 * SUB, LANES), F32)
    for s in range(0, slots, 2):
        left = [
            left_of(masked_line(pieces, slots, t, row_mask[t * SUB : (t + 1) * SUB, :]))
            for t in (s, s + 1)
        ]
        right = jnp.concatenate([turned[s], turned[s + 1]], axis=0)
        acc = acc + jnp.dot(
            jnp.concatenate(left, axis=1), right, preferred_element_type=F32
        )
    return fold3(acc)


def by_cols(tiles, rows, vec, msg):
    slots = tiles.shape[0]
    blocks = [jnp.broadcast_to(vec[r : r + 1, :], (SUB, LANES)) for r in range(SUB)]
    sub = iota((SUB, LANES), 0)
    for g in range(0, slots, SUB):
        row = rows[g : g + SUB, :]
        lines = jnp.zeros((SUB, LANES), F32)
        for r in range(SUB):
            lines = jnp.where(row == float(r), blocks[r], lines)
        group = split3(lines)
        acc = jnp.zeros((4 * SUB, LANES), F32)
        for s in range(0, SUB, 2):
            left = [left_of([jnp.where(sub == t, piece, 0.0) for piece in group]) for t in (s, s + 1)]
            right = jnp.concatenate([tiles[g + s], tiles[g + s + 1]], axis=0)
            acc = acc + jnp.dot(jnp.concatenate(left, axis=1), right, preferred_element_type=F32)
        msg[g : g + SUB, :] = fold3(acc)


def first_look_kernel(rows_hbm, cols_hbm, rows_out, slot_out, cols_out, rows_line, sems):
    pairs = ((rows_hbm, rows_line), (cols_hbm, cols_out))
    copies = [pltpu.make_async_copy(src, dst, sems.at[k]) for k, (src, dst) in enumerate(pairs)]
    for copy in copies:
        copy.start()
    slots = rows_line.shape[1]
    slot_out[...] = iota((slots, LANES), 0)
    copies[0].wait()
    line = rows_line[...].astype(F32)
    rows_out[...] = column_of(jnp.concatenate([line, line], axis=1), slots)
    copies[1].wait()


def start_kernel(cols, rows, tiles, w, part, row_mask, picked, pieces):
    slots = tiles.shape[0]
    sub = iota((SUB, LANES), 0).astype(F32)
    for t in range(slots):
        row_mask[t * SUB : (t + 1) * SUB, :] = (sub == rows[t : t + 1, :]).astype(F32)
    for t in range(slots):
        picked[t : t + 1, :] = w[pl.ds(cols[0, t], 1), :]
    save_pieces(picked[...], pieces)
    squares = jnp.zeros((SUB, LANES), F32)
    rows_w = w.shape[0]
    step_rows = min(rows_w, 256)
    for b in range(0, rows_w, step_rows):
        block = w[b : b + step_rows, :]
        squares = squares + jnp.sum((block * block).reshape(step_rows // SUB, SUB, LANES), axis=0)
    part[SUB : 2 * SUB, :] = squares
    acc = jnp.zeros((6 * SUB, 2 * LANES), F32)
    for s in range(0, slots, 4):
        a, b, c, d = (
            masked_line(pieces, slots, t, row_mask[t * SUB : (t + 1) * SUB, :]) for t in range(s, s + 4)
        )
        left = [jnp.concatenate([*x, *y], axis=0).astype(BF16) for x, y in ((a, c), (b, d))]
        right = [jnp.concatenate([tiles[t], tiles[t + 1]], axis=1) for t in (s, s + 2)]
        acc = acc + lax.dot_general(
            jnp.concatenate(left, axis=1),
            jnp.concatenate(right, axis=0),
            (((1,), (1,)), ((), ())),
            preferred_element_type=F32,
        )
    part[0:SUB, :] = fold3(acc[:, :LANES]) + fold3(acc[:, LANES:], 3 * SUB)


def turn_kernel(tiles, turned):
    for t in range(tiles.shape[0]):
        turned[t] = tiles[t].T


def ranks(line, column, parts):
    shift = CAP_RUN.bit_length() - 1
    run, run_column = line.astype(I32) >> shift, column.astype(I32) >> shift
    sub, lane = iota(column.shape, 0), iota(column.shape, 1)
    same = (run == run_column) & (sub < lane)
    if parts == 2:
        same = same & ((sub < LANES // 2) == (lane < LANES // 2))
    return run, jnp.sum(same.astype(F32), axis=0, keepdims=True).astype(I32)


def column_of(line, rows):
    wide = jnp.broadcast_to(line, (rows, LANES))
    own = jnp.where(iota((rows, LANES), 0) == iota((rows, LANES), 1), wide, 0.0)
    return jnp.broadcast_to(jnp.sum(own, axis=1, keepdims=True), (rows, LANES))


def prep_kernel(ids, rows, cols_line, index, mask_out, cols_out, own_out, *send_out):
    n = ids.shape[1]
    left = ((ids[...] >> 7) == iota((SUB, n), 0)).astype(F32).astype(BF16)
    right = ((ids[...] & (LANES - 1)) == iota((LANES, n), 0)).astype(F32).astype(BF16)
    hits = lax.dot_general(left, right, (((1,), (1,)), ((), ())), preferred_element_type=F32)
    mask_out[...] = jnp.minimum(hits, 1.0)
    slots = rows.shape[0]
    sub, lane = iota((slots, LANES), 0), iota((slots, LANES), 1)
    line = cols_line[...].astype(F32)
    line = jnp.concatenate([line, line], axis=1)
    own = jnp.where(rows[...] >= 0.0, column_of(line, slots), -1.0)
    line = jnp.sum(jnp.where(sub == (lane & (slots - 1)), own, 0.0), axis=0, keepdims=True)
    cols_out[...] = jnp.broadcast_to(line, (SUB, LANES))
    own_out[...] = own
    for out in send_out:
        run, rank = ranks(line, own, 1)
        row = iota((SHORT, LANES), 0)
        for j, k in enumerate((0, 3, 2, 1)):
            sent = (row == rank) & (run == (index[0] ^ k))
            out[j * SHORT : (j + 1) * SHORT, :] = sent.astype(F32)[:, :slots].astype(BF16)


def feat_sum(refs, first=0):
    out = None
    for ref, height in refs:
        for at in range(0, ref.shape[0], height):
            piece = ref[at + first : at + first + SUB, :]
            out = piece if out is None else out + piece
    return out


def parts_of(refs, slots):
    height = slots + TAIL
    return [(ref, at) for ref in refs for at in range(0, ref.shape[0], height)]


def summed(refs, slots, row):
    line = None
    for ref, at in parts_of(refs, slots):
        piece = ref[at + slots + row : at + slots + row + 1, :]
        line = piece if line is None else line + piece
    return total(line)


def slot_cols(refs, slots):
    parts = parts_of(refs, slots)
    low = iota((1, LANES), 1) < slots
    lines = []
    for a, b in zip(parts[::2], parts[1::2], strict=True):
        first, second = (r[at + slots + COLS_ROW : at + slots + COLS_ROW + 1, :] for r, at in (a, b))
        lines.append(jnp.where(low, first, second))
    return jnp.concatenate(lines, axis=1)


def slot_values(refs, slots):
    return jnp.concatenate([ref[at : at + slots, :] for ref, at in parts_of(refs, slots)], axis=0)


def write_tail(msg, slots, lines):
    pad = jnp.zeros((TAIL - len(lines), LANES), F32)
    msg[slots : slots + TAIL, :] = jnp.concatenate([*lines, pad], axis=0)


def line_of(x):
    return jnp.sum(x, axis=0, keepdims=True)


def margin_kernel(n_f, scale, tiles, rows, mask, labels, cols, *refs):
    got, (msg, m_out, c_out, e_out, ww_out) = refs[:n_f], refs[n_f:]
    slots = tiles.shape[0]
    pieces = [(ref, 2 * SUB) for ref in got]
    m = feat_sum(pieces)
    chance = jax.nn.sigmoid(m)
    e = chance - labels[...].astype(F32)
    by_cols(tiles, rows, e, msg)
    zero = jnp.zeros((1, LANES), F32)
    write_tail(msg, slots, [zero, zero, zero, cols[0:1, :]])
    ww_out[...] = feat_sum(pieces, SUB)
    c_out[...] = scale * mask[...] * chance * (1.0 - chance)
    m_out[...] = m
    e_out[...] = e


def match_kernel(n_i, order, own, *refs):
    got, (match,) = sorted_as(order, refs[:n_i]), refs[n_i:]
    slots = own.shape[0]
    line = slot_cols(got, slots)
    for at in range(0, line.shape[1], LANES):
        same = own[...] == line[:, at : at + LANES]
        match[:, at : at + LANES] = same.astype(F32).astype(BF16)


def forward_kernel(n_i, order, turned, row_mask, match, *refs):
    got, (out, pieces) = sorted_as(order, refs[:n_i]), refs[n_i:]
    slots = turned.shape[0]
    save_pieces(exact_pick(match[...], slot_values(got, slots)), pieces)
    out[...] = by_rows(turned, pieces, row_mask)


def first_kernel(n_f, tiles, rows, m, c, e, *refs):
    got, (msg, v_out) = refs[:n_f], refs[n_f:]
    slots = tiles.shape[0]
    v = -(LAMBDA * m[...] + feat_sum([(ref, SUB) for ref in got]))
    v_out[...] = v
    u = c[...] * v
    by_cols(tiles, rows, u, msg)
    s = -e[...]
    write_tail(msg, slots, [line_of(-LAMBDA * m[...] * s + s * v), line_of(u * v)])


NUMBERS = ("rr", "dd", "cur", "a_r", "a_d", "alpha", "beta")


def numbers_of(num):
    return {name: num[k : k + 1, 0:1] for k, name in enumerate(NUMBERS)}


def save_numbers(num, values):
    lines = [jnp.broadcast_to(values[name], (1, LANES)) for name in NUMBERS]
    num[...] = jnp.concatenate([*lines, jnp.zeros((1, LANES), F32)], axis=0)


def advance(msgs, slots, ww, old, shift=0):
    rr_new, cur_r = summed(msgs, slots, shift), summed(msgs, slots, shift + 1)
    if old is None:
        a_r = a_d = jnp.full((1, 1), -LAMBDA, F32)
        rr = a_r * a_r * total(ww[...]) + rr_new
        dd, cur, beta = rr, cur_r, jnp.zeros((1, 1), F32)
    else:
        cross = summed(msgs, slots, shift + 2)
        rr = old["a_r"] * old["a_r"] * total(ww[...]) + rr_new
        beta = rr / old["rr"]
        a_d = old["a_r"] + beta * old["a_d"]
        dd = rr + beta * beta * old["dd"]
        cur = cur_r + 2.0 * beta * cross + beta * beta * old["cur"]
        a_r = old["a_r"]
    alpha = rr / (cur + LAMBDA * dd)
    a_r = a_r - alpha * (LAMBDA * a_d)
    return {"rr": rr, "dd": dd, "cur": cur, "a_r": a_r, "a_d": a_d, "alpha": alpha, "beta": beta}


def at(ref, k):
    return ref[k * SUB : (k + 1) * SUB, :]


def save_all(ref, values):
    for k, value in enumerate(values):
        ref[k * SUB : (k + 1) * SUB, :] = value


def numbers_kernel(n_i, slots, first, m, c, ww, *refs):
    msgs = refs[:n_i]
    vec_out, num_out = refs[-2:]
    if first:
        e, v = refs[n_i:-2]
        new = advance(msgs, slots, ww, None)
        v_r, s_r = v[...], -e[...]
        v_d, s_d, gram = v_r, s_r, jnp.zeros((SUB, LANES), F32)
    else:
        v, gram_d, vec, num = refs[n_i:-2]
        new = advance(msgs, slots, ww, numbers_of(num))
        v_r, s_r = v[...], at(vec, 2)
        v_d = v_r + new["beta"] * at(vec, 1)
        s_d = s_r + new["beta"] * at(vec, 3)
        gram = new["beta"] * gram_d[...]
    v_r = v_r - new["alpha"] * (gram + LAMBDA * v_d)
    s_r = s_r - new["alpha"] * (c[...] * v_d + LAMBDA * s_d)
    save_all(vec_out, (v_r, v_d, s_r, s_d, new["a_r"] * m[...] * s_r, gram))
    save_numbers(num_out, new)


def next_kernel(n_f, short, tiles, rows, c, vec, num, *refs):
    got, (msg, *kept) = refs[:n_f], refs[n_f:]
    slots = tiles.shape[0]
    if short:
        send, *outs, msg = refs[n_f:]
    gram = feat_sum([(ref, SUB) for ref in got])
    v = at(vec, 0) - numbers_of(num)["alpha"] * gram
    u = c[...] * v
    by_cols(tiles, rows, u, msg)
    lines = [line_of(at(vec, 4) + at(vec, 2) * v), line_of(u * v), line_of(u * at(vec, 1))]
    if short:
        chosen = exact_pick(send[...], msg[...])
        pad = [jnp.zeros((n, LANES), F32) for n in (CAP, SHORT - CAP - len(lines))]
        tail = jnp.concatenate([pad[0], *lines, pad[1]], axis=0)
        for j, out in enumerate(outs):
            slots_rows = chosen[j * SHORT : (j + 1) * SHORT]
            out[...] = jnp.where(iota((SHORT, LANES), 0) < CAP, slots_rows, tail)
        return
    write_tail(msg, slots, lines)
    for out, value in zip(kept, (v, gram + at(vec, 5))):
        out[...] = value


def dense_kernel(n_i, short, orders, slots, iters, w, index, *refs):
    msgs = [sorted_as(orders[k], refs[k * n_i : (k + 1) * n_i]) for k in range(iters)]
    nums = [numbers_of(num) for num in refs[iters * n_i : iters * n_i + iters - 1]]
    res_out, dir_out, step_out, curved_out, pick_out = refs[iters * n_i + iters - 1 :][:5]
    if short:
        short_out, pick_out = refs[-2:]
    own_blocks = res_out.shape[0]
    line = slot_cols(msgs[0], slots)
    offset = index[0] * own_blocks
    own = (iota((own_blocks, LANES), 0) + offset).astype(F32)
    for a in range(0, line.shape[1], LANES):
        pick_out[:, a : a + LANES] = (own == line[:, a : a + LANES]).astype(F32).astype(BF16)
    mine = w[pl.ds(pl.multiple_of(offset, own_blocks), own_blocks), :]
    res = -LAMBDA * mine - exact_pick(pick_out[...], slot_values(msgs[0], slots))
    step = jnp.zeros_like(res)
    for k in range(iters - 1):
        image = exact_pick(pick_out[...], slot_values(msgs[k + 1], slots))
        if k == 0:
            direction, curved = res, image
        else:
            direction = res + nums[k]["beta"] * direction
            curved = image + nums[k]["beta"] * curved
        step = step + nums[k]["alpha"] * direction
        res = res - nums[k]["alpha"] * (curved + LAMBDA * direction)
    if short:
        blocks = []
        for a in range(0, line.shape[1], LANES):
            pair = line[:, a : a + LANES]
            run, rank = ranks(pair, column_of(pair, LANES), 2)
            first = a // slots * SHORT_PAD
            second = iota((1, LANES), 1) >= slots
            want = rank + jnp.where(second, first + SHORT_PAD, first)
            row = iota((LANES, LANES), 0)
            blocks.append(((row == want) & (run == index[0])).astype(F32).astype(BF16))
        short_out[...] = lax.dot_general(
            pick_out[...],
            jnp.concatenate(blocks, axis=1),
            (((1,), (1,)), ((), ())),
            preferred_element_type=F32,
        ).astype(BF16)
    res_out[...] = res
    dir_out[...] = direction
    step_out[...] = step
    curved_out[...] = curved


def last_kernel(n_i, short, order, slots, ww, num, res, direction, step, curved, pick, *refs):
    msgs, (step_out, res_out) = sorted_as(order, refs[:n_i]), refs[n_i:]
    if short:
        pad = jnp.zeros((SHORT_PAD - SHORT, LANES), F32)
        values = jnp.concatenate([piece for msg in msgs for piece in (msg[...], pad)], axis=0)
        new = advance(msgs, SHORT - TAIL, ww, numbers_of(num), CAP - (SHORT - TAIL))
    else:
        values = slot_values(msgs, slots)
        new = advance(msgs, slots, ww, numbers_of(num))
    image = exact_pick(pick[...], values)
    last = res[...] + new["beta"] * direction[...]
    step_out[...] = step[...] + new["alpha"] * last
    image = image + new["beta"] * curved[...] + LAMBDA * last
    res_out[...] = res[...] - new["alpha"] * image


def exchange(x, axis, order=FEAT_ORDER):
    size = lax.axis_size(axis)
    if size != 4:
        return [lax.all_gather(x, axis, axis=0, tiled=True)]
    return [x] + [lax.ppermute(x, axis, [(i, i ^ k) for i in range(size)]) for k in order]


def exchange_each(arrays, axis, order):
    to = dict(zip((3, 2, 1), arrays[1:], strict=True))
    return [arrays[0]] + [
        lax.ppermute(to[k], axis, [(i, i ^ k) for i in range(4)]) for k in order
    ]


def sorted_as(order, refs):
    if len(refs) == 1:
        return refs
    return [refs[0]] + [refs[1 + order.index(k)] for k in (3, 2, 1)]


def in_hbm(x):
    return pltpu.with_memory_space_constraint(x, pltpu.HBM)


def body(tiles, tile_rows, tile_cols, tile_count, sample_ids, labels, weights):
    slots, edge = tiles.shape[2], tiles.shape[3]
    row_total, feat_len = labels.shape[1], weights.shape[1]
    row_blocks, col_blocks = row_total // edge, feat_len // edge
    assert row_blocks == SUB and edge == LANES and 2 * slots == LANES
    inst = lax.axis_size("inst")
    own_len = feat_len // inst
    own_blocks = own_len // edge
    tiles = tiles.reshape(slots, edge, edge)
    scale = float(row_total) / float(sample_ids.shape[1])
    index = lax.axis_index("inst").astype(I32).reshape(1)
    grid, msg_shape = f32(SUB, LANES), f32(slots + TAIL, LANES)
    short = inst == 4 and own_blocks == CAP_RUN
    tile_shape = jax.ShapeDtypeStruct((slots, edge, edge), BF16)
    picks = jax.ShapeDtypeStruct

    w = weights.reshape(col_blocks, edge)
    rows, slot, cols = call(
        first_look_kernel,
        (in_hbm(tile_rows.reshape(1, slots)), in_hbm(tile_cols.reshape(1, slots))),
        [HBM] * 2,
        [f32(slots, LANES), picks((slots, LANES), I32), pltpu.SMEM((1, slots), I32)],
        [VM, VM, SM],
        scratch=[pltpu.VMEM((1, slots), I32), pltpu.SemaphoreType.DMA((2,))],
        flops=1 << 30,
    )
    rows = jnp.where(slot < tile_count, rows, -1.0)
    part, row_mask = call(
        start_kernel,
        (cols, rows, tiles, w),
        [SM, VM, VM, VM],
        [f32(2 * SUB, LANES), f32(slots * SUB, LANES)],
        scratch=[pltpu.VMEM((slots, LANES), F32), pltpu.VMEM((3 * slots, LANES), F32)],
    )
    mask, cols_line, own, *send = call(
        prep_kernel,
        (sample_ids, rows, tile_cols.reshape(1, slots), index),
        [VM] * 3 + [SM],
        [grid, grid, f32(slots, LANES)]
        + [picks((4 * SHORT, slots), BF16)] * short,
    )
    (turned,) = call(turn_kernel, (tiles,), [VM], [tile_shape])
    got = exchange(part, "feat")
    n_f = len(got)
    msg, m, c, e, ww = call(
        functools.partial(margin_kernel, n_f, scale),
        (tiles, rows, mask, labels.reshape(SUB, LANES), cols_line, *got),
        [VM] * (5 + n_f),
        [msg_shape, grid, grid, grid, grid],
    )
    msgs = exchange(msg, "inst", ORDERS[0])
    n_i = len(msgs)
    (match,) = call(
        functools.partial(match_kernel, n_i, ORDERS[0]),
        (own, *msgs),
        [VM] * (1 + n_i),
        [picks((slots, slots * inst), BF16)],
    )

    def forward(msgs, order):
        (out,) = call(
            functools.partial(forward_kernel, n_i, order),
            (turned, row_mask, match, *msgs),
            [VM] * (3 + n_i),
            [grid],
            scratch=[pltpu.VMEM((3 * slots, LANES), F32)],
        )
        return exchange(out, "feat")

    got = forward(msgs, ORDERS[0])
    msg, v = call(
        functools.partial(first_kernel, n_f),
        (tiles, rows, m, c, e, *got),
        [VM] * (5 + n_f),
        [msg_shape, grid],
    )
    history = [msgs, exchange(msg, "inst", ORDERS[1])]
    state, nums = (e, v), []
    for k in range(ITERS - 1):
        got = forward(history[-1], ORDERS[k + 1])
        vec, num = call(
            functools.partial(numbers_kernel, n_i, slots, k == 0),
            (m, c, ww, *history[-1], *state),
            [VM] * (3 + n_i + len(state)),
            [f32(6 * SUB, LANES), grid],
        )
        if short and k == ITERS - 2:
            to_each = call(
                functools.partial(next_kernel, n_f, True),
                (tiles, rows, c, vec, num, *got, *send),
                [VM] * (6 + n_f),
                [f32(SHORT, LANES)] * 4,
                scratch=[pltpu.VMEM((slots, LANES), F32)],
            )
            history.append(exchange_each(to_each, "inst", ORDERS[ITERS]))
            nums.append(num)
            break
        msg, *kept = call(
            functools.partial(next_kernel, n_f, False),
            (tiles, rows, c, vec, num, *got),
            [VM] * (5 + n_f),
            [msg_shape] + [grid, grid] * (k < ITERS - 2),
        )
        history.append(exchange(msg, "inst", ORDERS[k + 2]))
        state = (*kept, vec, num)
        nums.append(num)
    block = f32(own_blocks, edge)
    *dense, pick = call(
        functools.partial(dense_kernel, n_i, short, ORDERS, slots, ITERS),
        (w, index, *(ref for group in history[:ITERS] for ref in group), *nums),
        [VM, SM] + [VM] * (n_i * ITERS + len(nums)),
        [block] * 4 + [picks((own_blocks, LANES if short else slots * inst), BF16)],
        scratch=[pltpu.VMEM((own_blocks, slots * inst), BF16)] * short,
    )
    step, res = call(
        functools.partial(last_kernel, n_i, short, ORDERS[ITERS], slots),
        (ww, nums[-1], *dense, pick, *history[-1]),
        [VM] * (7 + n_i),
        [block, block],
    )
    return step.reshape(1, own_len), res.reshape(1, own_len)


def solution(mesh):
    return jax.shard_map(
        body,
        mesh=mesh,
        in_specs=(
            P(("groups", "inst"), "feat", None, None, None),
            P(("groups", "inst"), "feat", None),
            P(("groups", "inst"), "feat", None),
            P(("groups", "inst"), "feat"),
            P(("groups", "inst"), None),
            P(("groups", "inst"), None),
            P(("groups", "feat"), None),
        ),
        out_specs=(P(("groups", "feat"), "inst"), P(("groups", "feat"), "inst")),
        check_vma=False,
    )
```

```python
import functools

import jax
import jax.numpy as jnp
from jax import lax
from jax.experimental import pallas as pl
from jax.experimental.pallas import tpu as pltpu
from jax.sharding import PartitionSpec as P

ITERS = 3
LAMBDA = 0.02
ORDERS = ((1, 3, 2),) * ITERS + ((2, 3, 1),)
FEAT_ORDER = (1, 2, 3)

F32, BF16, I32 = jnp.float32, jnp.bfloat16, jnp.int32
LANES, SUB = 128, 8
TAIL = 8
COLS_ROW = 3
CAP, CAP_RUN = 17, 512
SHORT, SHORT_PAD = 24, 32


VM = pl.BlockSpec(memory_space=pltpu.VMEM)
SM = pl.BlockSpec(memory_space=pltpu.SMEM)
ANY = pl.BlockSpec(memory_space=pl.ANY)
HBM = pl.BlockSpec(memory_space=pltpu.HBM)


def call(kernel, ins, in_specs, outs, out_specs=None, scratch=(), flops=1 << 21):
    return pl.pallas_call(
        kernel,
        in_specs=in_specs,
        out_shape=outs,
        out_specs=out_specs or [VM] * len(outs),
        scratch_shapes=list(scratch),
        compiler_params=pltpu.CompilerParams(vmem_limit_bytes=24 << 20),
        cost_estimate=pl.CostEstimate(flops=flops, bytes_accessed=1 << 20, transcendentals=0),
    )(*ins)


def f32(*shape):
    return jax.ShapeDtypeStruct(shape, F32)


def iota(shape, dim):
    return lax.broadcasted_iota(I32, shape, dim)


def total(x):
    return jnp.sum(x, axis=(0, 1), keepdims=True)


def split3(x):
    hi = x.astype(BF16).astype(F32)
    rest = x - hi
    mid = rest.astype(BF16).astype(F32)
    return hi, mid, rest - mid


def exact_pick(pick, values):
    wide = values.shape[1]
    pieces = jnp.concatenate(split3(values), axis=1).astype(BF16)
    out = jnp.dot(pick, pieces, preferred_element_type=F32)
    return out[:, :wide] + out[:, wide : 2 * wide] + out[:, 2 * wide :]


def left_of(pieces):
    return jnp.concatenate([*pieces, jnp.zeros((SUB, LANES), F32)], axis=0).astype(BF16)


def fold3(acc, at=0):
    return acc[at : at + SUB] + acc[at + SUB : at + 2 * SUB] + acc[at + 2 * SUB : at + 3 * SUB]


def save_pieces(x, pieces):
    slots = x.shape[0]
    for p, piece in enumerate(split3(x)):
        pieces[p * slots : (p + 1) * slots, :] = piece


def masked_line(pieces, slots, slot, mask):
    return [
        mask * jnp.broadcast_to(pieces[p * slots + slot : p * slots + slot + 1, :], (SUB, LANES))
        for p in range(3)
    ]


def by_rows(turned, pieces, row_mask):
    slots = turned.shape[0]
    acc = jnp.zeros((4 * SUB, LANES), F32)
    for s in range(0, slots, 2):
        left = [
            left_of(masked_line(pieces, slots, t, row_mask[t * SUB : (t + 1) * SUB, :]))
            for t in (s, s + 1)
        ]
        right = jnp.concatenate([turned[s], turned[s + 1]], axis=0)
        acc = acc + jnp.dot(
            jnp.concatenate(left, axis=1), right, preferred_element_type=F32
        )
    return fold3(acc)


def by_cols(tiles, rows, vec, msg):
    slots = tiles.shape[0]
    blocks = [jnp.broadcast_to(vec[r : r + 1, :], (SUB, LANES)) for r in range(SUB)]
    sub = iota((SUB, LANES), 0)
    for g in range(0, slots, SUB):
        row = rows[g : g + SUB, :]
        lines = jnp.zeros((SUB, LANES), F32)
        for r in range(SUB):
            lines = jnp.where(row == float(r), blocks[r], lines)
        group = split3(lines)
        acc = jnp.zeros((4 * SUB, LANES), F32)
        for s in range(0, SUB, 2):
            left = [left_of([jnp.where(sub == t, piece, 0.0) for piece in group]) for t in (s, s + 1)]
            right = jnp.concatenate([tiles[g + s], tiles[g + s + 1]], axis=0)
            acc = acc + jnp.dot(jnp.concatenate(left, axis=1), right, preferred_element_type=F32)
        msg[g : g + SUB, :] = fold3(acc)


def first_look_kernel(rows_hbm, cols_hbm, rows_out, slot_out, cols_out, rows_line, sems):
    pairs = ((rows_hbm, rows_line), (cols_hbm, cols_out))
    copies = [pltpu.make_async_copy(src, dst, sems.at[k]) for k, (src, dst) in enumerate(pairs)]
    for copy in copies:
        copy.start()
    slots = rows_line.shape[1]
    slot_out[...] = iota((slots, LANES), 0)
    copies[0].wait()
    line = rows_line[...].astype(F32)
    rows_out[...] = column_of(jnp.concatenate([line, line], axis=1), slots)
    copies[1].wait()


def start_kernel(cols, rows, tiles, w, part, row_mask, picked, pieces):
    slots = tiles.shape[0]
    sub = iota((SUB, LANES), 0).astype(F32)
    for t in range(slots):
        row_mask[t * SUB : (t + 1) * SUB, :] = (sub == rows[t : t + 1, :]).astype(F32)
    for t in range(slots):
        picked[t : t + 1, :] = w[pl.ds(cols[0, t], 1), :]
    save_pieces(picked[...], pieces)
    squares = jnp.zeros((SUB, LANES), F32)
    rows_w = w.shape[0]
    step_rows = min(rows_w, 256)
    for b in range(0, rows_w, step_rows):
        block = w[b : b + step_rows, :]
        squares = squares + jnp.sum((block * block).reshape(step_rows // SUB, SUB, LANES), axis=0)
    part[SUB : 2 * SUB, :] = squares
    acc = jnp.zeros((6 * SUB, 2 * LANES), F32)
    for s in range(0, slots, 4):
        a, b, c, d = (
            masked_line(pieces, slots, t, row_mask[t * SUB : (t + 1) * SUB, :]) for t in range(s, s + 4)
        )
        left = [jnp.concatenate([*x, *y], axis=0).astype(BF16) for x, y in ((a, c), (b, d))]
        right = [jnp.concatenate([tiles[t], tiles[t + 1]], axis=1) for t in (s, s + 2)]
        acc = acc + lax.dot_general(
            jnp.concatenate(left, axis=1),
            jnp.concatenate(right, axis=0),
            (((1,), (1,)), ((), ())),
            preferred_element_type=F32,
        )
    part[0:SUB, :] = fold3(acc[:, :LANES]) + fold3(acc[:, LANES:], 3 * SUB)


def turn_kernel(tiles, turned):
    for t in range(tiles.shape[0]):
        turned[t] = tiles[t].T


def ranks(line, column, parts):
    shift = CAP_RUN.bit_length() - 1
    run, run_column = line.astype(I32) >> shift, column.astype(I32) >> shift
    sub, lane = iota(column.shape, 0), iota(column.shape, 1)
    same = (run == run_column) & (sub < lane)
    if parts == 2:
        same = same & ((sub < LANES // 2) == (lane < LANES // 2))
    return run, jnp.sum(same.astype(F32), axis=0, keepdims=True).astype(I32)


def column_of(line, rows):
    wide = jnp.broadcast_to(line, (rows, LANES))
    own = jnp.where(iota((rows, LANES), 0) == iota((rows, LANES), 1), wide, 0.0)
    return jnp.broadcast_to(jnp.sum(own, axis=1, keepdims=True), (rows, LANES))


def prep_kernel(ids, rows, cols_line, index, mask_out, cols_out, own_out, *send_out):
    n = ids.shape[1]
    left = ((ids[...] >> 7) == iota((SUB, n), 0)).astype(F32).astype(BF16)
    right = ((ids[...] & (LANES - 1)) == iota((LANES, n), 0)).astype(F32).astype(BF16)
    hits = lax.dot_general(left, right, (((1,), (1,)), ((), ())), preferred_element_type=F32)
    mask_out[...] = jnp.minimum(hits, 1.0)
    slots = rows.shape[0]
    sub, lane = iota((slots, LANES), 0), iota((slots, LANES), 1)
    line = cols_line[...].astype(F32)
    line = jnp.concatenate([line, line], axis=1)
    own = jnp.where(rows[...] >= 0.0, column_of(line, slots), -1.0)
    line = jnp.sum(jnp.where(sub == (lane & (slots - 1)), own, 0.0), axis=0, keepdims=True)
    cols_out[...] = jnp.broadcast_to(line, (SUB, LANES))
    own_out[...] = own
    for out in send_out:
        run, rank = ranks(line, own, 1)
        row = iota((SHORT, LANES), 0)
        sent = [((row == rank) & (run == (index[0] ^ k))).astype(F32) for k in (0, 3, 2, 1)]
        out[...] = jnp.concatenate(sent, axis=0)[:, :slots].astype(BF16)


def feat_sum(refs, first=0):
    out = None
    for ref, height in refs:
        for at in range(0, ref.shape[0], height):
            piece = ref[at + first : at + first + SUB, :]
            out = piece if out is None else out + piece
    return out


def parts_of(refs, slots):
    height = slots + TAIL
    return [(ref, at) for ref in refs for at in range(0, ref.shape[0], height)]


def summed(refs, slots, row):
    line = None
    for ref, at in parts_of(refs, slots):
        piece = ref[at + slots + row : at + slots + row + 1, :]
        line = piece if line is None else line + piece
    return total(line)


def slot_cols(refs, slots):
    parts = parts_of(refs, slots)
    low = iota((1, LANES), 1) < slots
    lines = []
    for a, b in zip(parts[::2], parts[1::2], strict=True):
        first, second = (r[at + slots + COLS_ROW : at + slots + COLS_ROW + 1, :] for r, at in (a, b))
        lines.append(jnp.where(low, first, second))
    return jnp.concatenate(lines, axis=1)


def slot_values(refs, slots):
    return jnp.concatenate([ref[at : at + slots, :] for ref, at in parts_of(refs, slots)], axis=0)


def write_tail(msg, slots, lines):
    pad = jnp.zeros((TAIL - len(lines), LANES), F32)
    msg[slots : slots + TAIL, :] = jnp.concatenate([*lines, pad], axis=0)


def line_of(x):
    return jnp.sum(x, axis=0, keepdims=True)


def margin_kernel(n_f, scale, tiles, rows, mask, labels, cols, *refs):
    got, (msg, m_out, c_out, e_out, ww_out) = refs[:n_f], refs[n_f:]
    slots = tiles.shape[0]
    pieces = [(ref, 2 * SUB) for ref in got]
    m = feat_sum(pieces)
    chance = jax.nn.sigmoid(m)
    e = chance - labels[...].astype(F32)
    by_cols(tiles, rows, e, msg)
    zero = jnp.zeros((1, LANES), F32)
    write_tail(msg, slots, [zero, zero, zero, cols[0:1, :]])
    ww_out[...] = feat_sum(pieces, SUB)
    c_out[...] = scale * mask[...] * chance * (1.0 - chance)
    m_out[...] = m
    e_out[...] = e


def match_kernel(n_i, order, own, *refs):
    got, (match,) = sorted_as(order, refs[:n_i]), refs[n_i:]
    slots = own.shape[0]
    line = slot_cols(got, slots)
    for at in range(0, line.shape[1], LANES):
        same = own[...] == line[:, at : at + LANES]
        match[:, at : at + LANES] = same.astype(F32).astype(BF16)


def forward_kernel(n_i, order, turned, row_mask, match, *refs):
    got, (out, pieces) = sorted_as(order, refs[:n_i]), refs[n_i:]
    slots = turned.shape[0]
    save_pieces(exact_pick(match[...], slot_values(got, slots)), pieces)
    out[...] = by_rows(turned, pieces, row_mask)


def first_kernel(n_f, tiles, rows, m, c, e, *refs):
    got, (msg, v_out) = refs[:n_f], refs[n_f:]
    slots = tiles.shape[0]
    v = -(LAMBDA * m[...] + feat_sum([(ref, SUB) for ref in got]))
    v_out[...] = v
    u = c[...] * v
    by_cols(tiles, rows, u, msg)
    s = -e[...]
    write_tail(msg, slots, [line_of(-LAMBDA * m[...] * s + s * v), line_of(u * v)])


NUMBERS = ("rr", "dd", "cur", "a_r", "a_d", "alpha", "beta")


def numbers_of(num):
    return {name: num[k : k + 1, 0:1] for k, name in enumerate(NUMBERS)}


def save_numbers(num, values):
    lines = [jnp.broadcast_to(values[name], (1, LANES)) for name in NUMBERS]
    num[...] = jnp.concatenate([*lines, jnp.zeros((1, LANES), F32)], axis=0)


def advance(msgs, slots, ww, old, shift=0):
    rr_new, cur_r = summed(msgs, slots, shift), summed(msgs, slots, shift + 1)
    if old is None:
        a_r = a_d = jnp.full((1, 1), -LAMBDA, F32)
        rr = a_r * a_r * total(ww[...]) + rr_new
        dd, cur, beta = rr, cur_r, jnp.zeros((1, 1), F32)
    else:
        cross = summed(msgs, slots, shift + 2)
        rr = old["a_r"] * old["a_r"] * total(ww[...]) + rr_new
        beta = rr / old["rr"]
        a_d = old["a_r"] + beta * old["a_d"]
        dd = rr + beta * beta * old["dd"]
        cur = cur_r + 2.0 * beta * cross + beta * beta * old["cur"]
        a_r = old["a_r"]
    alpha = rr / (cur + LAMBDA * dd)
    a_r = a_r - alpha * (LAMBDA * a_d)
    return {"rr": rr, "dd": dd, "cur": cur, "a_r": a_r, "a_d": a_d, "alpha": alpha, "beta": beta}


def at(ref, k):
    return ref[k * SUB : (k + 1) * SUB, :]


def save_all(ref, values):
    for k, value in enumerate(values):
        ref[k * SUB : (k + 1) * SUB, :] = value


def numbers_kernel(n_i, slots, first, m, c, ww, *refs):
    msgs = refs[:n_i]
    vec_out, num_out = refs[-2:]
    if first:
        e, v = refs[n_i:-2]
        new = advance(msgs, slots, ww, None)
        v_r, s_r = v[...], -e[...]
        v_d, s_d, gram = v_r, s_r, jnp.zeros((SUB, LANES), F32)
    else:
        v, gram_d, vec, num = refs[n_i:-2]
        new = advance(msgs, slots, ww, numbers_of(num))
        v_r, s_r = v[...], at(vec, 2)
        v_d = v_r + new["beta"] * at(vec, 1)
        s_d = s_r + new["beta"] * at(vec, 3)
        gram = new["beta"] * gram_d[...]
    v_r = v_r - new["alpha"] * (gram + LAMBDA * v_d)
    s_r = s_r - new["alpha"] * (c[...] * v_d + LAMBDA * s_d)
    save_all(vec_out, (v_r, v_d, s_r, s_d, new["a_r"] * m[...] * s_r, gram))
    save_numbers(num_out, new)


def next_kernel(n_f, short, tiles, rows, c, vec, num, *refs):
    got, (msg, *kept) = refs[:n_f], refs[n_f:]
    slots = tiles.shape[0]
    if short:
        send, *outs, msg = refs[n_f:]
    gram = feat_sum([(ref, SUB) for ref in got])
    v = at(vec, 0) - numbers_of(num)["alpha"] * gram
    u = c[...] * v
    by_cols(tiles, rows, u, msg)
    lines = [line_of(at(vec, 4) + at(vec, 2) * v), line_of(u * v), line_of(u * at(vec, 1))]
    if short:
        chosen = exact_pick(send[...], msg[...])
        pad = [jnp.zeros((n, LANES), F32) for n in (CAP, SHORT - CAP - len(lines))]
        tail = jnp.concatenate([pad[0], *lines, pad[1]], axis=0)
        for j, out in enumerate(outs):
            slots_rows = chosen[j * SHORT : (j + 1) * SHORT]
            out[...] = jnp.where(iota((SHORT, LANES), 0) < CAP, slots_rows, tail)
        return
    write_tail(msg, slots, lines)
    for out, value in zip(kept, (v, gram + at(vec, 5))):
        out[...] = value


def dense_kernel(n_i, short, orders, slots, iters, w, index, *refs):
    msgs = [sorted_as(orders[k], refs[k * n_i : (k + 1) * n_i]) for k in range(iters)]
    nums = [numbers_of(num) for num in refs[iters * n_i : iters * n_i + iters - 1]]
    res_out, dir_out, step_out, curved_out, pick_out = refs[iters * n_i + iters - 1 :][:5]
    if short:
        short_out, pick_out = refs[-2:]
    own_blocks = res_out.shape[0]
    line = slot_cols(msgs[0], slots)
    offset = index[0] * own_blocks
    own = (iota((own_blocks, LANES), 0) + offset).astype(F32)
    for a in range(0, line.shape[1], LANES):
        pick_out[:, a : a + LANES] = (own == line[:, a : a + LANES]).astype(F32).astype(BF16)
    mine = w[pl.ds(pl.multiple_of(offset, own_blocks), own_blocks), :]
    res = -LAMBDA * mine - exact_pick(pick_out[...], slot_values(msgs[0], slots))
    step = jnp.zeros_like(res)
    for k in range(iters - 1):
        image = exact_pick(pick_out[...], slot_values(msgs[k + 1], slots))
        if k == 0:
            direction, curved = res, image
        else:
            direction = res + nums[k]["beta"] * direction
            curved = image + nums[k]["beta"] * curved
        step = step + nums[k]["alpha"] * direction
        res = res - nums[k]["alpha"] * (curved + LAMBDA * direction)
    if short:
        blocks = []
        for a in range(0, line.shape[1], LANES):
            pair = line[:, a : a + LANES]
            run, rank = ranks(pair, column_of(pair, LANES), 2)
            first = a // slots * SHORT_PAD
            second = iota((1, LANES), 1) >= slots
            want = rank + jnp.where(second, first + SHORT_PAD, first)
            row = iota((LANES, LANES), 0)
            blocks.append(((row == want) & (run == index[0])).astype(F32).astype(BF16))
        short_out[...] = lax.dot_general(
            pick_out[...],
            jnp.concatenate(blocks, axis=1),
            (((1,), (1,)), ((), ())),
            preferred_element_type=F32,
        ).astype(BF16)
    res_out[...] = res
    dir_out[...] = direction
    step_out[...] = step
    curved_out[...] = curved


def last_kernel(n_i, short, order, slots, ww, num, res, direction, step, curved, pick, *refs):
    msgs, (step_out, res_out) = sorted_as(order, refs[:n_i]), refs[n_i:]
    if short:
        pad = jnp.zeros((SHORT_PAD - SHORT, LANES), F32)
        values = jnp.concatenate([piece for msg in msgs for piece in (msg[...], pad)], axis=0)
        new = advance(msgs, SHORT - TAIL, ww, numbers_of(num), CAP - (SHORT - TAIL))
    else:
        values = slot_values(msgs, slots)
        new = advance(msgs, slots, ww, numbers_of(num))
    image = exact_pick(pick[...], values)
    last = res[...] + new["beta"] * direction[...]
    step_out[...] = step[...] + new["alpha"] * last
    image = image + new["beta"] * curved[...] + LAMBDA * last
    res_out[...] = res[...] - new["alpha"] * image


def exchange(x, axis, order=FEAT_ORDER):
    size = lax.axis_size(axis)
    if size != 4:
        return [lax.all_gather(x, axis, axis=0, tiled=True)]
    return [x] + [lax.ppermute(x, axis, [(i, i ^ k) for i in range(size)]) for k in order]


def exchange_each(arrays, axis, order):
    to = dict(zip((3, 2, 1), arrays[1:], strict=True))
    return [arrays[0]] + [
        lax.ppermute(to[k], axis, [(i, i ^ k) for i in range(4)]) for k in order
    ]


def sorted_as(order, refs):
    if len(refs) == 1:
        return refs
    return [refs[0]] + [refs[1 + order.index(k)] for k in (3, 2, 1)]


def in_hbm(x):
    return pltpu.with_memory_space_constraint(x, pltpu.HBM)


def body(tiles, tile_rows, tile_cols, tile_count, sample_ids, labels, weights):
    slots, edge = tiles.shape[2], tiles.shape[3]
    row_total, feat_len = labels.shape[1], weights.shape[1]
    row_blocks, col_blocks = row_total // edge, feat_len // edge
    assert row_blocks == SUB and edge == LANES and 2 * slots == LANES
    inst = lax.axis_size("inst")
    own_len = feat_len // inst
    own_blocks = own_len // edge
    tiles = tiles.reshape(slots, edge, edge)
    scale = float(row_total) / float(sample_ids.shape[1])
    index = lax.axis_index("inst").astype(I32).reshape(1)
    grid, msg_shape = f32(SUB, LANES), f32(slots + TAIL, LANES)
    short = inst == 4 and own_blocks == CAP_RUN
    tile_shape = jax.ShapeDtypeStruct((slots, edge, edge), BF16)
    picks = jax.ShapeDtypeStruct

    w = weights.reshape(col_blocks, edge)
    rows, slot, cols = call(
        first_look_kernel,
        (in_hbm(tile_rows.reshape(1, slots)), in_hbm(tile_cols.reshape(1, slots))),
        [HBM] * 2,
        [f32(slots, LANES), picks((slots, LANES), I32), pltpu.SMEM((1, slots), I32)],
        [VM, VM, SM],
        scratch=[pltpu.VMEM((1, slots), I32), pltpu.SemaphoreType.DMA((2,))],
        flops=1 << 30,
    )
    rows = jnp.where(slot < tile_count, rows, -1.0)
    part, row_mask = call(
        start_kernel,
        (cols, rows, tiles, w),
        [SM, VM, VM, VM],
        [f32(2 * SUB, LANES), f32(slots * SUB, LANES)],
        scratch=[pltpu.VMEM((slots, LANES), F32), pltpu.VMEM((3 * slots, LANES), F32)],
    )
    mask, cols_line, own, *send = call(
        prep_kernel,
        (sample_ids, rows, tile_cols.reshape(1, slots), index),
        [VM] * 3 + [SM],
        [grid, grid, f32(slots, LANES)]
        + [picks((4 * SHORT, slots), BF16)] * short,
    )
    (turned,) = call(turn_kernel, (tiles,), [VM], [tile_shape])
    got = exchange(part, "feat")
    n_f = len(got)
    msg, m, c, e, ww = call(
        functools.partial(margin_kernel, n_f, scale),
        (tiles, rows, mask, labels.reshape(SUB, LANES), cols_line, *got),
        [VM] * (5 + n_f),
        [msg_shape, grid, grid, grid, grid],
    )
    msgs = exchange(msg, "inst", ORDERS[0])
    n_i = len(msgs)
    (match,) = call(
        functools.partial(match_kernel, n_i, ORDERS[0]),
        (own, *msgs),
        [VM] * (1 + n_i),
        [picks((slots, slots * inst), BF16)],
    )

    def forward(msgs, order):
        (out,) = call(
            functools.partial(forward_kernel, n_i, order),
            (turned, row_mask, match, *msgs),
            [VM] * (3 + n_i),
            [grid],
            scratch=[pltpu.VMEM((3 * slots, LANES), F32)],
        )
        return exchange(out, "feat")

    got = forward(msgs, ORDERS[0])
    msg, v = call(
        functools.partial(first_kernel, n_f),
        (tiles, rows, m, c, e, *got),
        [VM] * (5 + n_f),
        [msg_shape, grid],
    )
    history = [msgs, exchange(msg, "inst", ORDERS[1])]
    state, nums = (e, v), []
    for k in range(ITERS - 1):
        got = forward(history[-1], ORDERS[k + 1])
        vec, num = call(
            functools.partial(numbers_kernel, n_i, slots, k == 0),
            (m, c, ww, *history[-1], *state),
            [VM] * (3 + n_i + len(state)),
            [f32(6 * SUB, LANES), grid],
        )
        if short and k == ITERS - 2:
            to_each = call(
                functools.partial(next_kernel, n_f, True),
                (tiles, rows, c, vec, num, *got, *send),
                [VM] * (6 + n_f),
                [f32(SHORT, LANES)] * 4,
                scratch=[pltpu.VMEM((slots, LANES), F32)],
            )
            history.append(exchange_each(to_each, "inst", ORDERS[ITERS]))
            nums.append(num)
            break
        msg, *kept = call(
            functools.partial(next_kernel, n_f, False),
            (tiles, rows, c, vec, num, *got),
            [VM] * (5 + n_f),
            [msg_shape] + [grid, grid] * (k < ITERS - 2),
        )
        history.append(exchange(msg, "inst", ORDERS[k + 2]))
        state = (*kept, vec, num)
        nums.append(num)
    block = f32(own_blocks, edge)
    *dense, pick = call(
        functools.partial(dense_kernel, n_i, short, ORDERS, slots, ITERS),
        (w, index, *(ref for group in history[:ITERS] for ref in group), *nums),
        [VM, SM] + [VM] * (n_i * ITERS + len(nums)),
        [block] * 4 + [picks((own_blocks, LANES if short else slots * inst), BF16)],
        scratch=[pltpu.VMEM((own_blocks, slots * inst), BF16)] * short,
    )
    step, res = call(
        functools.partial(last_kernel, n_i, short, ORDERS[ITERS], slots),
        (ww, nums[-1], *dense, pick, *history[-1]),
        [VM] * (7 + n_i),
        [block, block],
    )
    return step.reshape(1, own_len), res.reshape(1, own_len)


def solution(mesh):
    return jax.shard_map(
        body,
        mesh=mesh,
        in_specs=(
            P(("groups", "inst"), "feat", None, None, None),
            P(("groups", "inst"), "feat", None),
            P(("groups", "inst"), "feat", None),
            P(("groups", "inst"), "feat"),
            P(("groups", "inst"), None),
            P(("groups", "inst"), None),
            P(("groups", "feat"), None),
        ),
        out_specs=(P(("groups", "feat"), "inst"), P(("groups", "feat"), "inst")),
        check_vma=False,
    )
```

```python
import functools

import jax
import jax.numpy as jnp
from jax import lax
from jax.experimental import pallas as pl
from jax.experimental.pallas import tpu as pltpu
from jax.sharding import PartitionSpec as P

ITERS = 3
LAMBDA = 0.02
ORDERS = ((1, 3, 2),) * ITERS + ((2, 3, 1),)
FEAT_ORDER = (1, 2, 3)

F32, BF16, I32 = jnp.float32, jnp.bfloat16, jnp.int32
LANES, SUB = 128, 8
TAIL = 8
COLS_ROW = 3
CAP, CAP_RUN = 17, 512
SHORT, SHORT_PAD = 24, 32


VM = pl.BlockSpec(memory_space=pltpu.VMEM)
SM = pl.BlockSpec(memory_space=pltpu.SMEM)
ANY = pl.BlockSpec(memory_space=pl.ANY)
HBM = pl.BlockSpec(memory_space=pltpu.HBM)


def call(kernel, ins, in_specs, outs, out_specs=None, scratch=(), flops=1 << 21):
    return pl.pallas_call(
        kernel,
        in_specs=in_specs,
        out_shape=outs,
        out_specs=out_specs or [VM] * len(outs),
        scratch_shapes=list(scratch),
        compiler_params=pltpu.CompilerParams(vmem_limit_bytes=24 << 20),
        cost_estimate=pl.CostEstimate(flops=flops, bytes_accessed=1 << 20, transcendentals=0),
    )(*ins)


def f32(*shape):
    return jax.ShapeDtypeStruct(shape, F32)


def iota(shape, dim):
    return lax.broadcasted_iota(I32, shape, dim)


def total(x):
    return jnp.sum(x, axis=(0, 1), keepdims=True)


def split3(x):
    hi = x.astype(BF16).astype(F32)
    rest = x - hi
    mid = rest.astype(BF16).astype(F32)
    return hi, mid, rest - mid


def exact_pick(pick, values):
    wide = values.shape[1]
    if values.shape[0] % LANES == 0:
        pieces = jnp.concatenate(split3(values), axis=0).astype(BF16)
        return jnp.dot(jnp.concatenate([pick] * 3, axis=1), pieces, preferred_element_type=F32)
    pieces = jnp.concatenate(split3(values), axis=1).astype(BF16)
    out = jnp.dot(pick, pieces, preferred_element_type=F32)
    return out[:, :wide] + out[:, wide : 2 * wide] + out[:, 2 * wide :]


def left_of(pieces):
    return jnp.concatenate([*pieces, jnp.zeros((SUB, LANES), F32)], axis=0).astype(BF16)


def fold3(acc, at=0):
    return acc[at : at + SUB] + acc[at + SUB : at + 2 * SUB] + acc[at + 2 * SUB : at + 3 * SUB]


def save_pieces(x, pieces):
    slots = x.shape[0]
    for p, piece in enumerate(split3(x)):
        pieces[p * slots : (p + 1) * slots, :] = piece


def masked_line(pieces, slots, slot, mask):
    return [
        mask * jnp.broadcast_to(pieces[p * slots + slot : p * slots + slot + 1, :], (SUB, LANES))
        for p in range(3)
    ]


def by_rows(turned, pieces, row_mask):
    slots = turned.shape[0]
    acc = jnp.zeros((4 * SUB, LANES), F32)
    for s in range(0, slots, 2):
        left = [
            left_of(masked_line(pieces, slots, t, row_mask[t * SUB : (t + 1) * SUB, :]))
            for t in (s, s + 1)
        ]
        right = jnp.concatenate([turned[s], turned[s + 1]], axis=0)
        acc = acc + jnp.dot(
            jnp.concatenate(left, axis=1), right, preferred_element_type=F32
        )
    return fold3(acc)


def by_cols(tiles, rows, vec, msg):
    slots = tiles.shape[0]
    blocks = [jnp.broadcast_to(vec[r : r + 1, :], (SUB, LANES)) for r in range(SUB)]
    sub = iota((SUB, LANES), 0)
    for g in range(0, slots, SUB):
        row = rows[g : g + SUB, :]
        lines = jnp.zeros((SUB, LANES), F32)
        for r in range(SUB):
            lines = jnp.where(row == float(r), blocks[r], lines)
        group = split3(lines)
        acc = jnp.zeros((4 * SUB, LANES), F32)
        for s in range(0, SUB, 2):
            left = [left_of([jnp.where(sub == t, piece, 0.0) for piece in group]) for t in (s, s + 1)]
            right = jnp.concatenate([tiles[g + s], tiles[g + s + 1]], axis=0)
            acc = acc + jnp.dot(jnp.concatenate(left, axis=1), right, preferred_element_type=F32)
        msg[g : g + SUB, :] = fold3(acc)


def first_look_kernel(rows_hbm, cols_hbm, rows_out, slot_out, cols_out, rows_line, sems):
    pairs = ((rows_hbm, rows_line), (cols_hbm, cols_out))
    copies = [pltpu.make_async_copy(src, dst, sems.at[k]) for k, (src, dst) in enumerate(pairs)]
    for copy in copies:
        copy.start()
    slots = rows_line.shape[1]
    slot_out[...] = iota((slots, LANES), 0)
    copies[0].wait()
    line = rows_line[...].astype(F32)
    rows_out[...] = column_of(jnp.concatenate([line, line], axis=1), slots)
    copies[1].wait()


def start_kernel(cols, rows, tiles, w, part, row_mask, picked, pieces):
    slots = tiles.shape[0]
    sub = iota((SUB, LANES), 0).astype(F32)
    for t in range(slots):
        row_mask[t * SUB : (t + 1) * SUB, :] = (sub == rows[t : t + 1, :]).astype(F32)
    for t in range(slots):
        picked[t : t + 1, :] = w[pl.ds(cols[0, t], 1), :]
    save_pieces(picked[...], pieces)
    squares = jnp.zeros((SUB, LANES), F32)
    rows_w = w.shape[0]
    step_rows = min(rows_w, 256)
    for b in range(0, rows_w, step_rows):
        block = w[b : b + step_rows, :]
        squares = squares + jnp.sum((block * block).reshape(step_rows // SUB, SUB, LANES), axis=0)
    part[SUB : 2 * SUB, :] = squares
    acc = jnp.zeros((6 * SUB, 2 * LANES), F32)
    for s in range(0, slots, 4):
        a, b, c, d = (
            masked_line(pieces, slots, t, row_mask[t * SUB : (t + 1) * SUB, :]) for t in range(s, s + 4)
        )
        left = [jnp.concatenate([*x, *y], axis=0).astype(BF16) for x, y in ((a, c), (b, d))]
        right = [jnp.concatenate([tiles[t], tiles[t + 1]], axis=1) for t in (s, s + 2)]
        acc = acc + lax.dot_general(
            jnp.concatenate(left, axis=1),
            jnp.concatenate(right, axis=0),
            (((1,), (1,)), ((), ())),
            preferred_element_type=F32,
        )
    part[0:SUB, :] = fold3(acc[:, :LANES]) + fold3(acc[:, LANES:], 3 * SUB)


def turn_kernel(tiles, turned):
    for t in range(tiles.shape[0]):
        turned[t] = tiles[t].T


def ranks(line, column, parts):
    shift = CAP_RUN.bit_length() - 1
    run, run_column = line.astype(I32) >> shift, column.astype(I32) >> shift
    sub, lane = iota(column.shape, 0), iota(column.shape, 1)
    same = (run == run_column) & (sub < lane)
    if parts == 2:
        same = same & ((sub < LANES // 2) == (lane < LANES // 2))
    return run, jnp.sum(same.astype(F32), axis=0, keepdims=True).astype(I32)


def column_of(line, rows):
    wide = jnp.broadcast_to(line, (rows, LANES))
    own = jnp.where(iota((rows, LANES), 0) == iota((rows, LANES), 1), wide, 0.0)
    return jnp.broadcast_to(jnp.sum(own, axis=1, keepdims=True), (rows, LANES))


def prep_kernel(ids, rows, cols_line, index, mask_out, cols_out, own_out, *send_out):
    n = ids.shape[1]
    left = ((ids[...] >> 7) == iota((SUB, n), 0)).astype(F32).astype(BF16)
    right = ((ids[...] & (LANES - 1)) == iota((LANES, n), 0)).astype(F32).astype(BF16)
    hits = lax.dot_general(left, right, (((1,), (1,)), ((), ())), preferred_element_type=F32)
    mask_out[...] = jnp.minimum(hits, 1.0)
    slots = rows.shape[0]
    sub, lane = iota((slots, LANES), 0), iota((slots, LANES), 1)
    line = cols_line[...].astype(F32)
    line = jnp.concatenate([line, line], axis=1)
    own = jnp.where(rows[...] >= 0.0, column_of(line, slots), -1.0)
    line = jnp.sum(jnp.where(sub == (lane & (slots - 1)), own, 0.0), axis=0, keepdims=True)
    cols_out[...] = jnp.broadcast_to(line, (SUB, LANES))
    own_out[...] = own
    for out in send_out:
        run, rank = ranks(line, own, 1)
        row = iota((SHORT, LANES), 0)
        sent = [((row == rank) & (run == (index[0] ^ k))).astype(F32) for k in (0, 3, 2, 1)]
        out[...] = jnp.concatenate(sent, axis=0)[:, :slots].astype(BF16)


def feat_sum(refs, first=0):
    out = None
    for ref, height in refs:
        for at in range(0, ref.shape[0], height):
            piece = ref[at + first : at + first + SUB, :]
            out = piece if out is None else out + piece
    return out


def parts_of(refs, slots):
    height = slots + TAIL
    return [(ref, at) for ref in refs for at in range(0, ref.shape[0], height)]


def summed(refs, slots, row):
    line = None
    for ref, at in parts_of(refs, slots):
        piece = ref[at + slots + row : at + slots + row + 1, :]
        line = piece if line is None else line + piece
    return total(line)


def slot_cols(refs, slots):
    parts = parts_of(refs, slots)
    low = iota((1, LANES), 1) < slots
    lines = []
    for a, b in zip(parts[::2], parts[1::2], strict=True):
        first, second = (r[at + slots + COLS_ROW : at + slots + COLS_ROW + 1, :] for r, at in (a, b))
        lines.append(jnp.where(low, first, second))
    return jnp.concatenate(lines, axis=1)


def slot_values(refs, slots):
    return jnp.concatenate([ref[at : at + slots, :] for ref, at in parts_of(refs, slots)], axis=0)


def write_tail(msg, slots, lines):
    pad = jnp.zeros((TAIL - len(lines), LANES), F32)
    msg[slots : slots + TAIL, :] = jnp.concatenate([*lines, pad], axis=0)


def line_of(x):
    return jnp.sum(x, axis=0, keepdims=True)


def margin_kernel(n_f, scale, tiles, rows, mask, labels, cols, *refs):
    got, (msg, m_out, c_out, e_out, ww_out) = refs[:n_f], refs[n_f:]
    slots = tiles.shape[0]
    pieces = [(ref, 2 * SUB) for ref in got]
    m = feat_sum(pieces)
    chance = jax.nn.sigmoid(m)
    e = chance - labels[...].astype(F32)
    by_cols(tiles, rows, e, msg)
    zero = jnp.zeros((1, LANES), F32)
    write_tail(msg, slots, [zero, zero, zero, cols[0:1, :]])
    ww_out[...] = feat_sum(pieces, SUB)
    c_out[...] = scale * mask[...] * chance * (1.0 - chance)
    m_out[...] = m
    e_out[...] = e


def match_kernel(n_i, order, own, *refs):
    got, (match,) = sorted_as(order, refs[:n_i]), refs[n_i:]
    slots = own.shape[0]
    line = slot_cols(got, slots)
    for at in range(0, line.shape[1], LANES):
        same = own[...] == line[:, at : at + LANES]
        match[:, at : at + LANES] = same.astype(F32).astype(BF16)


def forward_kernel(n_i, order, turned, row_mask, match, *refs):
    got, (out, pieces) = sorted_as(order, refs[:n_i]), refs[n_i:]
    slots = turned.shape[0]
    save_pieces(exact_pick(match[...], slot_values(got, slots)), pieces)
    out[...] = by_rows(turned, pieces, row_mask)


def first_kernel(n_f, tiles, rows, m, c, e, *refs):
    got, (msg, v_out) = refs[:n_f], refs[n_f:]
    slots = tiles.shape[0]
    v = -(LAMBDA * m[...] + feat_sum([(ref, SUB) for ref in got]))
    v_out[...] = v
    u = c[...] * v
    by_cols(tiles, rows, u, msg)
    s = -e[...]
    write_tail(msg, slots, [line_of(-LAMBDA * m[...] * s + s * v), line_of(u * v)])


NUMBERS = ("rr", "dd", "cur", "a_r", "a_d", "alpha", "beta")


def numbers_of(num):
    return {name: num[k : k + 1, 0:1] for k, name in enumerate(NUMBERS)}


def save_numbers(num, values):
    lines = [jnp.broadcast_to(values[name], (1, LANES)) for name in NUMBERS]
    num[...] = jnp.concatenate([*lines, jnp.zeros((1, LANES), F32)], axis=0)


def advance(msgs, slots, ww, old, shift=0):
    rr_new, cur_r = summed(msgs, slots, shift), summed(msgs, slots, shift + 1)
    if old is None:
        a_r = a_d = jnp.full((1, 1), -LAMBDA, F32)
        rr = a_r * a_r * total(ww[...]) + rr_new
        dd, cur, beta = rr, cur_r, jnp.zeros((1, 1), F32)
    else:
        cross = summed(msgs, slots, shift + 2)
        rr = old["a_r"] * old["a_r"] * total(ww[...]) + rr_new
        beta = rr / old["rr"]
        a_d = old["a_r"] + beta * old["a_d"]
        dd = rr + beta * beta * old["dd"]
        cur = cur_r + 2.0 * beta * cross + beta * beta * old["cur"]
        a_r = old["a_r"]
    alpha = rr / (cur + LAMBDA * dd)
    a_r = a_r - alpha * (LAMBDA * a_d)
    return {"rr": rr, "dd": dd, "cur": cur, "a_r": a_r, "a_d": a_d, "alpha": alpha, "beta": beta}


def at(ref, k):
    return ref[k * SUB : (k + 1) * SUB, :]


def save_all(ref, values):
    for k, value in enumerate(values):
        ref[k * SUB : (k + 1) * SUB, :] = value


def numbers_kernel(n_i, slots, first, m, c, ww, *refs):
    msgs = refs[:n_i]
    vec_out, num_out = refs[-2:]
    if first:
        e, v = refs[n_i:-2]
        new = advance(msgs, slots, ww, None)
        v_r, s_r = v[...], -e[...]
        v_d, s_d, gram = v_r, s_r, jnp.zeros((SUB, LANES), F32)
    else:
        v, gram_d, vec, num = refs[n_i:-2]
        new = advance(msgs, slots, ww, numbers_of(num))
        v_r, s_r = v[...], at(vec, 2)
        v_d = v_r + new["beta"] * at(vec, 1)
        s_d = s_r + new["beta"] * at(vec, 3)
        gram = new["beta"] * gram_d[...]
    v_r = v_r - new["alpha"] * (gram + LAMBDA * v_d)
    s_r = s_r - new["alpha"] * (c[...] * v_d + LAMBDA * s_d)
    save_all(vec_out, (v_r, v_d, s_r, s_d, new["a_r"] * m[...] * s_r, gram))
    save_numbers(num_out, new)


def next_kernel(n_f, short, tiles, rows, c, vec, num, *refs):
    got, (msg, *kept) = refs[:n_f], refs[n_f:]
    slots = tiles.shape[0]
    if short:
        send, *outs, msg = refs[n_f:]
    gram = feat_sum([(ref, SUB) for ref in got])
    v = at(vec, 0) - numbers_of(num)["alpha"] * gram
    u = c[...] * v
    by_cols(tiles, rows, u, msg)
    lines = [line_of(at(vec, 4) + at(vec, 2) * v), line_of(u * v), line_of(u * at(vec, 1))]
    if short:
        chosen = exact_pick(send[...], msg[...])
        pad = [jnp.zeros((n, LANES), F32) for n in (CAP, SHORT - CAP - len(lines))]
        tail = jnp.concatenate([pad[0], *lines, pad[1]], axis=0)
        for j, out in enumerate(outs):
            slots_rows = chosen[j * SHORT : (j + 1) * SHORT]
            out[...] = jnp.where(iota((SHORT, LANES), 0) < CAP, slots_rows, tail)
        return
    write_tail(msg, slots, lines)
    for out, value in zip(kept, (v, gram + at(vec, 5))):
        out[...] = value


def dense_kernel(n_i, short, orders, slots, iters, w, index, *refs):
    msgs = [sorted_as(orders[k], refs[k * n_i : (k + 1) * n_i]) for k in range(iters)]
    nums = [numbers_of(num) for num in refs[iters * n_i : iters * n_i + iters - 1]]
    res_out, dir_out, step_out, curved_out, pick_out = refs[iters * n_i + iters - 1 :][:5]
    if short:
        short_out, pick_out = refs[-2:]
    own_blocks = res_out.shape[0]
    line = slot_cols(msgs[0], slots)
    offset = index[0] * own_blocks
    own = (iota((own_blocks, LANES), 0) + offset).astype(F32)
    for a in range(0, line.shape[1], LANES):
        pick_out[:, a : a + LANES] = (own == line[:, a : a + LANES]).astype(F32).astype(BF16)
    mine = w[pl.ds(pl.multiple_of(offset, own_blocks), own_blocks), :]
    res = -LAMBDA * mine - exact_pick(pick_out[...], slot_values(msgs[0], slots))
    step = jnp.zeros_like(res)
    for k in range(iters - 1):
        image = exact_pick(pick_out[...], slot_values(msgs[k + 1], slots))
        if k == 0:
            direction, curved = res, image
        else:
            direction = res + nums[k]["beta"] * direction
            curved = image + nums[k]["beta"] * curved
        step = step + nums[k]["alpha"] * direction
        res = res - nums[k]["alpha"] * (curved + LAMBDA * direction)
    if short:
        blocks = []
        for a in range(0, line.shape[1], LANES):
            pair = line[:, a : a + LANES]
            run, rank = ranks(pair, column_of(pair, LANES), 2)
            first = a // slots * SHORT_PAD
            second = iota((1, LANES), 1) >= slots
            want = rank + jnp.where(second, first + SHORT_PAD, first)
            row = iota((LANES, LANES), 0)
            blocks.append(((row == want) & (run == index[0])).astype(F32).astype(BF16))
        short_out[...] = lax.dot_general(
            pick_out[...],
            jnp.concatenate(blocks, axis=1),
            (((1,), (1,)), ((), ())),
            preferred_element_type=F32,
        ).astype(BF16)
    res_out[...] = res
    dir_out[...] = direction
    step_out[...] = step
    curved_out[...] = curved


def last_kernel(n_i, short, order, slots, ww, num, res, direction, step, curved, pick, *refs):
    msgs, (step_out, res_out) = sorted_as(order, refs[:n_i]), refs[n_i:]
    if short:
        pad = jnp.zeros((SHORT_PAD - SHORT, LANES), F32)
        values = jnp.concatenate([piece for msg in msgs for piece in (msg[...], pad)], axis=0)
        new = advance(msgs, SHORT - TAIL, ww, numbers_of(num), CAP - (SHORT - TAIL))
    else:
        values = slot_values(msgs, slots)
        new = advance(msgs, slots, ww, numbers_of(num))
    image = exact_pick(pick[...], values)
    last = res[...] + new["beta"] * direction[...]
    step_out[...] = step[...] + new["alpha"] * last
    image = image + new["beta"] * curved[...] + LAMBDA * last
    res_out[...] = res[...] - new["alpha"] * image


def exchange(x, axis, order=FEAT_ORDER):
    size = lax.axis_size(axis)
    if size != 4:
        return [lax.all_gather(x, axis, axis=0, tiled=True)]
    return [x] + [lax.ppermute(x, axis, [(i, i ^ k) for i in range(size)]) for k in order]


def exchange_each(arrays, axis, order):
    to = dict(zip((3, 2, 1), arrays[1:], strict=True))
    return [arrays[0]] + [
        lax.ppermute(to[k], axis, [(i, i ^ k) for i in range(4)]) for k in order
    ]


def sorted_as(order, refs):
    if len(refs) == 1:
        return refs
    return [refs[0]] + [refs[1 + order.index(k)] for k in (3, 2, 1)]


def in_hbm(x):
    return pltpu.with_memory_space_constraint(x, pltpu.HBM)


def body(tiles, tile_rows, tile_cols, tile_count, sample_ids, labels, weights):
    slots, edge = tiles.shape[2], tiles.shape[3]
    row_total, feat_len = labels.shape[1], weights.shape[1]
    row_blocks, col_blocks = row_total // edge, feat_len // edge
    assert row_blocks == SUB and edge == LANES and 2 * slots == LANES
    inst = lax.axis_size("inst")
    own_len = feat_len // inst
    own_blocks = own_len // edge
    tiles = tiles.reshape(slots, edge, edge)
    scale = float(row_total) / float(sample_ids.shape[1])
    index = lax.axis_index("inst").astype(I32).reshape(1)
    grid, msg_shape = f32(SUB, LANES), f32(slots + TAIL, LANES)
    short = inst == 4 and own_blocks == CAP_RUN
    tile_shape = jax.ShapeDtypeStruct((slots, edge, edge), BF16)
    picks = jax.ShapeDtypeStruct

    w = weights.reshape(col_blocks, edge)
    rows, slot, cols = call(
        first_look_kernel,
        (in_hbm(tile_rows.reshape(1, slots)), in_hbm(tile_cols.reshape(1, slots))),
        [HBM] * 2,
        [f32(slots, LANES), picks((slots, LANES), I32), pltpu.SMEM((1, slots), I32)],
        [VM, VM, SM],
        scratch=[pltpu.VMEM((1, slots), I32), pltpu.SemaphoreType.DMA((2,))],
        flops=1 << 30,
    )
    rows = jnp.where(slot < tile_count, rows, -1.0)
    part, row_mask = call(
        start_kernel,
        (cols, rows, tiles, w),
        [SM, VM, VM, VM],
        [f32(2 * SUB, LANES), f32(slots * SUB, LANES)],
        scratch=[pltpu.VMEM((slots, LANES), F32), pltpu.VMEM((3 * slots, LANES), F32)],
    )
    mask, cols_line, own, *send = call(
        prep_kernel,
        (sample_ids, rows, tile_cols.reshape(1, slots), index),
        [VM] * 3 + [SM],
        [grid, grid, f32(slots, LANES)]
        + [picks((4 * SHORT, slots), BF16)] * short,
    )
    (turned,) = call(turn_kernel, (tiles,), [VM], [tile_shape])
    got = exchange(part, "feat")
    n_f = len(got)
    msg, m, c, e, ww = call(
        functools.partial(margin_kernel, n_f, scale),
        (tiles, rows, mask, labels.reshape(SUB, LANES), cols_line, *got),
        [VM] * (5 + n_f),
        [msg_shape, grid, grid, grid, grid],
    )
    msgs = exchange(msg, "inst", ORDERS[0])
    n_i = len(msgs)
    (match,) = call(
        functools.partial(match_kernel, n_i, ORDERS[0]),
        (own, *msgs),
        [VM] * (1 + n_i),
        [picks((slots, slots * inst), BF16)],
    )

    def forward(msgs, order):
        (out,) = call(
            functools.partial(forward_kernel, n_i, order),
            (turned, row_mask, match, *msgs),
            [VM] * (3 + n_i),
            [grid],
            scratch=[pltpu.VMEM((3 * slots, LANES), F32)],
        )
        return exchange(out, "feat")

    got = forward(msgs, ORDERS[0])
    msg, v = call(
        functools.partial(first_kernel, n_f),
        (tiles, rows, m, c, e, *got),
        [VM] * (5 + n_f),
        [msg_shape, grid],
    )
    history = [msgs, exchange(msg, "inst", ORDERS[1])]
    state, nums = (e, v), []
    for k in range(ITERS - 1):
        got = forward(history[-1], ORDERS[k + 1])
        vec, num = call(
            functools.partial(numbers_kernel, n_i, slots, k == 0),
            (m, c, ww, *history[-1], *state),
            [VM] * (3 + n_i + len(state)),
            [f32(6 * SUB, LANES), grid],
        )
        if short and k == ITERS - 2:
            to_each = call(
                functools.partial(next_kernel, n_f, True),
                (tiles, rows, c, vec, num, *got, *send),
                [VM] * (6 + n_f),
                [f32(SHORT, LANES)] * 4,
                scratch=[pltpu.VMEM((slots, LANES), F32)],
            )
            history.append(exchange_each(to_each, "inst", ORDERS[ITERS]))
            nums.append(num)
            break
        msg, *kept = call(
            functools.partial(next_kernel, n_f, False),
            (tiles, rows, c, vec, num, *got),
            [VM] * (5 + n_f),
            [msg_shape] + [grid, grid] * (k < ITERS - 2),
        )
        history.append(exchange(msg, "inst", ORDERS[k + 2]))
        state = (*kept, vec, num)
        nums.append(num)
    block = f32(own_blocks, edge)
    *dense, pick = call(
        functools.partial(dense_kernel, n_i, short, ORDERS, slots, ITERS),
        (w, index, *(ref for group in history[:ITERS] for ref in group), *nums),
        [VM, SM] + [VM] * (n_i * ITERS + len(nums)),
        [block] * 4 + [picks((own_blocks, LANES if short else slots * inst), BF16)],
        scratch=[pltpu.VMEM((own_blocks, slots * inst), BF16)] * short,
    )
    step, res = call(
        functools.partial(last_kernel, n_i, short, ORDERS[ITERS], slots),
        (ww, nums[-1], *dense, pick, *history[-1]),
        [VM] * (7 + n_i),
        [block, block],
    )
    return step.reshape(1, own_len), res.reshape(1, own_len)


def solution(mesh):
    return jax.shard_map(
        body,
        mesh=mesh,
        in_specs=(
            P(("groups", "inst"), "feat", None, None, None),
            P(("groups", "inst"), "feat", None),
            P(("groups", "inst"), "feat", None),
            P(("groups", "inst"), "feat"),
            P(("groups", "inst"), None),
            P(("groups", "inst"), None),
            P(("groups", "feat"), None),
        ),
        out_specs=(P(("groups", "feat"), "inst"), P(("groups", "feat"), "inst")),
        check_vma=False,
    )
```
